32 devices in a mesh: leaf: 8 (over z, x), grp: 4 (over y, core).
Axes of the slice: x: 2, y: 2, z: 4, core: 2. Of those that a mesh axis runs over, the one named last changes fastest.
Arguments:
- vectors: float32 [16, 262144], P(None, ('leaf', 'grp')), may hold values from -6 to 6
- coords: float32 [2, 262144], P(None, ('leaf', 'grp')), may hold values from 0 to 1, as said below
- perm: int32 [262144], P(('leaf', 'grp')), may hold values from 0 to 8191, as said below
- bases: float32 [512, 64, 512], P(('leaf', 'grp')), may hold values from -0.25 to 0.25
- leaf_maps: float32 [512, 64, 64], P(('leaf', 'grp')), may hold values from -0.1875 to 0.1875
- node_maps: float32 [32, 64, 64], P(('leaf', 'grp')), may hold values from -0.375 to 0.375
- leaf_skel: float32 [512, 2, 64], P(('leaf', 'grp')), may hold values from 0 to 1
- node_skel: float32 [32, 2, 64], P(('leaf', 'grp')), may hold values from 0 to 1
- sub_skel: float32 [8, 2, 64], P('leaf'), may hold values from 0 to 1
- leaf_src: int32 [512, 16], P(('leaf', 'grp')), may hold values from 0 to 63
- leaf_count: int32 [512], P(('leaf', 'grp')), may hold values from 1 to 16
- node_src: int32 [32, 8], P(('leaf', 'grp')), may hold values from 0 to 11, as said below
- node_count: int32 [32], P(('leaf', 'grp')), may hold values from 1 to 8
Outputs:
- product: float32 [16, 262144], P(None, ('leaf', 'grp'))
The draws below stay inside these ranges and needn't reach their ends.
Inputs may be any that keep to these rules, and one draw needn't show every extreme that they name: `perm`: each aligned block of 8192 entries holds every number of 0 to 8191 once. `coords`: rows 3k, 3k + 1 and 3k + 2 share one site's coordinates. `node_src`: entries index the device nodes of subtrees s - 1, s, s + 1 in order (s the node's own subtree), only subtrees that exist.
All inputs are finite; a program needn't handle non-finite values.
Results may differ from the reference program's by a relative error of at most 0.0003.
Values sent between devices are 32-bit elements; how exact they have to be, the bound alone decides.
No kernel may reach another device: no remote copies, remote signals or barrier semaphores. Data moves between devices by JAX's collectives and lax.ppermute only.
A program may use at most 64 MiB of HBM per device.

```python
import math
import jax
import jax.numpy as jnp
import numpy as np
from jax import lax

B = 512
R = 64
NV = 16
K0 = 16
K1 = 8
LEAF_DEV = 16
ROWS_DEV = 8192
NODES = 32
ROWS = 262144
NLEAF = 512
LEAF_GROUP = 64
N_LEAF = 8
N_GRP = 4


def draw_coords(key, part):
    key = jax.random.fold_in(key, 11)
    sites = (ROWS + 2) // 3
    points = jax.random.uniform(key, (2, sites), jnp.float32)
    return jnp.repeat(points, 3, axis=1)[:, :ROWS]


def draw_perm(key, part):
    key = jax.random.fold_in(key, 12)
    keys = jax.random.split(key, NODES)
    blocks = jax.vmap(lambda one: jax.random.permutation(one, ROWS_DEV))(keys)
    return blocks.astype(jnp.int32).reshape(ROWS)


def draw_leaf_count(key, part):
    key = jax.random.fold_in(key, 13)
    first, second = jax.random.split(key)
    shifts = jax.random.randint(first, (NODES,), 0, 4)
    caps = jnp.maximum(K0 // jnp.left_shift(jnp.ones((NODES,), jnp.int32), shifts), 1)
    per_leaf = jnp.repeat(caps, LEAF_DEV)
    counts = jax.random.randint(second, (NLEAF,), 1, per_leaf + 1)
    return counts.at[0].set(K0).astype(jnp.int32)


def draw_node_src(key, part):
    key = jax.random.fold_in(key, 14)
    subtree = jnp.arange(NODES, dtype=jnp.int32) // N_GRP
    lower = jnp.where(subtree > 0, 0, N_GRP)
    upper = jnp.where(subtree < N_LEAF - 1, 3 * N_GRP, 2 * N_GRP)
    return jax.random.randint(key, (NODES, K1), lower[:, None], upper[:, None]).astype(jnp.int32)


def draw_node_count(key, part):
    key = jax.random.fold_in(key, 15)
    counts = jax.random.randint(key, (NODES,), 1, K1 + 1)
    return counts.at[0].set(K1).astype(jnp.int32)


def place_ends(values, key, least, largest):
    index_at = [jax.random.randint(jax.random.fold_in(key, axis), (), 0, length) for axis, length in enumerate(values.shape)]
    main_axis = values.shape.index(max(values.shape))
    beside = index_at[:main_axis] + [(index_at[main_axis] + 1) % values.shape[main_axis]] + index_at[main_axis + 1:]
    return values.at[tuple(index_at)].set(least).at[tuple(beside)].set(largest)


def levels(own_key, dims, cuts, smallest, top_value):
    factor_of, own = 1.0, jax.random.fold_in(own_key, 6)
    for dim, parts in cuts:
        heights = jnp.exp(jax.random.uniform(jax.random.fold_in(own, dim), (parts,), jnp.float32, smallest / len(cuts), top_value / len(cuts)))
        factor_of = factor_of * jnp.repeat(heights, dims[dim] // parts).reshape([-1 if axis == dim else 1 for axis in range(len(dims))])
    return factor_of


def gaussian(stream_key, extent, width, bound, cuts=(), kind=jnp.bfloat16):
    result = jax.random.normal(stream_key, extent, jnp.float32) * width
    if len(cuts) > 0:
        result = levels(stream_key, extent, cuts, -0.22, 0.18) * result
    return jnp.clip(result, min=-bound, max=bound).astype(kind)


def setup_inputs(seed: int = 0) -> dict:
    splits = jax.random.split(jax.random.key(seed), 14)
    return {
        "vectors": gaussian(splits[0], (NV, ROWS), 1.0, 6.0, ((1, 32),), jnp.float32),
        "coords": draw_coords(jax.random.fold_in(splits[13], 71), 0),
        "perm": draw_perm(jax.random.fold_in(splits[13], 71), 0),
        "bases": gaussian(splits[3], (NLEAF, R, B), B ** -0.5, 0.25, ((0, 32),), jnp.float32),
        "leaf_maps": gaussian(splits[4], (NLEAF, R, R), (R * LEAF_DEV) ** -0.5, 0.1875, ((0, 32),), jnp.float32),
        "node_maps": gaussian(splits[5], (NODES, R, R), (R * N_GRP) ** -0.5, 0.375, ((0, 32),), jnp.float32),
        "leaf_skel": jnp.clip(1.0 * jax.random.uniform(splits[6], (NLEAF, 2, R), jnp.float32) ** levels(splits[6], (NLEAF, 2, R), ((0, 32),), -0.2, 0.2), 0.0, 1.0),
        "node_skel": jnp.clip(1.0 * jax.random.uniform(splits[7], (NODES, 2, R), jnp.float32) ** levels(splits[7], (NODES, 2, R), ((0, 32),), -0.2, 0.2), 0.0, 1.0),
        "sub_skel": jnp.clip(1.0 * jax.random.uniform(splits[8], (N_LEAF, 2, R), jnp.float32) ** levels(splits[8], (N_LEAF, 2, R), ((0, 8),), -0.2, 0.2), 0.0, 1.0),
        "leaf_src": place_ends(jax.random.randint(splits[9], (NLEAF, K0), 0, LEAF_GROUP), jax.random.fold_in(splits[9], 1), 0, LEAF_GROUP - 1).astype(jnp.int32),
        "leaf_count": draw_leaf_count(jax.random.fold_in(splits[13], 71), 0),
        "node_src": draw_node_src(jax.random.fold_in(splits[13], 71), 0),
        "node_count": draw_node_count(jax.random.fold_in(splits[13], 71), 0),
    }


def make_tables():
    smooth = [0, 2, 4]
    sigmas = [1.0, 0.8, 1.2]
    rho = [[1.0, 0.5, 0.3], [0.5, 1.0, 0.4], [0.3, 0.4, 1.0]]
    scale_table = np.zeros((3, 3))
    poly_tables = np.zeros((5, 3, 3))
    for first in range(3):
        for second in range(3):
            order = (smooth[first] + smooth[second]) // 2
            scale_table[first, second] = math.sqrt(2.0 * order + 1.0) / 0.3
            amp = sigmas[first] * sigmas[second] * rho[first][second]
            for power in range(order + 1):
                kterm = order - power
                coeff = math.factorial(order) / math.factorial(2 * order)
                coeff = coeff * math.factorial(order + kterm) / (math.factorial(kterm) * math.factorial(order - kterm))
                poly_tables[power, first, second] = amp * coeff * 2.0 ** power
    return (scale_table, poly_tables)

def cross_cov(coords_a, vars_a, coords_b, vars_b):
    kernel_tables = make_tables()
    diff_x = coords_a[0][:, None] - coords_b[0][None, :]
    diff_y = coords_a[1][:, None] - coords_b[1][None, :]
    dist = jnp.sqrt(diff_x * diff_x + diff_y * diff_y)
    col_zero = (vars_b == 0)[None, :]
    col_one = (vars_b == 1)[None, :]

    def lookup(table):
        rows = jnp.asarray(table, jnp.float32)[vars_a]
        return jnp.where(col_zero, rows[:, 0:1], jnp.where(col_one, rows[:, 1:2], rows[:, 2:3]))
    scaled = lookup(kernel_tables[0]) * dist
    poly = lookup(kernel_tables[1][4])
    for power in (3, 2, 1, 0):
        poly = poly * scaled + lookup(kernel_tables[1][power])
    return jnp.exp(-scaled) * poly

def couple(coef, src_skel, dst_skel, skel_var, weight):
    blocks = jax.vmap(lambda one, two: cross_cov(one, skel_var, two, skel_var))(src_skel, dst_skel)
    terms = jnp.einsum('nvr,nrq->nvq', coef, blocks, precision=lax.Precision.HIGHEST)
    return terms * weight[:, None, None] / math.sqrt(coef.shape[2])

def reference(vectors, coords, perm, bases, leaf_maps, node_maps, leaf_skel, node_skel, sub_skel, leaf_src, leaf_count, node_src, node_count):
    high = lax.Precision.HIGHEST
    offsets = jnp.arange(ROWS, dtype=jnp.int32) // ROWS_DEV * ROWS_DEV
    site_rows = (perm.astype(jnp.int32) + offsets).astype(jnp.int32)
    tree_vec = vectors[:, site_rows]
    tree_crd = coords[:, site_rows]
    tree_var = site_rows % 3
    leaf_vec = tree_vec.reshape(NV, NLEAF, B).transpose(1, 0, 2)
    leaf_crd = tree_crd.reshape(2, NLEAF, B).transpose(1, 0, 2)
    leaf_var = tree_var.reshape(NLEAF, B)
    skel_var = jnp.arange(R, dtype=jnp.int32) % 3
    up_leaf = jnp.einsum('lvb,lrb->lvr', leaf_vec, bases, precision=high)

    def leaf_far(packed):
        target, row_src, count = packed
        src = row_src + target // LEAF_GROUP * LEAF_GROUP
        weight = (jnp.arange(K0, dtype=jnp.int32) < count).astype(jnp.float32)
        dst = jnp.broadcast_to(leaf_skel[target], (K0, 2, R))
        return couple(up_leaf[src], leaf_skel[src], dst, skel_var, weight).sum(axis=0)
    far_leaf = lax.map(leaf_far, (jnp.arange(NLEAF, dtype=jnp.int32), leaf_src, leaf_count))
    maps_by_node = leaf_maps.reshape(NODES, LEAF_DEV, R, R)
    up_node = jnp.einsum('nlvr,nlrq->nvq', up_leaf.reshape(NODES, LEAF_DEV, NV, R), maps_by_node, precision=high)
    up_sub = jnp.einsum('sgvr,sgrq->svq', up_node.reshape(N_LEAF, N_GRP, NV, R), node_maps.reshape(N_LEAF, N_GRP, R, R), precision=high)

    def node_far(packed):
        target, row_src, count = packed
        src = row_src + (target // N_GRP - 1) * N_GRP
        weight = (jnp.arange(K1, dtype=jnp.int32) < count).astype(jnp.float32)
        dst = jnp.broadcast_to(node_skel[target], (K1, 2, R))
        return couple(up_node[src], node_skel[src], dst, skel_var, weight).sum(axis=0)
    far_node = lax.map(node_far, (jnp.arange(NODES, dtype=jnp.int32), node_src, node_count))

    def sub_far(target):
        others = jnp.arange(N_LEAF, dtype=jnp.int32)
        weight = (jnp.abs(others - target) >= 2).astype(jnp.float32)
        dst = jnp.broadcast_to(sub_skel[target], (N_LEAF, 2, R))
        return couple(up_sub, sub_skel, dst, skel_var, weight).sum(axis=0)
    far_sub = lax.map(sub_far, jnp.arange(N_LEAF, dtype=jnp.int32))
    parent_sub = far_sub[jnp.arange(NODES, dtype=jnp.int32) // N_GRP]
    down_node = far_node + jnp.einsum('nvq,nrq->nvr', parent_sub, node_maps, precision=high)
    down_leaf = far_leaf + jnp.einsum('nvq,nlrq->nlvr', down_node, maps_by_node, precision=high).reshape(NLEAF, NV, R)
    far_rows = jnp.einsum('lvr,lrb->lvb', down_leaf, bases, precision=high)

    def near_block(packed):
        rows_vec, rows_crd, rows_var = packed
        block = cross_cov(rows_crd, rows_var, rows_crd, rows_var)
        return jnp.dot(rows_vec, block, precision=high) / math.sqrt(B)
    near = lax.map(near_block, (leaf_vec, leaf_crd, leaf_var))
    tree_out = (far_rows + near).transpose(1, 0, 2).reshape(NV, ROWS)
    return jnp.zeros_like(vectors).at[:, site_rows].set(tree_out)
```

```python
import math

import jax
import jax.numpy as jnp
import numpy as np
from jax import lax
from jax.sharding import PartitionSpec as P


def make_tables():
    smooth = [0, 2, 4]
    sigmas = [1.0, 0.8, 1.2]
    rho = [[1.0, 0.5, 0.3], [0.5, 1.0, 0.4], [0.3, 0.4, 1.0]]
    scale_table = np.zeros((3, 3))
    poly_tables = np.zeros((5, 3, 3))
    for first in range(3):
        for second in range(3):
            order = (smooth[first] + smooth[second]) // 2
            scale_table[first, second] = math.sqrt(2.0 * order + 1.0) / 0.3
            amp = sigmas[first] * sigmas[second] * rho[first][second]
            for power in range(order + 1):
                kterm = order - power
                coeff = math.factorial(order) / math.factorial(2 * order)
                coeff = (
                    coeff
                    * math.factorial(order + kterm)
                    / (math.factorial(kterm) * math.factorial(order - kterm))
                )
                poly_tables[power, first, second] = amp * coeff * 2.0**power
    return (scale_table, poly_tables)


def cross_cov(coords_a, vars_a, coords_b, vars_b):
    kernel_tables = make_tables()
    diff_x = coords_a[0][:, None] - coords_b[0][None, :]
    diff_y = coords_a[1][:, None] - coords_b[1][None, :]
    dist = jnp.sqrt(diff_x * diff_x + diff_y * diff_y)
    col_zero = (vars_b == 0)[None, :]
    col_one = (vars_b == 1)[None, :]

    def lookup(table):
        rows = jnp.asarray(table, jnp.float32)[vars_a]
        return jnp.where(col_zero, rows[:, 0:1], jnp.where(col_one, rows[:, 1:2], rows[:, 2:3]))

    scaled = lookup(kernel_tables[0]) * dist
    poly = lookup(kernel_tables[1][4])
    for power in (3, 2, 1, 0):
        poly = poly * scaled + lookup(kernel_tables[1][power])
    return jnp.exp(-scaled) * poly


def couple(coef, src_skel, dst_skel, skel_var, weight):
    blocks = jax.vmap(lambda one, two: cross_cov(one, skel_var, two, skel_var))(src_skel, dst_skel)
    terms = jnp.einsum("nvr,nrq->nvq", coef, blocks, precision=lax.Precision.HIGHEST)
    return terms * weight[:, None, None] / math.sqrt(coef.shape[2])


def shards(
    vectors,
    coords,
    perm,
    bases,
    leaf_maps,
    node_maps,
    leaf_skel,
    node_skel,
    sub_skel,
    leaf_src,
    leaf_count,
    node_src,
    node_count,
):
    high = lax.Precision.HIGHEST
    nvec, rows_dev = vectors.shape
    leaves, rank, block = bases.shape
    node_len = node_src.shape[1]
    groups = lax.axis_size("grp")
    subtrees = lax.axis_size("leaf")
    device_pos = lax.axis_index("leaf") * groups + lax.axis_index("grp")
    tree_vec = jnp.take(vectors, perm, axis=1)
    tree_crd = jnp.take(coords, perm, axis=1)
    leaf_vec = tree_vec.reshape(nvec, leaves, block).transpose(1, 0, 2)
    leaf_crd = tree_crd.reshape(2, leaves, block).transpose(1, 0, 2)
    leaf_var = ((perm + device_pos * rows_dev % 3) % 3).reshape(leaves, block)
    skel_var = jnp.arange(rank, dtype=jnp.int32) % 3
    up_leaf = jnp.einsum("lvb,lrb->lvr", leaf_vec, bases, precision=high)
    grp_pos = lax.axis_index("grp")
    mine = lax.axis_index("leaf")
    leaf_pack = jnp.concatenate([up_leaf, leaf_skel], axis=1)
    leaf_slots = jnp.zeros((groups * leaves, nvec + 2, rank), jnp.float32)
    leaf_slots = lax.dynamic_update_slice(leaf_slots, leaf_pack, (grp_pos * leaves, 0, 0))
    group_all = lax.psum(leaf_slots, "grp")
    group_coef, group_skel = group_all[:, :nvec], group_all[:, nvec:]
    up_node = jnp.einsum("lvr,lrq->vq", up_leaf, leaf_maps, precision=high)
    node_pack = jnp.concatenate([up_node[None], node_skel], axis=1)
    sub_part = jnp.dot(up_node, node_maps[0], precision=high)
    sub_pack = jnp.concatenate(
        [sub_part[None], jnp.where(grp_pos == 0, sub_skel, 0.0)], axis=1
    )
    nodes = subtrees * groups
    slots = jnp.zeros((nodes + subtrees, nvec + 2, rank), jnp.float32)
    slots = lax.dynamic_update_slice(slots, node_pack, (device_pos, 0, 0))
    slots = lax.dynamic_update_slice(slots, sub_pack, (nodes + mine, 0, 0))
    tree_all = lax.psum(slots, ("leaf", "grp"))
    all_subs = tree_all[nodes:]

    def owner_step(order, total):
        src = lax.dynamic_slice_in_dim(leaf_src, order, 1, 1)[:, 0]
        weight = (order < leaf_count).astype(jnp.float32)
        return total + couple(group_coef[src], group_skel[src], leaf_skel, skel_var, weight)

    far_leaf = lax.fori_loop(
        jnp.int32(0), jnp.max(leaf_count), owner_step, jnp.zeros((leaves, nvec, rank), jnp.float32)
    )
    beside = jnp.clip(node_src[0] + (mine - 1) * groups, 0, nodes - 1)
    pieces = tree_all[beside]
    node_weight = (jnp.arange(node_len, dtype=jnp.int32) < node_count[0]).astype(jnp.float32)
    node_dst = jnp.broadcast_to(node_skel[0], (node_len, 2, rank))
    far_node = couple(pieces[:, :nvec], pieces[:, nvec:], node_dst, skel_var, node_weight).sum(
        axis=0
    )
    others = jnp.arange(subtrees, dtype=jnp.int32)
    sub_weight = (jnp.abs(others - mine) >= 2).astype(jnp.float32)
    sub_dst = jnp.broadcast_to(sub_skel[0], (subtrees, 2, rank))
    far_sub = couple(all_subs[:, :nvec], all_subs[:, nvec:], sub_dst, skel_var, sub_weight).sum(
        axis=0
    )
    down_node = far_node + jnp.dot(far_sub, node_maps[0].T, precision=high)
    down_leaf = far_leaf + jnp.einsum("vq,lrq->lvr", down_node, leaf_maps, precision=high)
    far_rows = jnp.einsum("lvr,lrb->lvb", down_leaf, bases, precision=high)

    def near_block(packed_rows):
        rows_vec, rows_crd, rows_var = packed_rows
        dense = cross_cov(rows_crd, rows_var, rows_crd, rows_var)
        return jnp.dot(rows_vec, dense, precision=high) / math.sqrt(block)

    near = lax.map(near_block, (leaf_vec, leaf_crd, leaf_var))
    tree_out = (far_rows + near).transpose(1, 0, 2).reshape(nvec, rows_dev)
    return jnp.zeros_like(vectors).at[:, perm].set(tree_out)


def solution(mesh):
    placed = (
        P(None, ("leaf", "grp")),
        P(None, ("leaf", "grp")),
        P(("leaf", "grp")),
        P(("leaf", "grp"), None, None),
        P(("leaf", "grp"), None, None),
        P(("leaf", "grp"), None, None),
        P(("leaf", "grp"), None, None),
        P(("leaf", "grp"), None, None),
        P("leaf", None, None),
        P(("leaf", "grp"), None),
        P(("leaf", "grp")),
        P(("leaf", "grp"), None),
        P(("leaf", "grp")),
    )
    return jax.shard_map(
        shards, mesh=mesh, in_specs=placed, out_specs=P(None, ("leaf", "grp")), check_vma=False
    )
```

```python
import math

import jax
import jax.numpy as jnp
import numpy as np
from jax import lax
from jax.sharding import PartitionSpec as P


def make_tables():
    smooth = [0, 2, 4]
    sigmas = [1.0, 0.8, 1.2]
    rho = [[1.0, 0.5, 0.3], [0.5, 1.0, 0.4], [0.3, 0.4, 1.0]]
    scale_table = np.zeros((3, 3))
    poly_tables = np.zeros((5, 3, 3))
    for first in range(3):
        for second in range(3):
            order = (smooth[first] + smooth[second]) // 2
            scale_table[first, second] = math.sqrt(2.0 * order + 1.0) / 0.3
            amp = sigmas[first] * sigmas[second] * rho[first][second]
            for power in range(order + 1):
                kterm = order - power
                coeff = math.factorial(order) / math.factorial(2 * order)
                coeff = (
                    coeff
                    * math.factorial(order + kterm)
                    / (math.factorial(kterm) * math.factorial(order - kterm))
                )
                poly_tables[power, first, second] = amp * coeff * 2.0**power
    return (scale_table, poly_tables)


def cross_cov(coords_a, vars_a, coords_b, vars_b):
    kernel_tables = make_tables()
    diff_x = coords_a[0][:, None] - coords_b[0][None, :]
    diff_y = coords_a[1][:, None] - coords_b[1][None, :]
    dist = jnp.sqrt(diff_x * diff_x + diff_y * diff_y)
    col_zero = (vars_b == 0)[None, :]
    col_one = (vars_b == 1)[None, :]

    def lookup(table):
        rows = jnp.asarray(table, jnp.float32)[vars_a]
        return jnp.where(col_zero, rows[:, 0:1], jnp.where(col_one, rows[:, 1:2], rows[:, 2:3]))

    scaled = lookup(kernel_tables[0]) * dist
    poly = lookup(kernel_tables[1][4])
    for power in (3, 2, 1, 0):
        poly = poly * scaled + lookup(kernel_tables[1][power])
    return jnp.exp(-scaled) * poly


def couple(coef, src_skel, dst_skel, skel_var, weight):
    blocks = jax.vmap(lambda one, two: cross_cov(one, skel_var, two, skel_var))(src_skel, dst_skel)
    terms = jnp.einsum("nvr,nrq->nvq", coef, blocks, precision=lax.Precision.HIGHEST)
    return terms * weight[:, None, None] / math.sqrt(coef.shape[2])


def shards(
    vectors,
    coords,
    perm,
    bases,
    leaf_maps,
    node_maps,
    leaf_skel,
    node_skel,
    sub_skel,
    leaf_src,
    leaf_count,
    node_src,
    node_count,
):
    high = lax.Precision.HIGHEST
    nvec, rows_dev = vectors.shape
    leaves, rank, block = bases.shape
    node_len = node_src.shape[1]
    groups = lax.axis_size("grp")
    subtrees = lax.axis_size("leaf")
    device_pos = lax.axis_index("leaf") * groups + lax.axis_index("grp")
    tree_vec = jnp.take(vectors, perm, axis=1)
    tree_crd = jnp.take(coords, perm, axis=1)
    leaf_vec = tree_vec.reshape(nvec, leaves, block).transpose(1, 0, 2)
    leaf_crd = tree_crd.reshape(2, leaves, block).transpose(1, 0, 2)
    leaf_var = ((perm + device_pos * rows_dev % 3) % 3).reshape(leaves, block)
    skel_var = jnp.arange(rank, dtype=jnp.int32) % 3
    up_leaf = jnp.einsum("lvb,lrb->lvr", leaf_vec, bases, precision=high)
    grp_pos = lax.axis_index("grp")
    mine = lax.axis_index("leaf")
    leaf_pack = jnp.concatenate([up_leaf, leaf_skel], axis=1)
    group_all = lax.all_gather(leaf_pack, "grp", axis=0, tiled=True)
    group_coef, group_skel = group_all[:, :nvec], group_all[:, nvec:]
    up_node = jnp.einsum("lvr,lrq->vq", up_leaf, leaf_maps, precision=high)
    node_pack = jnp.concatenate([up_node[None], node_skel], axis=1)
    sub_part = jnp.dot(up_node, node_maps[0], precision=high)
    sub_pack = jnp.concatenate([sub_part[None], sub_skel], axis=1)
    nodes = subtrees * groups
    pack = jnp.concatenate([node_pack, sub_pack], axis=2)
    tree_all = lax.all_to_all(
        jnp.broadcast_to(pack, (nodes,) + pack.shape[1:]), ("leaf", "grp"), 0, 0, tiled=True
    )
    subs = tree_all[:, :, rank:].reshape(subtrees, groups, nvec + 2, rank)
    all_subs = jnp.concatenate([subs[:, :, :nvec].sum(axis=1), subs[:, 0, nvec:]], axis=1)

    def owner_step(order, total):
        src = lax.dynamic_slice_in_dim(leaf_src, order, 1, 1)[:, 0]
        weight = (order < leaf_count).astype(jnp.float32)
        return total + couple(group_coef[src], group_skel[src], leaf_skel, skel_var, weight)

    far_leaf = lax.fori_loop(
        jnp.int32(0), jnp.max(leaf_count), owner_step, jnp.zeros((leaves, nvec, rank), jnp.float32)
    )
    beside = jnp.clip(node_src[0] + (mine - 1) * groups, 0, nodes - 1)
    pieces = tree_all[:, :, :rank][beside]
    node_weight = (jnp.arange(node_len, dtype=jnp.int32) < node_count[0]).astype(jnp.float32)
    node_dst = jnp.broadcast_to(node_skel[0], (node_len, 2, rank))
    far_node = couple(pieces[:, :nvec], pieces[:, nvec:], node_dst, skel_var, node_weight).sum(
        axis=0
    )
    others = jnp.arange(subtrees, dtype=jnp.int32)
    sub_weight = (jnp.abs(others - mine) >= 2).astype(jnp.float32)
    sub_dst = jnp.broadcast_to(sub_skel[0], (subtrees, 2, rank))
    far_sub = couple(all_subs[:, :nvec], all_subs[:, nvec:], sub_dst, skel_var, sub_weight).sum(
        axis=0
    )
    down_node = far_node + jnp.dot(far_sub, node_maps[0].T, precision=high)
    down_leaf = far_leaf + jnp.einsum("vq,lrq->lvr", down_node, leaf_maps, precision=high)
    far_rows = jnp.einsum("lvr,lrb->lvb", down_leaf, bases, precision=high)

    def near_block(packed_rows):
        rows_vec, rows_crd, rows_var = packed_rows
        dense = cross_cov(rows_crd, rows_var, rows_crd, rows_var)
        return jnp.dot(rows_vec, dense, precision=high) / math.sqrt(block)

    near = lax.map(near_block, (leaf_vec, leaf_crd, leaf_var))
    tree_out = (far_rows + near).transpose(1, 0, 2).reshape(nvec, rows_dev)
    return jnp.zeros_like(vectors).at[:, perm].set(tree_out)


def solution(mesh):
    placed = (
        P(None, ("leaf", "grp")),
        P(None, ("leaf", "grp")),
        P(("leaf", "grp")),
        P(("leaf", "grp"), None, None),
        P(("leaf", "grp"), None, None),
        P(("leaf", "grp"), None, None),
        P(("leaf", "grp"), None, None),
        P(("leaf", "grp"), None, None),
        P("leaf", None, None),
        P(("leaf", "grp"), None),
        P(("leaf", "grp")),
        P(("leaf", "grp"), None),
        P(("leaf", "grp")),
    )
    return jax.shard_map(
        shards, mesh=mesh, in_specs=placed, out_specs=P(None, ("leaf", "grp")), check_vma=False
    )
```

```python
import math

import jax
import jax.numpy as jnp
import numpy as np
from jax import lax
from jax.experimental import pallas as pl
from jax.experimental.pallas import tpu as pltpu
from jax.sharding import PartitionSpec as P

F32 = jnp.float32
BF16 = jnp.bfloat16
WIDE = 256
SHIFT = 8
LOG2E = math.log2(math.e)
TINY = 1e-37
PACK_ROWS = 24


def make_tables(norm):
    smooth = [0, 2, 4]
    sigmas = [1.0, 0.8, 1.2]
    rho = [[1.0, 0.5, 0.3], [0.5, 1.0, 0.4], [0.3, 0.4, 1.0]]
    scale = np.zeros((3, 3))
    poly = np.zeros((5, 3, 3))
    for first in range(3):
        for second in range(3):
            order = (smooth[first] + smooth[second]) // 2
            scale[first, second] = -(2.0 * order + 1.0) * (LOG2E / 0.3) ** 2
            amp = sigmas[first] * sigmas[second] * rho[first][second] * norm
            for power in range(order + 1):
                kterm = order - power
                coeff = math.factorial(order) / math.factorial(2 * order)
                coeff = (
                    coeff
                    * math.factorial(order + kterm)
                    / (math.factorial(kterm) * math.factorial(order - kterm))
                )
                poly[power, first, second] = amp * coeff * 2.0**power * (-1.0 / LOG2E) ** power
    return scale, poly


def dot(one, two, turned=False):
    dims = (((1,), (1 if turned else 0,)), ((), ()))
    return lax.dot_general(one, two, dims, preferred_element_type=F32)


def parts(value):
    high = value.astype(BF16)
    return high, (value - high.astype(F32)).astype(BF16)


def product(one, two, turned=False):
    rows = one.shape[0]
    one_hi, one_lo = parts(one)
    two_hi, two_lo = parts(two)
    both = dot(jnp.concatenate([one_hi, one_lo], axis=0), two_hi, turned)
    return both[:rows] + both[rows:] + dot(one_hi, two_lo, turned)


def one_hot(low):
    rows = lax.broadcasted_iota(jnp.int32, (WIDE, low.shape[1]), 0)
    return jnp.where(rows == low, 1.0, 0.0).astype(BF16)


def fill(source, value, at, nvec):
    high, low = parts(value)
    source[pl.ds(at, nvec), :WIDE] = high
    source[pl.ds(at, nvec), WIDE:] = low


def pick(source, index, nvec):
    count = index.shape[1]
    hot = one_hot(index & (WIDE - 1))
    hot = jnp.concatenate([hot, hot], axis=0)
    chunk = jnp.broadcast_to(index >> SHIFT, (8, count))[None]
    out = jnp.zeros((nvec // 8, 8, count), F32)
    chunks = source.shape[0] // nvec
    step = 4
    for first in range(0, chunks, step):
        found = dot(source[first * nvec : (first + step) * nvec, :], hot)
        found = found.reshape(step, nvec // 8, 8, count)
        for each in range(step):
            out = jnp.where(chunk == first + each, found[each], out)
    return out.reshape(nvec, count)


def up_kernel(
    vec, perm, bases, leaf_maps, node_maps, leaf_skel, node_skel, sub_skel, tree_vec, leaf_pack, tree_pack, source
):
    leaves, nvec, block = tree_vec.shape
    for each in range(vec.shape[1] // WIDE):
        fill(source, vec[:, each * WIDE : (each + 1) * WIDE], each * nvec, nvec)

    def gather(leaf, carry):
        tree_vec[leaf] = pick(source, perm[pl.ds(leaf, 1), :], nvec)
        return carry

    lax.fori_loop(0, leaves, gather, 0)
    rank = bases.shape[1]
    up_node = jnp.zeros((nvec, rank), F32)
    blank = jnp.zeros((PACK_ROWS - nvec - 2, 2 * rank), F32)
    for leaf in range(leaves):
        up = product(tree_vec[leaf], bases[leaf], True)
        skel = leaf_skel[leaf]
        twice = jnp.concatenate(
            [
                jnp.concatenate([up, up], axis=1),
                jnp.concatenate([skel, skel], axis=1),
                blank,
            ],
            axis=0,
        )
        for each in range(leaf_pack.shape[0]):
            leaf_pack[each, leaf] = twice
        up_node = up_node + product(up, leaf_maps[leaf])
    up_sub = product(up_node, node_maps[0])
    packed = jnp.concatenate(
        [
            jnp.concatenate([up_node, up_sub], axis=1),
            jnp.concatenate([node_skel[0], sub_skel[0]], axis=1),
            blank,
        ],
        axis=0,
    )

    def spread(each, carry):
        tree_pack[each] = packed
        return carry

    lax.fori_loop(0, tree_pack.shape[0], spread, 0)


def near_kernel(shift, tree_vec, crd, perm, near, inverse, flat, source, across, down, slots):
    leaves, nvec, block = tree_vec.shape
    chunks = crd.shape[1] // WIDE
    scale, poly = make_tables(1.0 / math.sqrt(block))
    slope = scale[0, 1] - scale[0, 0]
    for axis in range(2):
        for each in range(chunks):
            row = axis * chunks + each
            flat[row : row + 1, :] = crd[axis : axis + 1, each * WIDE : (each + 1) * WIDE]
    rest = flat[...]
    for piece in range(3):
        rounded = rest.astype(BF16)
        source[:, piece * WIDE : (piece + 1) * WIDE] = rounded
        rest = rest - rounded.astype(F32)
    slots[...] = jnp.zeros_like(slots)
    side = 128
    tiles = block // side

    def one_leaf(leaf, carry):
        index = perm[pl.ds(leaf, 1), :]
        hot = one_hot(index & (WIDE - 1))
        found = (
            dot(source[:, :WIDE], hot)
            + dot(source[:, WIDE : 2 * WIDE], hot)
            + dot(source[:, 2 * WIDE :], hot)
        )
        mine = lax.broadcasted_iota(jnp.int32, (chunks, block), 0) == index >> SHIFT
        lane = lax.broadcasted_iota(jnp.int32, (chunks, block), 1) + leaf * block
        lane_low = (lane % WIDE).astype(F32)
        lane_high = (lane // WIDE).astype(F32)
        marks = jnp.concatenate(
            [jnp.where(mine, lane_low, 0.0), jnp.where(mine, lane_high, 0.0)], axis=0
        ).astype(BF16)
        slots[...] += dot(marks, hot, True)
        row_x = jnp.sum(jnp.where(mine, found[:chunks], 0.0), axis=0, keepdims=True)
        row_y = jnp.sum(jnp.where(mine, found[chunks:], 0.0), axis=0, keepdims=True)
        moved = index + shift[0]
        kind = moved - 3 * ((moved * 43691) >> 17)
        row_w = kind.astype(F32) * slope
        for place, row in enumerate((row_x, row_y, row_w)):
            turned = jnp.transpose(jnp.broadcast_to(row, (side, block)))
            down[place] = turned.reshape(block // 8, 8, side)
        wide_kind = jnp.broadcast_to(kind, (8, block))
        is_zero, is_one = wide_kind == 0, wide_kind == 1
        across[0] = jnp.broadcast_to(row_x, (8, block))
        across[1] = jnp.broadcast_to(row_y, (8, block))
        across[2] = jnp.broadcast_to(row_w, (8, block)) + scale[0, 0]
        for power in range(5):
            for first in range(3):
                across[3 + power * 3 + first] = jnp.where(
                    is_zero,
                    poly[power, first, 0],
                    jnp.where(is_one, poly[power, first, 1], poly[power, first, 2]),
                )
        vec_hi, vec_lo = parts(tree_vec[leaf])
        vec_both = jnp.concatenate([vec_hi, vec_lo], axis=0)
        total = [None] * tiles
        for col in range(tiles):
            cols = slice(col * side, (col + 1) * side)
            table = [across[each, :, cols][None] for each in range(18)]
            high, low = [], []
            for row in range(col + 1):
                rows = slice(row * side // 8, (row + 1) * side // 8)
                diff_x = down[0, rows] - table[0]
                diff_y = down[1, rows] - table[1]
                down_w = down[2, rows]
                var_zero, var_one = down_w > 0.5 * slope, down_w > 1.5 * slope
                square = (diff_x * diff_x + diff_y * diff_y) * (down_w + table[2])
                arg = square * lax.rsqrt(TINY - square)

                def lookup(power):
                    a, b, c = table[3 + power * 3 : 6 + power * 3]
                    return jnp.where(var_zero, a, jnp.where(var_one, b, c))

                value = lookup(4)
                for power in (3, 2, 1, 0):
                    value = value * arg + lookup(power)
                value = (value * jnp.exp2(arg)).reshape(side, side)
                value_hi, value_lo = parts(value)
                high.append(value_hi)
                low.append(value_lo)
            high = jnp.concatenate(high, axis=0)
            low = jnp.concatenate(low, axis=0)
            upto = (col + 1) * side
            both = dot(vec_both[:, :upto], high)
            total[col] = both[:nvec] + both[nvec:] + dot(vec_hi[:, :upto], low)
            if col > 0:
                both = dot(vec_both[:, cols], high[: col * side], True)
                back = both[:nvec] + both[nvec:] + dot(vec_hi[:, cols], low[: col * side], True)
                for row in range(col):
                    total[row] = total[row] + back[:, row * side : (row + 1) * side]
        for col in range(tiles):
            near[leaf, :, col * side : (col + 1) * side] = total[col]
        return carry

    lax.fori_loop(0, leaves, one_leaf, 0)
    inverse[...] = (slots[:chunks] + slots[chunks:] * WIDE).astype(jnp.int32)


def far_kernel(
    place,
    leaf_src,
    leaf_count,
    node_src,
    node_count,
    leaf_all,
    tree_all,
    leaf_skel,
    node_skel,
    sub_skel,
    near,
    inverse,
    bases,
    leaf_maps,
    node_maps,
    tables,
    out,
    source,
    coef,
    subs,
):
    leaves, nvec, block = near.shape
    rank = bases.shape[1]
    subtrees = subs.shape[0]
    groups = tree_all.shape[0] // subtrees
    sub_pos = place[0]
    left = lax.broadcasted_iota(jnp.int32, (PACK_ROWS, 2 * rank), 1) < rank
    left_vec = lax.broadcasted_iota(jnp.int32, (nvec, 2 * rank), 1)

    def upright(row):
        return jnp.transpose(jnp.broadcast_to(row, (2 * rank, rank)))

    def term(packs, lives, col_x, col_y):
        row_x, row_y = packs[nvec : nvec + 1], packs[nvec + 1 : nvec + 2]
        diff_x, diff_y = col_x - row_x, col_y - row_y
        square = (diff_x * diff_x + diff_y * diff_y) * tables[0]
        arg = square * lax.rsqrt(TINY - square)
        value = tables[5]
        for power in (4, 3, 2, 1):
            value = value * arg + tables[power]
        value = value * jnp.exp2(arg)
        return product(jnp.where(lives, packs[:nvec], 0.0), value, True)

    def one_leaf(leaf, carry):
        count = leaf_count[leaf]
        skel = leaf_skel[leaf]
        col_x, col_y = upright(skel[0:1]), upright(skel[1:2])

        def pair(step, total):
            first = leaf_src[leaf, 2 * step]
            second = leaf_src[leaf, 2 * step + 1]
            packs = jnp.where(left, leaf_all[first], leaf_all[second])
            lives = left_vec < (count - 2 * step) * rank
            return total + term(packs, lives, col_x, col_y)

        coef[leaf] = lax.fori_loop(0, (count + 1) // 2, pair, jnp.zeros((nvec, rank), F32))
        return carry

    lax.fori_loop(0, leaves, one_leaf, 0)

    nodes = tree_all.shape[0]
    count = node_count[0]
    col_x, col_y = upright(node_skel[0, 0:1]), upright(node_skel[0, 1:2])
    base = (sub_pos - 1) * groups

    def node_pair(step, total):
        first = jnp.clip(node_src[0, 2 * step] + base, 0, nodes - 1)
        second = jnp.clip(node_src[0, 2 * step + 1] + base, 0, nodes - 1)
        packs = jnp.where(left, tree_all[first], pltpu.roll(tree_all[second], rank, 1))
        lives = left_vec < (count - 2 * step) * rank
        return total + term(packs, lives, col_x, col_y)

    down_node = lax.fori_loop(0, (count + 1) // 2, node_pair, jnp.zeros((nvec, rank), F32))

    def add_up(sub, carry):
        total = tree_all[sub * groups]
        for each in range(1, groups):
            total = total + tree_all[sub * groups + each]
        subs[sub, :nvec] = total[:nvec]
        subs[sub, nvec:] = tree_all[sub * groups, nvec:]
        return carry

    lax.fori_loop(0, subtrees, add_up, 0)
    col_x, col_y = upright(sub_skel[0, 0:1]), upright(sub_skel[0, 1:2])

    def sub_pair(step, total):
        first = 2 * step
        packs = jnp.where(left, pltpu.roll(subs[first], rank, 1), subs[first + 1])
        apart = jnp.abs(jnp.where(left_vec < rank, first, first + 1) - sub_pos)
        return total + term(packs, apart >= 2, col_x, col_y)

    far_sub = lax.fori_loop(0, subtrees // 2, sub_pair, jnp.zeros((nvec, rank), F32))
    down_node = down_node + product(far_sub, node_maps[0], True)
    for leaf in range(leaves):
        down_leaf = coef[leaf] + product(down_node, leaf_maps[leaf], True)
        rows = near[leaf] + product(down_leaf, bases[leaf])
        for each in range(block // WIDE):
            fill(
                source,
                rows[:, each * WIDE : (each + 1) * WIDE],
                (leaf * (block // WIDE) + each) * nvec,
                nvec,
            )

    def scatter(each, carry):
        at = pl.multiple_of(each * WIDE, WIDE)
        out[:, pl.ds(at, WIDE)] = pick(source, inverse[pl.ds(each, 1), :], nvec)
        return carry

    lax.fori_loop(0, inverse.shape[0], scatter, 0)


def skeleton_tables(rank):
    scale, poly = make_tables(1.0 / math.sqrt(rank))
    var = np.arange(rank) % 3
    rows, cols = var[:, None], np.tile(var, 2)[None, :]
    return np.stack([scale[rows, cols]] + [poly[power][rows, cols] for power in range(5)]).astype(
        np.float32
    )


def shards(
    vectors,
    coords,
    perm,
    bases,
    leaf_maps,
    node_maps,
    leaf_skel,
    node_skel,
    sub_skel,
    leaf_src,
    leaf_count,
    node_src,
    node_count,
):
    nvec, rows_dev = vectors.shape
    leaves, rank, block = bases.shape
    groups = lax.axis_size("grp")
    subtrees = lax.axis_size("leaf")
    nodes = groups * subtrees
    sub_pos = lax.axis_index("leaf")
    device_pos = sub_pos * groups + lax.axis_index("grp")
    chunks = rows_dev // WIDE
    vmem = pl.BlockSpec(memory_space=pltpu.VMEM)
    smem = pl.BlockSpec(memory_space=pltpu.SMEM)
    params = pltpu.CompilerParams(vmem_limit_bytes=48 * 1024 * 1024)
    order = perm.reshape(leaves, block)
    tree_vec, leaf_pack, tree_pack = pl.pallas_call(
        up_kernel,
        out_shape=(
            jax.ShapeDtypeStruct((leaves, nvec, block), F32),
            jax.ShapeDtypeStruct((groups, leaves, PACK_ROWS, 2 * rank), F32),
            jax.ShapeDtypeStruct((nodes, PACK_ROWS, 2 * rank), F32),
        ),
        in_specs=[vmem] * 8,
        out_specs=(vmem,) * 3,
        scratch_shapes=[pltpu.VMEM((chunks * nvec, 2 * WIDE), BF16)],
        compiler_params=params,
        name="up",
    )(vectors, order, bases, leaf_maps, node_maps, leaf_skel, node_skel, sub_skel)
    tree_all = lax.all_to_all(tree_pack, ("leaf", "grp"), 0, 0, tiled=True)
    leaf_all = lax.all_to_all(leaf_pack, "grp", 0, 0, tiled=True)
    shift = (device_pos * (rows_dev % 3) % 3).astype(jnp.int32).reshape(1)
    near, inverse = pl.pallas_call(
        near_kernel,
        out_shape=(
            jax.ShapeDtypeStruct((leaves, nvec, block), F32),
            jax.ShapeDtypeStruct((chunks, WIDE), jnp.int32),
        ),
        in_specs=[smem] + [vmem] * 3,
        out_specs=(vmem,) * 2,
        scratch_shapes=[
            pltpu.VMEM((2 * chunks, WIDE), F32),
            pltpu.VMEM((2 * chunks, 3 * WIDE), BF16),
            pltpu.VMEM((18, 8, block), F32),
            pltpu.VMEM((3, block // 8, 8, 128), F32),
            pltpu.VMEM((2 * chunks, WIDE), F32),
        ],
        compiler_params=params,
        cost_estimate=pl.CostEstimate(
            flops=2 * 16 * leaves * block * block * 4, bytes_accessed=4 * leaves * nvec * block * 2, transcendentals=leaves * block * block
        ),
        name="near",
    )(shift, tree_vec, coords, order)
    return pl.pallas_call(
        far_kernel,
        out_shape=jax.ShapeDtypeStruct((nvec, rows_dev), F32),
        in_specs=[smem] * 5 + [vmem] * 11,
        out_specs=vmem,
        scratch_shapes=[
            pltpu.VMEM((chunks * nvec, 2 * WIDE), BF16),
            pltpu.VMEM((leaves, nvec, rank), F32),
            pltpu.VMEM((subtrees, PACK_ROWS, 2 * rank), F32),
        ],
        compiler_params=params,
        name="far",
    )(
        sub_pos.astype(jnp.int32).reshape(1),
        leaf_src,
        leaf_count,
        node_src,
        node_count,
        leaf_all.reshape(groups * leaves, PACK_ROWS, 2 * rank),
        tree_all,
        leaf_skel,
        node_skel,
        sub_skel,
        near,
        inverse,
        bases,
        leaf_maps,
        node_maps,
        jnp.asarray(skeleton_tables(rank)),
    )


def solution(mesh):
    placed = (
        P(None, ("leaf", "grp")),
        P(None, ("leaf", "grp")),
        P(("leaf", "grp")),
        P(("leaf", "grp"), None, None),
        P(("leaf", "grp"), None, None),
        P(("leaf", "grp"), None, None),
        P(("leaf", "grp"), None, None),
        P(("leaf", "grp"), None, None),
        P("leaf", None, None),
        P(("leaf", "grp"), None),
        P(("leaf", "grp")),
        P(("leaf", "grp"), None),
        P(("leaf", "grp")),
    )
    return jax.shard_map(
        shards, mesh=mesh, in_specs=placed, out_specs=P(None, ("leaf", "grp")), check_vma=False
    )
```

```python
import functools
import math

import jax
import jax.numpy as jnp
import numpy as np
from jax import lax
from jax.experimental import pallas as pl
from jax.experimental.pallas import tpu as pltpu
from jax.sharding import PartitionSpec as P

F32 = jnp.float32
BF16 = jnp.bfloat16
WIDE = 256
SHIFT = 8
LOG2E = math.log2(math.e)
TINY = 1e-37
PACK_ROWS = 24
AT_ONCE = 4


def make_tables(norm):
    smooth = [0, 2, 4]
    sigmas = [1.0, 0.8, 1.2]
    rho = [[1.0, 0.5, 0.3], [0.5, 1.0, 0.4], [0.3, 0.4, 1.0]]
    scale = np.zeros((3, 3))
    poly = np.zeros((5, 3, 3))
    for first in range(3):
        for second in range(3):
            order = (smooth[first] + smooth[second]) // 2
            scale[first, second] = -(2.0 * order + 1.0) * (LOG2E / 0.3) ** 2
            amp = sigmas[first] * sigmas[second] * rho[first][second] * norm
            for power in range(order + 1):
                kterm = order - power
                coeff = math.factorial(order) / math.factorial(2 * order)
                coeff = (
                    coeff
                    * math.factorial(order + kterm)
                    / (math.factorial(kterm) * math.factorial(order - kterm))
                )
                poly[power, first, second] = amp * coeff * 2.0**power * (-1.0 / LOG2E) ** power
    return scale, poly


def dot(one, two, turned=False):
    dims = (((1,), (1 if turned else 0,)), ((), ()))
    return lax.dot_general(one, two, dims, preferred_element_type=F32)


def parts(value):
    high = value.astype(BF16)
    return high, (value - high.astype(F32)).astype(BF16)


def product(one, two, turned=False):
    rows = one.shape[0]
    one_hi, one_lo = parts(one)
    two_hi, two_lo = parts(two)
    both = dot(jnp.concatenate([one_hi, one_lo], axis=0), two_hi, turned)
    return both[:rows] + both[rows:] + dot(one_hi, two_lo, turned)


def one_hot(low):
    rows = lax.broadcasted_iota(jnp.int32, (WIDE, low.shape[1]), 0)
    return jnp.where(rows == low, 1.0, 0.0).astype(BF16)


def fill(source, value, at, nvec):
    high, low = parts(value)
    source[pl.ds(at, nvec), :WIDE] = high
    source[pl.ds(at, nvec), WIDE:] = low


def pick(source, index, nvec):
    count = index.shape[1]
    hot = one_hot(index & (WIDE - 1))
    hot = jnp.concatenate([hot, hot], axis=0)
    chunk = jnp.broadcast_to(index >> SHIFT, (8, count))[None]
    out = jnp.zeros((nvec // 8, 8, count), F32)
    chunks = source.shape[0] // nvec
    found = dot(source[...], hot).reshape(chunks, nvec // 8, 8, count)
    for each in range(chunks):
        out = jnp.where(chunk == each, found[each], out)
    return out.reshape(nvec, count)


def leaf_index(perm, leaf, block):
    rows = block // 128
    return jnp.concatenate([perm[pl.ds(leaf * rows + each, 1), :] for each in range(rows)], axis=1)


def fetch(pairs, sems):
    copies = [pltpu.make_async_copy(src, dst, sems.at[each]) for each, (src, dst) in enumerate(pairs)]
    for copy in copies:
        copy.start()
    return copies


def up_kernel(*refs):
    given, (tree_vec, leaf_pack, tree_pack) = refs[:8], refs[8:11]
    held, source, sems = refs[11:19], refs[19], refs[20]
    copies = fetch(list(zip(given, held)), sems)
    vec, perm, bases, leaf_maps, node_maps, leaf_skel, node_skel, sub_skel = held
    leaves, nvec, block = tree_vec.shape
    rank = bases.shape[1]
    copies[0].wait()
    for each in range(vec.shape[1] // WIDE):
        fill(source, vec[:, each * WIDE : (each + 1) * WIDE], each * nvec, nvec)
    copies[1].wait()

    def gather(leaf, carry):
        tree_vec[leaf] = pick(source, leaf_index(perm, leaf, block), nvec)
        return carry

    lax.fori_loop(0, leaves, gather, 0)
    for copy in copies[2:]:
        copy.wait()
    up_node = jnp.zeros((nvec, rank), F32)
    blank = jnp.zeros((PACK_ROWS - nvec - 2, 2 * rank), F32)
    for leaf in range(0, leaves, 2):
        up = [product(tree_vec[leaf + each], bases[leaf + each], True) for each in range(2)]
        leaf_pack[leaf // 2] = jnp.concatenate(
            [
                jnp.concatenate(up, axis=1),
                jnp.concatenate([leaf_skel[leaf], leaf_skel[leaf + 1]], axis=1),
                blank,
            ],
            axis=0,
        )
        for each in range(2):
            up_node = up_node + product(up[each], leaf_maps[leaf + each])
    up_sub = product(up_node, node_maps[0])
    packed = jnp.concatenate(
        [
            jnp.concatenate([up_node, up_sub], axis=1),
            jnp.concatenate([node_skel[0], sub_skel[0]], axis=1),
            blank,
        ],
        axis=0,
    )

    def spread(each, carry):
        tree_pack[each] = packed
        return carry

    lax.fori_loop(0, tree_pack.shape[0], spread, 0)


def near_kernel(
    shift, tree_vec, crd_in, perm_in, near, inverse, crd, perm, flat, source, across, down, slots, sems
):
    copies = fetch([(crd_in, crd), (perm_in, perm)], sems)
    for copy in copies:
        copy.wait()
    leaves, nvec, block = tree_vec.shape
    chunks = crd.shape[1] // WIDE
    scale, poly = make_tables(1.0 / math.sqrt(block))
    slope = scale[0, 1] - scale[0, 0]
    for axis in range(2):
        for each in range(chunks):
            row = axis * chunks + each
            flat[row : row + 1, :] = crd[axis : axis + 1, each * WIDE : (each + 1) * WIDE]
    rest = flat[...]
    for piece in range(3):
        rounded = rest.astype(BF16)
        source[:, piece * WIDE : (piece + 1) * WIDE] = rounded
        rest = rest - rounded.astype(F32)
    slots[...] = jnp.zeros_like(slots)
    side = 128
    tiles = block // side

    def one_leaf(leaf, carry):
        index = leaf_index(perm, leaf, block)
        hot = one_hot(index & (WIDE - 1))
        found = (
            dot(source[:, :WIDE], hot)
            + dot(source[:, WIDE : 2 * WIDE], hot)
            + dot(source[:, 2 * WIDE :], hot)
        )
        mine = lax.broadcasted_iota(jnp.int32, (chunks, block), 0) == index >> SHIFT
        lane = lax.broadcasted_iota(jnp.int32, (chunks, block), 1) + leaf * block
        lane_low = (lane % WIDE).astype(F32)
        lane_high = (lane // WIDE).astype(F32)
        marks = jnp.concatenate(
            [jnp.where(mine, lane_low, 0.0), jnp.where(mine, lane_high, 0.0)], axis=0
        ).astype(BF16)
        slots[...] += dot(marks, hot, True)
        row_x = jnp.sum(jnp.where(mine, found[:chunks], 0.0), axis=0, keepdims=True)
        row_y = jnp.sum(jnp.where(mine, found[chunks:], 0.0), axis=0, keepdims=True)
        moved = index + shift[0]
        kind = moved - 3 * ((moved * 43691) >> 17)
        row_w = kind.astype(F32) * slope
        for place, row in enumerate((row_x, row_y, row_w)):
            turned = jnp.transpose(jnp.broadcast_to(row, (side, block)))
            down[place] = turned.reshape(block // 8, 8, side)
        wide_kind = jnp.broadcast_to(kind, (8, block))
        is_zero, is_one = wide_kind == 0, wide_kind == 1
        across[0] = jnp.broadcast_to(row_x, (8, block))
        across[1] = jnp.broadcast_to(row_y, (8, block))
        across[2] = jnp.broadcast_to(row_w, (8, block)) + scale[0, 0]
        for power in range(5):
            for first in range(3):
                across[3 + power * 3 + first] = jnp.where(
                    is_zero,
                    poly[power, first, 0],
                    jnp.where(is_one, poly[power, first, 1], poly[power, first, 2]),
                )
        vec_hi, vec_lo = parts(tree_vec[leaf])
        vec_both = jnp.concatenate([vec_hi, vec_lo], axis=0)
        total = [None] * tiles
        for col in range(tiles):
            cols = slice(col * side, (col + 1) * side)
            table = [across[each, :, cols][None] for each in range(18)]
            high, low = [], []
            for row in range(col + 1):
                rows = slice(row * side // 8, (row + 1) * side // 8)
                diff_x = down[0, rows] - table[0]
                diff_y = down[1, rows] - table[1]
                down_w = down[2, rows]
                var_zero, var_one = down_w > 0.5 * slope, down_w > 1.5 * slope
                square = (diff_x * diff_x + diff_y * diff_y) * (down_w + table[2])
                arg = square * lax.rsqrt(TINY - square)

                def lookup(power):
                    a, b, c = table[3 + power * 3 : 6 + power * 3]
                    return jnp.where(var_zero, a, jnp.where(var_one, b, c))

                value = lookup(4)
                for power in (3, 2, 1, 0):
                    value = value * arg + lookup(power)
                value = (value * jnp.exp2(arg)).reshape(side, side)
                value_hi, value_lo = parts(value)
                high.append(value_hi)
                low.append(value_lo)
            high = jnp.concatenate(high, axis=0)
            low = jnp.concatenate(low, axis=0)
            upto = (col + 1) * side
            both = dot(vec_both[:, :upto], high)
            total[col] = both[:nvec] + both[nvec:] + dot(vec_hi[:, :upto], low)
            if col > 0:
                both = dot(vec_both[:, cols], high[: col * side], True)
                back = both[:nvec] + both[nvec:] + dot(vec_hi[:, cols], low[: col * side], True)
                for row in range(col):
                    total[row] = total[row] + back[:, row * side : (row + 1) * side]
        for col in range(tiles):
            near[leaf, :, col * side : (col + 1) * side] = total[col]
        return carry

    lax.fori_loop(0, leaves, one_leaf, 0)
    inverse[...] = (slots[:chunks] + slots[chunks:] * WIDE).astype(jnp.int32)


def far_kernel(groups, subtrees, *refs):
    place, leaf_src, leaf_count, node_src, node_count, leaf_all, tree_all, near, inverse = refs[:9]
    given, out = refs[9:16], refs[16]
    held = refs[17:24]
    source, coef, twice, cols, srcs, dsts, sems = refs[24:]
    copies = fetch(list(zip(given, held)), sems)
    leaf_skel, node_skel, sub_skel, tables, leaf_maps, node_maps, bases = held
    leaves, nvec, block = near.shape
    rank = bases.shape[1]
    nodes = tree_all.shape[0]
    pairs = leaf_all.shape[0]
    node_at = 2 * pairs
    beside = 3 * groups
    sub_at = node_at + beside
    blank = sub_at + subtrees
    sub_pos = place[0]
    left = lax.broadcasted_iota(jnp.int32, (PACK_ROWS, 2 * rank), 1) < rank

    def list_leaf(leaf, at):
        count = leaf_count[leaf]

        def one(step, carry):
            srcs[2 * (at + step)] = leaf_src[leaf, 2 * step]
            second = jnp.where(2 * step + 1 < count, leaf_src[leaf, 2 * step + 1], blank)
            srcs[2 * (at + step) + 1] = second
            dsts[at + step] = leaf
            return carry

        steps = (count + 1) // 2
        lax.fori_loop(0, steps, one, 0)
        return at + steps

    size = lax.fori_loop(0, leaves, list_leaf, 0)
    count = node_count[0]

    def list_node(step, carry):
        srcs[2 * (size + step)] = node_at + node_src[0, 2 * step]
        second = jnp.where(2 * step + 1 < count, node_at + node_src[0, 2 * step + 1], blank)
        srcs[2 * (size + step) + 1] = second
        dsts[size + step] = leaves
        return carry

    steps = (count + 1) // 2
    lax.fori_loop(0, steps, list_node, 0)

    def list_sub(sub, at):
        srcs[at] = sub_at + sub
        dsts[at // 2] = leaves + 1
        return at + jnp.where(jnp.abs(sub - sub_pos) >= 2, 1, 0)

    ends = lax.fori_loop(0, subtrees, list_sub, 2 * (size + steps))
    srcs[ends] = blank
    dsts[ends // 2] = leaves + 1
    ends = (ends + 1) // 2
    for each in range(AT_ONCE):
        srcs[2 * (ends + each)] = blank
        srcs[2 * (ends + each) + 1] = blank
        dsts[ends + each] = leaves + 1

    def both_leaves(pair, carry):
        packs = leaf_all[pair]
        turned = pltpu.roll(packs, rank, 1)
        twice[2 * pair] = jnp.where(left, packs, turned)
        twice[2 * pair + 1] = jnp.where(left, turned, packs)
        return carry

    lax.fori_loop(0, pairs, both_leaves, 0)

    def both_node(each, carry):
        packs = tree_all[jnp.clip((sub_pos - 1) * groups + each, 0, nodes - 1)]
        twice[node_at + each] = jnp.where(left, packs, pltpu.roll(packs, rank, 1))
        return carry

    lax.fori_loop(0, beside, both_node, 0)

    def both_sub(sub, carry):
        total = tree_all[sub * groups, :nvec]
        for each in range(1, groups):
            total = total + tree_all[sub * groups + each, :nvec]
        packs = jnp.concatenate([total, tree_all[sub * groups, nvec:]], axis=0)
        twice[sub_at + sub] = jnp.where(left, pltpu.roll(packs, rank, 1), packs)
        return carry

    lax.fori_loop(0, subtrees, both_sub, 0)
    twice[blank] = jnp.zeros_like(twice[blank])
    coef[...] = jnp.zeros_like(coef)
    for copy in copies[:4]:
        copy.wait()

    def upright(skel, at):
        for axis in range(2):
            row = jnp.broadcast_to(skel[axis : axis + 1], (2 * rank, rank))
            cols[at, axis] = jnp.transpose(row)

    def upright_leaf(leaf, carry):
        upright(leaf_skel[leaf], leaf)
        return carry

    lax.fori_loop(0, leaves, upright_leaf, 0)
    upright(node_skel[0], leaves)
    upright(sub_skel[0], leaves + 1)

    def couple(step, carry):
        terms = []
        for each in range(AT_ONCE):
            item = step * AT_ONCE + each
            packs = jnp.where(left, twice[srcs[2 * item]], twice[srcs[2 * item + 1]])
            target = dsts[item]
            diff_x = cols[target, 0] - packs[nvec : nvec + 1]
            diff_y = cols[target, 1] - packs[nvec + 1 : nvec + 2]
            square = (diff_x * diff_x + diff_y * diff_y) * tables[0]
            arg = square * lax.rsqrt(TINY - square)
            value = tables[5]
            for power in (4, 3, 2, 1):
                value = value * arg + tables[power]
            value = value * jnp.exp2(arg)
            terms.append((target, product(packs[:nvec], value, True)))
        for target, total in terms:
            coef[target] += total
        return carry

    lax.fori_loop(0, (ends + AT_ONCE - 1) // AT_ONCE, couple, 0)
    for copy in copies[4:]:
        copy.wait()
    down_node = coef[leaves] + product(coef[leaves + 1], node_maps[0], True)
    for leaf in range(leaves):
        down_leaf = coef[leaf] + product(down_node, leaf_maps[leaf], True)
        rows = near[leaf] + product(down_leaf, bases[leaf])
        for each in range(block // WIDE):
            fill(
                source,
                rows[:, each * WIDE : (each + 1) * WIDE],
                (leaf * (block // WIDE) + each) * nvec,
                nvec,
            )

    def scatter(each, carry):
        at = pl.multiple_of(each * 2 * WIDE, 2 * WIDE)
        index = jnp.concatenate(
            [inverse[pl.ds(2 * each, 1), :], inverse[pl.ds(2 * each + 1, 1), :]], axis=1
        )
        out[:, pl.ds(at, 2 * WIDE)] = pick(source, index, nvec)
        return carry

    lax.fori_loop(0, inverse.shape[0] // 2, scatter, 0)


def skeleton_tables(rank):
    scale, poly = make_tables(1.0 / math.sqrt(rank))
    var = np.arange(rank) % 3
    rows, cols = var[:, None], np.tile(var, 2)[None, :]
    return np.stack([scale[rows, cols]] + [poly[power][rows, cols] for power in range(5)]).astype(
        np.float32
    )


def shards(
    vectors,
    coords,
    perm,
    bases,
    leaf_maps,
    node_maps,
    leaf_skel,
    node_skel,
    sub_skel,
    leaf_src,
    leaf_count,
    node_src,
    node_count,
):
    nvec, rows_dev = vectors.shape
    leaves, rank, block = bases.shape
    groups = lax.axis_size("grp")
    subtrees = lax.axis_size("leaf")
    nodes = groups * subtrees
    sub_pos = lax.axis_index("leaf")
    device_pos = sub_pos * groups + lax.axis_index("grp")
    chunks = rows_dev // WIDE
    vmem = pl.BlockSpec(memory_space=pltpu.VMEM)
    smem = pl.BlockSpec(memory_space=pltpu.SMEM)
    hbm = pl.BlockSpec(memory_space=pl.ANY)
    params = pltpu.CompilerParams(vmem_limit_bytes=20 * 1024 * 1024)
    order = perm.reshape(rows_dev // 128, 128)

    def like(*arrays):
        return [pltpu.VMEM(each.shape, each.dtype) for each in arrays]

    given = (vectors, order, bases, leaf_maps, node_maps, leaf_skel, node_skel, sub_skel)
    tree_vec, leaf_pack, tree_pack = pl.pallas_call(
        up_kernel,
        out_shape=(
            jax.ShapeDtypeStruct((leaves, nvec, block), F32),
            jax.ShapeDtypeStruct((leaves // 2, PACK_ROWS, 2 * rank), F32),
            jax.ShapeDtypeStruct((nodes, PACK_ROWS, 2 * rank), F32),
        ),
        in_specs=[hbm] * 8,
        out_specs=(vmem,) * 3,
        scratch_shapes=like(*given)
        + [pltpu.VMEM((chunks * nvec, 2 * WIDE), BF16), pltpu.SemaphoreType.DMA((8,))],
        compiler_params=params,
        name="up",
    )(*given)
    tree_all = lax.all_to_all(tree_pack, ("leaf", "grp"), 0, 0, tiled=True)
    leaf_all = lax.all_gather(leaf_pack, "grp", axis=0, tiled=True)
    shift = (device_pos * (rows_dev % 3) % 3).astype(jnp.int32).reshape(1)
    near, inverse = pl.pallas_call(
        near_kernel,
        out_shape=(
            jax.ShapeDtypeStruct((leaves, nvec, block), F32),
            jax.ShapeDtypeStruct((chunks, WIDE), jnp.int32),
        ),
        in_specs=[smem, vmem, hbm, hbm],
        out_specs=(vmem,) * 2,
        scratch_shapes=like(coords, order)
        + [
            pltpu.VMEM((2 * chunks, WIDE), F32),
            pltpu.VMEM((2 * chunks, 3 * WIDE), BF16),
            pltpu.VMEM((18, 8, block), F32),
            pltpu.VMEM((3, block // 8, 8, 128), F32),
            pltpu.VMEM((2 * chunks, WIDE), F32),
            pltpu.SemaphoreType.DMA((2,)),
        ],
        compiler_params=params,
        cost_estimate=pl.CostEstimate(
            flops=128 * leaves * block * block,
            bytes_accessed=8 * leaves * nvec * block,
            transcendentals=leaves * block * block,
        ),
        name="near",
    )(shift, tree_vec, coords, order)
    given = (leaf_skel, node_skel, sub_skel, jnp.asarray(skeleton_tables(rank)), leaf_maps, node_maps, bases)
    items = (leaf_src.size + node_src.size + subtrees + 2) // 2 + AT_ONCE
    sources = groups * leaves + 3 * groups + subtrees + 1
    return pl.pallas_call(
        functools.partial(far_kernel, groups, subtrees),
        out_shape=jax.ShapeDtypeStruct((nvec, rows_dev), F32),
        in_specs=[smem] * 5 + [vmem] * 4 + [hbm] * 7,
        out_specs=vmem,
        scratch_shapes=like(*given)
        + [
            pltpu.VMEM((chunks * nvec, 2 * WIDE), BF16),
            pltpu.VMEM((leaves + 2, nvec, rank), F32),
            pltpu.VMEM((sources, PACK_ROWS, 2 * rank), F32),
            pltpu.VMEM((leaves + 2, 2, rank, 2 * rank), F32),
            pltpu.SMEM((2 * items,), jnp.int32),
            pltpu.SMEM((items,), jnp.int32),
            pltpu.SemaphoreType.DMA((7,)),
        ],
        compiler_params=params,
        name="far",
    )(
        sub_pos.astype(jnp.int32).reshape(1),
        leaf_src,
        leaf_count,
        node_src,
        node_count,
        leaf_all,
        tree_all,
        near,
        inverse,
        *given,
    )


def solution(mesh):
    placed = (
        P(None, ("leaf", "grp")),
        P(None, ("leaf", "grp")),
        P(("leaf", "grp")),
        P(("leaf", "grp"), None, None),
        P(("leaf", "grp"), None, None),
        P(("leaf", "grp"), None, None),
        P(("leaf", "grp"), None, None),
        P(("leaf", "grp"), None, None),
        P("leaf", None, None),
        P(("leaf", "grp"), None),
        P(("leaf", "grp")),
        P(("leaf", "grp"), None),
        P(("leaf", "grp")),
    )
    return jax.shard_map(
        shards, mesh=mesh, in_specs=placed, out_specs=P(None, ("leaf", "grp")), check_vma=False
    )
```

```python
import functools
import math

import jax
import jax.numpy as jnp
import numpy as np
from jax import lax
from jax.experimental import pallas as pl
from jax.experimental.pallas import tpu as pltpu
from jax.sharding import PartitionSpec as P

F32 = jnp.float32
BF16 = jnp.bfloat16
WIDE = 256
SHIFT = 8
LOG2E = math.log2(math.e)
TINY = 1e-37
PACK_ROWS = 24
AT_ONCE = 4


def make_tables(norm):
    smooth = [0, 2, 4]
    sigmas = [1.0, 0.8, 1.2]
    rho = [[1.0, 0.5, 0.3], [0.5, 1.0, 0.4], [0.3, 0.4, 1.0]]
    scale = np.zeros((3, 3))
    poly = np.zeros((5, 3, 3))
    for first in range(3):
        for second in range(3):
            order = (smooth[first] + smooth[second]) // 2
            scale[first, second] = -(2.0 * order + 1.0) * (LOG2E / 0.3) ** 2
            amp = sigmas[first] * sigmas[second] * rho[first][second] * norm
            for power in range(order + 1):
                kterm = order - power
                coeff = math.factorial(order) / math.factorial(2 * order)
                coeff = (
                    coeff
                    * math.factorial(order + kterm)
                    / (math.factorial(kterm) * math.factorial(order - kterm))
                )
                poly[power, first, second] = amp * coeff * 2.0**power * (-1.0 / LOG2E) ** power
    return scale, poly


def dot(one, two, turned=False):
    dims = (((1,), (1 if turned else 0,)), ((), ()))
    return lax.dot_general(one, two, dims, preferred_element_type=F32)


def parts(value):
    high = value.astype(BF16)
    return high, (value - high.astype(F32)).astype(BF16)


def product(one, two, turned=False):
    rows = one.shape[0]
    one_hi, one_lo = parts(one)
    two_hi, two_lo = parts(two)
    both = dot(jnp.concatenate([one_hi, one_lo], axis=0), two_hi, turned)
    return both[:rows] + both[rows:] + dot(one_hi, two_lo, turned)


def count_rows(rows):
    rows[...] = lax.broadcasted_iota(jnp.int32, rows.shape, 0).astype(jnp.int16)


def one_hot(rows, low):
    count = low.shape[1]
    low = jnp.broadcast_to(low, (16, count)).astype(jnp.int16)[None]
    same = rows[:, :count].reshape(WIDE // 16, 16, count) == low
    return jnp.where(same, jnp.bfloat16(1), jnp.bfloat16(0)).reshape(WIDE, count)


def fill(source, value, at, nvec):
    high, low = parts(value)
    source[pl.ds(at, nvec), :WIDE] = high
    source[pl.ds(at, nvec), WIDE:] = low


def pick(rows, source, index, nvec):
    count = index.shape[1]
    hot = one_hot(rows, index & (WIDE - 1))
    hot = jnp.concatenate([hot, hot], axis=0)
    chunk = jnp.broadcast_to(index >> SHIFT, (8, count))[None]
    out = jnp.zeros((nvec // 8, 8, count), F32)
    chunks = source.shape[0] // nvec
    found = dot(source[...], hot).reshape(chunks, nvec // 8, 8, count)
    for each in range(chunks):
        out = jnp.where(chunk == each, found[each], out)
    return out.reshape(nvec, count)


def leaf_index(perm, leaf, block):
    rows = block // 128
    return jnp.concatenate([perm[pl.ds(leaf * rows + each, 1), :] for each in range(rows)], axis=1)


def fetch(pairs, sems):
    copies = [pltpu.make_async_copy(src, dst, sems.at[each]) for each, (src, dst) in enumerate(pairs)]
    for copy in copies:
        copy.start()
    return copies


def up_kernel(*refs):
    given, (tree_out, leaf_pack, tree_pack) = refs[:8], refs[8:11]
    held = refs[11:19]
    tree_vec, source, rows, sems = refs[19:]
    count_rows(rows)
    copies = fetch(list(zip(given, held)), sems)
    vec, perm, bases, leaf_maps, node_maps, leaf_skel, node_skel, sub_skel = held
    leaves, nvec, block = tree_vec.shape
    rank = bases.shape[1]
    copies[0].wait()
    for each in range(vec.shape[1] // WIDE):
        fill(source, vec[:, each * WIDE : (each + 1) * WIDE], each * nvec, nvec)
    copies[1].wait()

    def gather(leaf, carry):
        tree_vec[leaf] = pick(rows, source, leaf_index(perm, leaf, block), nvec)
        return carry

    lax.fori_loop(0, leaves, gather, 0, unroll=2)
    leave = pltpu.make_async_copy(tree_vec, tree_out, sems.at[len(copies)])
    leave.start()
    for copy in copies[2:]:
        copy.wait()
    up_node = jnp.zeros((nvec, rank), F32)
    blank = jnp.zeros((PACK_ROWS - nvec - 2, 2 * rank), F32)
    for leaf in range(0, leaves, 2):
        up = [product(tree_vec[leaf + each], bases[leaf + each], True) for each in range(2)]
        leaf_pack[leaf // 2] = jnp.concatenate(
            [
                jnp.concatenate(up, axis=1),
                jnp.concatenate([leaf_skel[leaf], leaf_skel[leaf + 1]], axis=1),
                blank,
            ],
            axis=0,
        )
        for each in range(2):
            up_node = up_node + product(up[each], leaf_maps[leaf + each])
    up_sub = product(up_node, node_maps[0])
    packed = jnp.concatenate(
        [
            jnp.concatenate([up_node, up_sub], axis=1),
            jnp.concatenate([node_skel[0], sub_skel[0]], axis=1),
            blank,
        ],
        axis=0,
    )

    def spread(each, carry):
        tree_pack[each] = packed
        return carry

    lax.fori_loop(0, tree_pack.shape[0], spread, 0)
    leave.wait()


def near_kernel(shift, *refs):
    given, (near_out, inverse_out) = refs[:3], refs[3:5]
    held = refs[5:8]
    near, inverse, flat, source, rows, across, down, slots, sems = refs[8:]
    copies = fetch(list(zip(given, held)), sems)
    crd, perm, tree_vec = held
    count_rows(rows)
    leaves, nvec, block = tree_vec.shape
    chunks = crd.shape[1] // WIDE
    scale, poly = make_tables(1.0 / math.sqrt(block))
    slope = scale[0, 1] - scale[0, 0]
    copies[0].wait()
    for axis in range(2):
        for each in range(chunks):
            row = axis * chunks + each
            flat[row : row + 1, :] = crd[axis : axis + 1, each * WIDE : (each + 1) * WIDE]
    rest = flat[...]
    for piece in range(3):
        rounded = rest.astype(BF16)
        source[piece * 2 * chunks : (piece + 1) * 2 * chunks, :] = rounded
        rest = rest - rounded.astype(F32)
    slots[...] = jnp.zeros_like(slots)
    copies[1].wait()
    side = 128
    tiles = block // side

    def place_leaf(leaf, carry):
        index = leaf_index(perm, leaf, block)
        hot = one_hot(rows, index & (WIDE - 1))
        found = dot(source[...], hot)
        found = (
            found[: 2 * chunks] + found[2 * chunks : 4 * chunks] + found[4 * chunks :]
        )
        mine = lax.broadcasted_iota(jnp.int32, (chunks, block), 0) == index >> SHIFT
        lane = lax.broadcasted_iota(jnp.int32, (chunks, block), 1) + leaf * block
        lane_low = (lane & (WIDE - 1)).astype(F32)
        lane_high = (lane >> SHIFT).astype(F32)
        marks = jnp.concatenate(
            [jnp.where(mine, lane_low, 0.0), jnp.where(mine, lane_high, 0.0)], axis=0
        ).astype(BF16)
        slots[...] += dot(marks, hot, True)
        row_x = jnp.sum(jnp.where(mine, found[:chunks], 0.0), axis=0, keepdims=True)
        row_y = jnp.sum(jnp.where(mine, found[chunks:], 0.0), axis=0, keepdims=True)
        moved = index + shift[0]
        kind = moved - 3 * ((moved * 43691) >> 17)
        row_w = kind.astype(F32) * slope
        for place, row in enumerate((row_x, row_y, row_w)):
            across[leaf, place] = jnp.broadcast_to(row, (8, block))
            turned = jnp.transpose(jnp.broadcast_to(row, (side, block)))
            down[leaf, place] = turned.reshape(block // 8, 8, side)
        return carry

    lax.fori_loop(0, leaves, place_leaf, 0, unroll=2)
    inverse[...] = (slots[:chunks] + slots[chunks:] * WIDE).astype(jnp.int32)
    leave = pltpu.make_async_copy(inverse, inverse_out, sems.at[3])
    leave.start()
    copies[2].wait()

    def one_leaf(leaf, carry):
        vec_hi, vec_lo = parts(tree_vec[leaf])
        vec_both = jnp.concatenate([vec_hi, vec_lo], axis=0)
        total = [0.0] * tiles
        for col in reversed(range(tiles)):
            cols = slice(col * side, (col + 1) * side)
            over_x, over_y, over_w = [across[leaf, each, :, cols] for each in range(3)]
            over_zero, over_one = over_w > 0.5 * slope, over_w > 1.5 * slope

            def across_table(power, first):
                zero, one, two = [float(each) for each in poly[power, first]]
                return jnp.where(over_zero, zero, jnp.where(over_one, one, two))[None]

            table = [[across_table(power, first) for first in range(3)] for power in range(5)]
            over_w = (over_w + float(scale[0, 0]))[None]
            over_x, over_y = over_x[None], over_y[None]
            high, low = [], []
            for row in range(col + 1):
                at = slice(row * side // 8, (row + 1) * side // 8)
                diff_x = down[leaf, 0, at] - over_x
                diff_y = down[leaf, 1, at] - over_y
                down_w = down[leaf, 2, at]
                var_zero, var_one = down_w > 0.5 * slope, down_w > 1.5 * slope
                square = (diff_x * diff_x + diff_y * diff_y) * (down_w + over_w)
                arg = square * lax.rsqrt(TINY - square)
                value = jnp.where(var_one, 0.0, table[4][2])
                value = value * arg + jnp.where(
                    var_zero, 0.0, jnp.where(var_one, table[3][1], table[3][2])
                )
                for power in (2, 1, 0):
                    a, b, c = table[power]
                    value = value * arg + jnp.where(var_zero, a, jnp.where(var_one, b, c))
                value = (value * jnp.exp2(arg)).reshape(side, side)
                value_hi, value_lo = parts(value)
                high.append(value_hi)
                low.append(value_lo)
            high = jnp.concatenate(high, axis=0)
            low = jnp.concatenate(low, axis=0)
            upto = (col + 1) * side
            both = dot(vec_both[:, :upto], high)
            direct = both[:nvec] + both[nvec:] + dot(vec_hi[:, :upto], low)
            total[col] = total[col] + direct
            if col > 0:
                both = dot(vec_both[:, cols], high[: col * side], True)
                back = both[:nvec] + both[nvec:] + dot(vec_hi[:, cols], low[: col * side], True)
                for row in range(col):
                    total[row] = total[row] + back[:, row * side : (row + 1) * side]
        for col in range(tiles):
            near[leaf, :, col * side : (col + 1) * side] = total[col]
        return carry

    lax.fori_loop(0, leaves, one_leaf, 0)
    leave.wait()
    leave = pltpu.make_async_copy(near, near_out, sems.at[3])
    leave.start()
    leave.wait()


def far_kernel(groups, subtrees, *refs):
    place, leaf_src, leaf_count, node_src, node_count = refs[:5]
    given, out_at = refs[5:16], refs[16]
    held = refs[17:28]
    source, coef, twice, cols, out, rows, srcs, dsts, sems = refs[28:]
    copies = fetch(list(zip(given, held)), sems)
    leaf_all, tree_all, leaf_skel, node_skel, sub_skel, tables = held[:6]
    leaf_maps, node_maps, bases, near, inverse = held[6:]
    count_rows(rows)
    leaves, nvec, block = near.shape
    rank = bases.shape[1]
    nodes = tree_all.shape[0]
    pairs = leaf_all.shape[0]
    node_at = 2 * pairs
    beside = 3 * groups
    sub_at = node_at + beside
    blank = sub_at + subtrees
    sub_pos = place[0]
    left = lax.broadcasted_iota(jnp.int32, (PACK_ROWS, 2 * rank), 1) < rank

    def list_leaf(leaf, at):
        count = leaf_count[leaf]

        def one(step, carry):
            srcs[2 * (at + step)] = leaf_src[leaf, 2 * step]
            second = jnp.where(2 * step + 1 < count, leaf_src[leaf, 2 * step + 1], blank)
            srcs[2 * (at + step) + 1] = second
            dsts[at + step] = leaf
            return carry

        steps = (count + 1) // 2
        lax.fori_loop(0, steps, one, 0)
        return at + steps

    size = lax.fori_loop(0, leaves, list_leaf, 0)
    count = node_count[0]

    def list_node(step, carry):
        srcs[2 * (size + step)] = node_at + node_src[0, 2 * step]
        second = jnp.where(2 * step + 1 < count, node_at + node_src[0, 2 * step + 1], blank)
        srcs[2 * (size + step) + 1] = second
        dsts[size + step] = leaves
        return carry

    steps = (count + 1) // 2
    lax.fori_loop(0, steps, list_node, 0)

    def list_sub(sub, at):
        srcs[at] = sub_at + sub
        dsts[at // 2] = leaves + 1
        return at + jnp.where(jnp.abs(sub - sub_pos) >= 2, 1, 0)

    ends = lax.fori_loop(0, subtrees, list_sub, 2 * (size + steps))
    srcs[ends] = blank
    dsts[ends // 2] = leaves + 1
    ends = (ends + 1) // 2
    for each in range(AT_ONCE):
        srcs[2 * (ends + each)] = blank
        srcs[2 * (ends + each) + 1] = blank
        dsts[ends + each] = leaves + 1

    copies[0].wait()

    def both_leaves(pair, carry):
        packs = leaf_all[pair]
        turned = pltpu.roll(packs, rank, 1)
        twice[2 * pair] = jnp.where(left, packs, turned)
        twice[2 * pair + 1] = jnp.where(left, turned, packs)
        return carry

    lax.fori_loop(0, pairs, both_leaves, 0, unroll=4)
    copies[1].wait()

    def both_node(each, carry):
        packs = tree_all[jnp.clip((sub_pos - 1) * groups + each, 0, nodes - 1)]
        twice[node_at + each] = jnp.where(left, packs, pltpu.roll(packs, rank, 1))
        return carry

    lax.fori_loop(0, beside, both_node, 0, unroll=4)

    def both_sub(sub, carry):
        total = tree_all[sub * groups, :nvec]
        for each in range(1, groups):
            total = total + tree_all[sub * groups + each, :nvec]
        packs = jnp.concatenate([total, tree_all[sub * groups, nvec:]], axis=0)
        twice[sub_at + sub] = jnp.where(left, pltpu.roll(packs, rank, 1), packs)
        return carry

    lax.fori_loop(0, subtrees, both_sub, 0, unroll=2)
    twice[blank] = jnp.zeros_like(twice[blank])
    coef[...] = jnp.zeros_like(coef)
    for copy in copies[2:6]:
        copy.wait()

    def upright(skel, at):
        for axis in range(2):
            row = jnp.broadcast_to(skel[axis : axis + 1], (2 * rank, rank))
            cols[at, axis] = jnp.transpose(row)

    def upright_leaf(leaf, carry):
        upright(leaf_skel[leaf], leaf)
        return carry

    lax.fori_loop(0, leaves, upright_leaf, 0, unroll=4)
    upright(node_skel[0], leaves)
    upright(sub_skel[0], leaves + 1)

    def couple(step, carry):
        terms = []
        for each in range(AT_ONCE):
            item = step * AT_ONCE + each
            packs = jnp.where(left, twice[srcs[2 * item]], twice[srcs[2 * item + 1]])
            target = dsts[item]
            diff_x = cols[target, 0] - packs[nvec : nvec + 1]
            diff_y = cols[target, 1] - packs[nvec + 1 : nvec + 2]
            square = (diff_x * diff_x + diff_y * diff_y) * tables[0]
            arg = square * lax.rsqrt(TINY - square)
            value = tables[5]
            for power in (4, 3, 2, 1):
                value = value * arg + tables[power]
            value = value * jnp.exp2(arg)
            terms.append((target, product(packs[:nvec], value, True)))
        for target, total in terms:
            coef[target] += total
        return carry

    lax.fori_loop(0, (ends + AT_ONCE - 1) // AT_ONCE, couple, 0)
    for copy in copies[6:]:
        copy.wait()
    down_node = coef[leaves] + product(coef[leaves + 1], node_maps[0], True)
    for leaf in range(leaves):
        down_leaf = coef[leaf] + product(down_node, leaf_maps[leaf], True)
        whole = near[leaf] + product(down_leaf, bases[leaf])
        for each in range(block // WIDE):
            fill(
                source,
                whole[:, each * WIDE : (each + 1) * WIDE],
                (leaf * (block // WIDE) + each) * nvec,
                nvec,
            )

    def scatter(each, carry):
        at = pl.multiple_of(each * 2 * WIDE, 2 * WIDE)
        index = jnp.concatenate(
            [inverse[pl.ds(2 * each, 1), :], inverse[pl.ds(2 * each + 1, 1), :]], axis=1
        )
        out[:, pl.ds(at, 2 * WIDE)] = pick(rows, source, index, nvec)
        return carry

    steps = inverse.shape[0] // 2
    segments = 4
    leaving = []
    for each in range(segments):
        start, stop = each * steps // segments, (each + 1) * steps // segments
        lax.fori_loop(start, stop, scatter, 0, unroll=2)
        span = slice(start * 2 * WIDE, stop * 2 * WIDE)
        leaving.append(pltpu.make_async_copy(out.at[:, span], out_at.at[:, span], sems.at[each]))
        leaving[-1].start()
    for copy in leaving:
        copy.wait()


def skeleton_tables(rank):
    scale, poly = make_tables(1.0 / math.sqrt(rank))
    var = np.arange(rank) % 3
    rows, cols = var[:, None], np.tile(var, 2)[None, :]
    return np.stack([scale[rows, cols]] + [poly[power][rows, cols] for power in range(5)]).astype(
        np.float32
    )


def shards(
    vectors,
    coords,
    perm,
    bases,
    leaf_maps,
    node_maps,
    leaf_skel,
    node_skel,
    sub_skel,
    leaf_src,
    leaf_count,
    node_src,
    node_count,
):
    nvec, rows_dev = vectors.shape
    leaves, rank, block = bases.shape
    groups = lax.axis_size("grp")
    subtrees = lax.axis_size("leaf")
    nodes = groups * subtrees
    sub_pos = lax.axis_index("leaf")
    device_pos = sub_pos * groups + lax.axis_index("grp")
    chunks = rows_dev // WIDE
    vmem = pl.BlockSpec(memory_space=pltpu.VMEM)
    smem = pl.BlockSpec(memory_space=pltpu.SMEM)
    hbm = pl.BlockSpec(memory_space=pltpu.HBM)
    params = pltpu.CompilerParams(vmem_limit_bytes=40 * 1024 * 1024)
    order = perm.reshape(rows_dev // 128, 128)

    def like(*arrays):
        return [pltpu.VMEM(each.shape, each.dtype) for each in arrays]

    given = (vectors, order, bases, leaf_maps, node_maps, leaf_skel, node_skel, sub_skel)
    tree_vec, leaf_pack, tree_pack = pl.pallas_call(
        up_kernel,
        out_shape=(
            jax.ShapeDtypeStruct((leaves, nvec, block), F32),
            jax.ShapeDtypeStruct((leaves // 2, PACK_ROWS, 2 * rank), F32),
            jax.ShapeDtypeStruct((nodes, PACK_ROWS, 2 * rank), F32),
        ),
        in_specs=[hbm] * 8,
        out_specs=(hbm, vmem, vmem),
        scratch_shapes=like(*given)
        + [
            pltpu.VMEM((leaves, nvec, block), F32),
            pltpu.VMEM((chunks * nvec, 2 * WIDE), BF16),
            pltpu.VMEM((WIDE, block), jnp.int16),
            pltpu.SemaphoreType.DMA((9,)),
        ],
        compiler_params=params,
        name="up",
    )(*given)
    tree_all = lax.all_to_all(tree_pack, ("leaf", "grp"), 0, 0, tiled=True)
    leaf_all = lax.all_gather(leaf_pack, "grp", axis=0, tiled=True)
    shift = (device_pos * (rows_dev % 3) % 3).astype(jnp.int32).reshape(1)
    near, inverse = pl.pallas_call(
        near_kernel,
        out_shape=(
            jax.ShapeDtypeStruct((leaves, nvec, block), F32),
            jax.ShapeDtypeStruct((chunks, WIDE), jnp.int32),
        ),
        in_specs=[smem, hbm, hbm, hbm],
        out_specs=(hbm,) * 2,
        scratch_shapes=like(coords, order, tree_vec)
        + [
            pltpu.VMEM((leaves, nvec, block), F32),
            pltpu.VMEM((chunks, WIDE), jnp.int32),
            pltpu.VMEM((2 * chunks, WIDE), F32),
            pltpu.VMEM((6 * chunks, WIDE), BF16),
            pltpu.VMEM((WIDE, block), jnp.int16),
            pltpu.VMEM((leaves, 3, 8, block), F32),
            pltpu.VMEM((leaves, 3, block // 8, 8, 128), F32),
            pltpu.VMEM((2 * chunks, WIDE), F32),
            pltpu.SemaphoreType.DMA((4,)),
        ],
        compiler_params=params,
        cost_estimate=pl.CostEstimate(
            flops=128 * leaves * block * block,
            bytes_accessed=8 * leaves * nvec * block,
            transcendentals=leaves * block * block,
        ),
        name="near",
    )(shift, coords, order, tree_vec)
    tables = jnp.asarray(skeleton_tables(rank))
    given = (leaf_all, tree_all, leaf_skel, node_skel, sub_skel, tables)
    given = given + (leaf_maps, node_maps, bases, near, inverse)
    items = (leaf_src.size + node_src.size + subtrees + 2) // 2 + AT_ONCE
    sources = groups * leaves + 3 * groups + subtrees + 1
    return pl.pallas_call(
        functools.partial(far_kernel, groups, subtrees),
        out_shape=jax.ShapeDtypeStruct((nvec, rows_dev), F32),
        in_specs=[smem] * 5 + [hbm] * 11,
        out_specs=hbm,
        scratch_shapes=like(*given)
        + [
            pltpu.VMEM((chunks * nvec, 2 * WIDE), BF16),
            pltpu.VMEM((leaves + 2, nvec, rank), F32),
            pltpu.VMEM((sources, PACK_ROWS, 2 * rank), F32),
            pltpu.VMEM((leaves + 2, 2, rank, 2 * rank), F32),
            pltpu.VMEM((nvec, rows_dev), F32),
            pltpu.VMEM((WIDE, 2 * WIDE), jnp.int16),
            pltpu.SMEM((2 * items,), jnp.int32),
            pltpu.SMEM((items,), jnp.int32),
            pltpu.SemaphoreType.DMA((11,)),
        ],
        compiler_params=params,
        name="far",
    )(
        sub_pos.astype(jnp.int32).reshape(1),
        leaf_src,
        leaf_count,
        node_src,
        node_count,
        *given,
    )


def solution(mesh):
    placed = (
        P(None, ("leaf", "grp")),
        P(None, ("leaf", "grp")),
        P(("leaf", "grp")),
        P(("leaf", "grp"), None, None),
        P(("leaf", "grp"), None, None),
        P(("leaf", "grp"), None, None),
        P(("leaf", "grp"), None, None),
        P(("leaf", "grp"), None, None),
        P("leaf", None, None),
        P(("leaf", "grp"), None),
        P(("leaf", "grp")),
        P(("leaf", "grp"), None),
        P(("leaf", "grp")),
    )
    return jax.shard_map(
        shards, mesh=mesh, in_specs=placed, out_specs=P(None, ("leaf", "grp")), check_vma=False
    )
```

```python
import functools
import math

import jax
import jax.numpy as jnp
import numpy as np
from jax import lax
from jax.experimental import pallas as pl
from jax.experimental.pallas import tpu as pltpu
from jax.sharding import PartitionSpec as P

F32 = jnp.float32
BF16 = jnp.bfloat16
WIDE = 256
SHIFT = 8
LOG2E = math.log2(math.e)
TINY = 1e-37
PACK_ROWS = 24
LEAF_ROWS = 32
AT_ONCE = 4


def make_tables(norm):
    smooth = [0, 2, 4]
    sigmas = [1.0, 0.8, 1.2]
    rho = [[1.0, 0.5, 0.3], [0.5, 1.0, 0.4], [0.3, 0.4, 1.0]]
    scale = np.zeros((3, 3))
    poly = np.zeros((5, 3, 3))
    for first in range(3):
        for second in range(3):
            order = (smooth[first] + smooth[second]) // 2
            scale[first, second] = -(2.0 * order + 1.0) * (LOG2E / 0.3) ** 2
            amp = sigmas[first] * sigmas[second] * rho[first][second] * norm
            for power in range(order + 1):
                kterm = order - power
                coeff = math.factorial(order) / math.factorial(2 * order)
                coeff = (
                    coeff
                    * math.factorial(order + kterm)
                    / (math.factorial(kterm) * math.factorial(order - kterm))
                )
                poly[power, first, second] = amp * coeff * 2.0**power * (-1.0 / LOG2E) ** power
    return scale, poly


def dot(one, two, turned=False):
    dims = (((1,), (1 if turned else 0,)), ((), ()))
    return lax.dot_general(one, two, dims, preferred_element_type=F32)


def parts(value):
    high = value.astype(BF16)
    return high, (value - high.astype(F32)).astype(BF16)


def product(one, two, turned=False):
    rows = one.shape[0]
    one_hi, one_lo = parts(one)
    two_hi, two_lo = parts(two)
    both = dot(jnp.concatenate([one_hi, one_lo], axis=0), two_hi, turned)
    return both[:rows] + both[rows:] + dot(one_hi, two_lo, turned)


def count_rows(rows):
    rows[...] = lax.broadcasted_iota(jnp.int32, rows.shape, 0).astype(jnp.int16)


def one_hot(rows, low):
    count = low.shape[1]
    low = jnp.broadcast_to(low, (16, count)).astype(jnp.int16)[None]
    same = rows[:, :count].reshape(WIDE // 16, 16, count) == low
    return jnp.where(same, jnp.bfloat16(1), jnp.bfloat16(0)).reshape(WIDE, count)


def fill(source, value, at, nvec):
    high, low = parts(value)
    source[pl.ds(at, nvec), :WIDE] = high
    source[pl.ds(at, nvec), WIDE:] = low


def pick(rows, source, index, nvec):
    count = index.shape[1]
    hot = one_hot(rows, index & (WIDE - 1))
    hot = jnp.concatenate([hot, hot], axis=0)
    chunk = jnp.broadcast_to(index >> SHIFT, (8, count))[None]
    out = jnp.zeros((nvec // 8, 8, count), F32)
    chunks = source.shape[0] // nvec
    found = dot(source[...], hot).reshape(chunks, nvec // 8, 8, count)
    for each in range(chunks):
        out = jnp.where(chunk == each, found[each], out)
    return out.reshape(nvec, count)


def leaf_index(perm, leaf, block):
    rows = block // 128
    return jnp.concatenate([perm[pl.ds(leaf * rows + each, 1), :] for each in range(rows)], axis=1)


def fetch(pairs, sems):
    copies = [pltpu.make_async_copy(src, dst, sems.at[each]) for each, (src, dst) in enumerate(pairs)]
    for copy in copies:
        copy.start()
    return copies


def up_kernel(*refs):
    given, (tree_out, leaf_pack, tree_pack) = refs[:8], refs[8:11]
    held = refs[11:19]
    tree_vec, source, rows, sems = refs[19:]
    count_rows(rows)
    copies = fetch(list(zip(given, held)), sems)
    vec, perm, bases, leaf_maps, node_maps, leaf_skel, node_skel, sub_skel = held
    leaves, nvec, block = tree_vec.shape
    rank = bases.shape[1]
    copies[0].wait()
    for each in range(vec.shape[1] // WIDE):
        fill(source, vec[:, each * WIDE : (each + 1) * WIDE], each * nvec, nvec)
    copies[1].wait()

    def gather(leaf, carry):
        tree_vec[leaf] = pick(rows, source, leaf_index(perm, leaf, block), nvec)
        return carry

    lax.fori_loop(0, leaves, gather, 0, unroll=2)
    leave = pltpu.make_async_copy(tree_vec, tree_out, sems.at[len(copies)])
    leave.start()
    for copy in copies[2:]:
        copy.wait()
    up_node = jnp.zeros((nvec, rank), F32)
    blank = jnp.zeros((leaf_pack.shape[1] - nvec - 2, 2 * rank), F32)
    for leaf in range(leaves):
        up = product(tree_vec[leaf], bases[leaf], True)
        leaf_pack[leaf] = jnp.concatenate(
            [
                jnp.concatenate([up, up], axis=1),
                jnp.concatenate([leaf_skel[leaf], leaf_skel[leaf]], axis=1),
                blank,
            ],
            axis=0,
        )
        up_node = up_node + product(up, leaf_maps[leaf])
    up_sub = product(up_node, node_maps[0])
    packed = jnp.concatenate(
        [
            jnp.concatenate([up_node, up_sub], axis=1),
            jnp.concatenate([node_skel[0], sub_skel[0]], axis=1),
            blank[: PACK_ROWS - nvec - 2],
        ],
        axis=0,
    )

    def spread(each, carry):
        tree_pack[each] = packed
        return carry

    lax.fori_loop(0, tree_pack.shape[0], spread, 0)
    leave.wait()


def near_kernel(shift, *refs):
    given, (near_out, inverse_out) = refs[:3], refs[3:5]
    held = refs[5:8]
    near, inverse, flat, source, rows, across, down, slots, sems = refs[8:]
    copies = fetch(list(zip(given, held)), sems)
    crd, perm, tree_vec = held
    count_rows(rows)
    leaves, nvec, block = tree_vec.shape
    chunks = crd.shape[1] // WIDE
    scale, poly = make_tables(1.0 / math.sqrt(block))
    slope = scale[0, 1] - scale[0, 0]
    copies[0].wait()
    for axis in range(2):
        for each in range(chunks):
            row = axis * chunks + each
            flat[row : row + 1, :] = crd[axis : axis + 1, each * WIDE : (each + 1) * WIDE]
    rest = flat[...]
    for piece in range(3):
        rounded = rest.astype(BF16)
        source[piece * 2 * chunks : (piece + 1) * 2 * chunks, :] = rounded
        rest = rest - rounded.astype(F32)
    slots[...] = jnp.zeros_like(slots)
    copies[1].wait()
    side = 128
    tiles = block // side

    def place_leaf(leaf, carry):
        index = leaf_index(perm, leaf, block)
        hot = one_hot(rows, index & (WIDE - 1))
        found = dot(source[...], hot)
        found = (
            found[: 2 * chunks] + found[2 * chunks : 4 * chunks] + found[4 * chunks :]
        )
        mine = lax.broadcasted_iota(jnp.int32, (chunks, block), 0) == index >> SHIFT
        lane = lax.broadcasted_iota(jnp.int32, (chunks, block), 1) + leaf * block
        lane_low = (lane & (WIDE - 1)).astype(F32)
        lane_high = (lane >> SHIFT).astype(F32)
        marks = jnp.concatenate(
            [jnp.where(mine, lane_low, 0.0), jnp.where(mine, lane_high, 0.0)], axis=0
        ).astype(BF16)
        slots[...] += dot(marks, hot, True)
        row_x = jnp.sum(jnp.where(mine, found[:chunks], 0.0), axis=0, keepdims=True)
        row_y = jnp.sum(jnp.where(mine, found[chunks:], 0.0), axis=0, keepdims=True)
        moved = index + shift[0]
        kind = moved - 3 * ((moved * 43691) >> 17)
        row_w = kind.astype(F32) * slope
        for place, row in enumerate((row_x, row_y, row_w)):
            across[leaf, place] = jnp.broadcast_to(row, (8, block))
            turned = jnp.transpose(jnp.broadcast_to(row, (side, block)))
            down[leaf, place] = turned.reshape(block // 8, 8, side)
        return carry

    lax.fori_loop(0, leaves, place_leaf, 0, unroll=2)
    inverse[...] = (slots[:chunks] + slots[chunks:] * WIDE).astype(jnp.int32)
    leave = pltpu.make_async_copy(inverse, inverse_out, sems.at[3])
    leave.start()
    copies[2].wait()

    def one_leaf(leaf, carry):
        vec_hi, vec_lo = parts(tree_vec[leaf])
        vec_both = jnp.concatenate([vec_hi, vec_lo], axis=0)
        total = [0.0] * tiles
        for col in reversed(range(tiles)):
            cols = slice(col * side, (col + 1) * side)
            over_x, over_y, over_w = [across[leaf, each, :, cols] for each in range(3)]
            over_zero, over_one = over_w > 0.5 * slope, over_w > 1.5 * slope

            def across_table(power, first):
                zero, one, two = [float(each) for each in poly[power, first]]
                return jnp.where(over_zero, zero, jnp.where(over_one, one, two))[None]

            table = [[across_table(power, first) for first in range(3)] for power in range(5)]
            over_w = (over_w + float(scale[0, 0]))[None]
            over_x, over_y = over_x[None], over_y[None]
            high, low = [], []
            for row in range(col + 1):
                at = slice(row * side // 8, (row + 1) * side // 8)
                diff_x = down[leaf, 0, at] - over_x
                diff_y = down[leaf, 1, at] - over_y
                down_w = down[leaf, 2, at]
                var_zero, var_one = down_w > 0.5 * slope, down_w > 1.5 * slope
                square = (diff_x * diff_x + diff_y * diff_y) * (down_w + over_w)
                arg = square * lax.rsqrt(TINY - square)
                value = jnp.where(var_one, 0.0, table[4][2])
                value = value * arg + jnp.where(
                    var_zero, 0.0, jnp.where(var_one, table[3][1], table[3][2])
                )
                for power in (2, 1, 0):
                    a, b, c = table[power]
                    value = value * arg + jnp.where(var_zero, a, jnp.where(var_one, b, c))
                value = (value * jnp.exp2(arg)).reshape(side, side)
                value_hi, value_lo = parts(value)
                high.append(value_hi)
                low.append(value_lo)
            high = jnp.concatenate(high, axis=0)
            low = jnp.concatenate(low, axis=0)
            upto = (col + 1) * side
            both = dot(vec_both[:, :upto], high)
            direct = both[:nvec] + both[nvec:] + dot(vec_hi[:, :upto], low)
            total[col] = total[col] + direct
            if col > 0:
                both = dot(vec_both[:, cols], high[: col * side], True)
                back = both[:nvec] + both[nvec:] + dot(vec_hi[:, cols], low[: col * side], True)
                for row in range(col):
                    total[row] = total[row] + back[:, row * side : (row + 1) * side]
        for col in range(tiles):
            near[leaf, :, col * side : (col + 1) * side] = total[col]
        return carry

    lax.fori_loop(0, leaves, one_leaf, 0)
    leave.wait()
    leave = pltpu.make_async_copy(near, near_out, sems.at[3])
    leave.start()
    leave.wait()


def far_kernel(groups, subtrees, *refs):
    place, leaf_src, leaf_count, node_src, node_count = refs[:5]
    given, out_at = refs[5:16], refs[16]
    held = refs[17:27]
    source, coef, twice, cols, out, rows, srcs, dsts, sems = refs[27:]
    leaf_now = given[0].at[:, :PACK_ROWS, :]
    held = (twice.at[: given[0].shape[0]],) + held
    copies = fetch(list(zip((leaf_now,) + given[1:], held)), sems)
    leaf_all, tree_all, leaf_skel, node_skel, sub_skel, tables = held[:6]
    leaf_maps, node_maps, bases, near, inverse = held[6:]
    count_rows(rows)
    leaves, nvec, block = near.shape
    rank = bases.shape[1]
    nodes = tree_all.shape[0]
    node_at = leaf_all.shape[0]
    beside = 3 * groups
    sub_at = node_at + beside
    blank = sub_at + subtrees
    sub_pos = place[0]
    left = lax.broadcasted_iota(jnp.int32, (PACK_ROWS, 2 * rank), 1) < rank

    def list_leaf(leaf, at):
        count = leaf_count[leaf]

        def one(step, carry):
            srcs[2 * (at + step)] = leaf_src[leaf, 2 * step]
            second = jnp.where(2 * step + 1 < count, leaf_src[leaf, 2 * step + 1], blank)
            srcs[2 * (at + step) + 1] = second
            dsts[at + step] = leaf
            return carry

        steps = (count + 1) // 2
        lax.fori_loop(0, steps, one, 0)
        return at + steps

    size = lax.fori_loop(0, leaves, list_leaf, 0)
    count = node_count[0]

    def list_node(step, carry):
        srcs[2 * (size + step)] = node_at + node_src[0, 2 * step]
        second = jnp.where(2 * step + 1 < count, node_at + node_src[0, 2 * step + 1], blank)
        srcs[2 * (size + step) + 1] = second
        dsts[size + step] = leaves
        return carry

    steps = (count + 1) // 2
    lax.fori_loop(0, steps, list_node, 0)

    def list_sub(sub, at):
        srcs[at] = sub_at + sub
        dsts[at // 2] = leaves + 1
        return at + jnp.where(jnp.abs(sub - sub_pos) >= 2, 1, 0)

    ends = lax.fori_loop(0, subtrees, list_sub, 2 * (size + steps))
    srcs[ends] = blank
    dsts[ends // 2] = leaves + 1
    ends = (ends + 1) // 2
    for each in range(AT_ONCE):
        srcs[2 * (ends + each)] = blank
        srcs[2 * (ends + each) + 1] = blank
        dsts[ends + each] = leaves + 1

    copies[1].wait()

    def both_node(each, carry):
        packs = tree_all[jnp.clip((sub_pos - 1) * groups + each, 0, nodes - 1)]
        twice[node_at + each] = jnp.where(left, packs, pltpu.roll(packs, rank, 1))
        return carry

    lax.fori_loop(0, beside, both_node, 0, unroll=4)

    def both_sub(sub, carry):
        total = tree_all[sub * groups, :nvec]
        for each in range(1, groups):
            total = total + tree_all[sub * groups + each, :nvec]
        packs = jnp.concatenate([total, tree_all[sub * groups, nvec:]], axis=0)
        twice[sub_at + sub] = jnp.where(left, pltpu.roll(packs, rank, 1), packs)
        return carry

    lax.fori_loop(0, subtrees, both_sub, 0, unroll=2)
    twice[blank] = jnp.zeros_like(twice[blank])
    coef[...] = jnp.zeros_like(coef)
    for copy in (copies[0], *copies[2:6]):
        copy.wait()

    def upright(skel, at):
        for axis in range(2):
            row = jnp.broadcast_to(skel[axis : axis + 1], (2 * rank, rank))
            cols[at, axis] = jnp.transpose(row)

    def upright_leaf(leaf, carry):
        upright(leaf_skel[leaf], leaf)
        return carry

    lax.fori_loop(0, leaves, upright_leaf, 0, unroll=4)
    upright(node_skel[0], leaves)
    upright(sub_skel[0], leaves + 1)

    def couple(step, carry):
        terms = []
        for each in range(AT_ONCE):
            item = step * AT_ONCE + each
            packs = jnp.where(left, twice[srcs[2 * item]], twice[srcs[2 * item + 1]])
            target = dsts[item]
            diff_x = cols[target, 0] - packs[nvec : nvec + 1]
            diff_y = cols[target, 1] - packs[nvec + 1 : nvec + 2]
            square = (diff_x * diff_x + diff_y * diff_y) * tables[0]
            arg = square * lax.rsqrt(TINY - square)
            value = tables[5]
            for power in (4, 3, 2, 1):
                value = value * arg + tables[power]
            value = value * jnp.exp2(arg)
            terms.append((target, product(packs[:nvec], value, True)))
        for target, total in terms:
            coef[target] += total
        return carry

    lax.fori_loop(0, (ends + AT_ONCE - 1) // AT_ONCE, couple, 0)
    for copy in copies[6:]:
        copy.wait()
    down_node = coef[leaves] + product(coef[leaves + 1], node_maps[0], True)
    for leaf in range(leaves):
        down_leaf = coef[leaf] + product(down_node, leaf_maps[leaf], True)
        whole = near[leaf] + product(down_leaf, bases[leaf])
        for each in range(block // WIDE):
            fill(
                source,
                whole[:, each * WIDE : (each + 1) * WIDE],
                (leaf * (block // WIDE) + each) * nvec,
                nvec,
            )

    def scatter(each, carry):
        at = pl.multiple_of(each * 2 * WIDE, 2 * WIDE)
        index = jnp.concatenate(
            [inverse[pl.ds(2 * each, 1), :], inverse[pl.ds(2 * each + 1, 1), :]], axis=1
        )
        out[:, pl.ds(at, 2 * WIDE)] = pick(rows, source, index, nvec)
        return carry

    steps = inverse.shape[0] // 2
    segments = 4
    leaving = []
    for each in range(segments):
        start, stop = each * steps // segments, (each + 1) * steps // segments
        lax.fori_loop(start, stop, scatter, 0, unroll=2)
        span = slice(start * 2 * WIDE, stop * 2 * WIDE)
        leaving.append(pltpu.make_async_copy(out.at[:, span], out_at.at[:, span], sems.at[each]))
        leaving[-1].start()
    for copy in leaving:
        copy.wait()


def skeleton_tables(rank):
    scale, poly = make_tables(1.0 / math.sqrt(rank))
    var = np.arange(rank) % 3
    rows, cols = var[:, None], np.tile(var, 2)[None, :]
    return np.stack([scale[rows, cols]] + [poly[power][rows, cols] for power in range(5)]).astype(
        np.float32
    )


def shards(
    vectors,
    coords,
    perm,
    bases,
    leaf_maps,
    node_maps,
    leaf_skel,
    node_skel,
    sub_skel,
    leaf_src,
    leaf_count,
    node_src,
    node_count,
):
    nvec, rows_dev = vectors.shape
    leaves, rank, block = bases.shape
    groups = lax.axis_size("grp")
    subtrees = lax.axis_size("leaf")
    nodes = groups * subtrees
    sub_pos = lax.axis_index("leaf")
    device_pos = sub_pos * groups + lax.axis_index("grp")
    chunks = rows_dev // WIDE
    vmem = pl.BlockSpec(memory_space=pltpu.VMEM)
    smem = pl.BlockSpec(memory_space=pltpu.SMEM)
    hbm = pl.BlockSpec(memory_space=pltpu.HBM)
    params = pltpu.CompilerParams(vmem_limit_bytes=60 * 1024 * 1024)
    order = perm.reshape(rows_dev // 128, 128)

    def like(*arrays):
        return [pltpu.VMEM(each.shape, each.dtype) for each in arrays]

    given = (vectors, order, bases, leaf_maps, node_maps, leaf_skel, node_skel, sub_skel)
    tree_vec, leaf_pack, tree_pack = pl.pallas_call(
        up_kernel,
        out_shape=(
            jax.ShapeDtypeStruct((leaves, nvec, block), F32),
            jax.ShapeDtypeStruct((leaves, LEAF_ROWS, 2 * rank), F32),
            jax.ShapeDtypeStruct((nodes, PACK_ROWS, 2 * rank), F32),
        ),
        in_specs=[hbm] * 8,
        out_specs=(hbm, vmem, vmem),
        scratch_shapes=like(*given)
        + [
            pltpu.VMEM((leaves, nvec, block), F32),
            pltpu.VMEM((chunks * nvec, 2 * WIDE), BF16),
            pltpu.VMEM((WIDE, block), jnp.int16),
            pltpu.SemaphoreType.DMA((9,)),
        ],
        compiler_params=params,
        name="up",
    )(*given)
    tree_all = lax.all_to_all(tree_pack, ("leaf", "grp"), 0, 0, tiled=True)
    leaf_all = lax.all_gather(leaf_pack, "grp", axis=0, tiled=True)
    shift = (device_pos * (rows_dev % 3) % 3).astype(jnp.int32).reshape(1)
    near, inverse = pl.pallas_call(
        near_kernel,
        out_shape=(
            jax.ShapeDtypeStruct((leaves, nvec, block), F32),
            jax.ShapeDtypeStruct((chunks, WIDE), jnp.int32),
        ),
        in_specs=[smem, hbm, hbm, hbm],
        out_specs=(hbm,) * 2,
        scratch_shapes=like(coords, order, tree_vec)
        + [
            pltpu.VMEM((leaves, nvec, block), F32),
            pltpu.VMEM((chunks, WIDE), jnp.int32),
            pltpu.VMEM((2 * chunks, WIDE), F32),
            pltpu.VMEM((6 * chunks, WIDE), BF16),
            pltpu.VMEM((WIDE, block), jnp.int16),
            pltpu.VMEM((leaves, 3, 8, block), F32),
            pltpu.VMEM((leaves, 3, block // 8, 8, 128), F32),
            pltpu.VMEM((2 * chunks, WIDE), F32),
            pltpu.SemaphoreType.DMA((4,)),
        ],
        compiler_params=params,
        cost_estimate=pl.CostEstimate(
            flops=128 * leaves * block * block,
            bytes_accessed=8 * leaves * nvec * block,
            transcendentals=leaves * block * block,
        ),
        name="near",
    )(shift, coords, order, tree_vec)
    tables = jnp.asarray(skeleton_tables(rank))
    given = (leaf_all, tree_all, leaf_skel, node_skel, sub_skel, tables)
    given = given + (leaf_maps, node_maps, bases, near, inverse)
    items = (leaf_src.size + node_src.size + subtrees + 2) // 2 + AT_ONCE
    sources = groups * leaves + 3 * groups + subtrees + 1
    return pl.pallas_call(
        functools.partial(far_kernel, groups, subtrees),
        out_shape=jax.ShapeDtypeStruct((nvec, rows_dev), F32),
        in_specs=[smem] * 5 + [hbm] * 11,
        out_specs=hbm,
        scratch_shapes=like(*given[1:])
        + [
            pltpu.VMEM((chunks * nvec, 2 * WIDE), BF16),
            pltpu.VMEM((leaves + 2, nvec, rank), F32),
            pltpu.VMEM((sources, PACK_ROWS, 2 * rank), F32),
            pltpu.VMEM((leaves + 2, 2, rank, 2 * rank), F32),
            pltpu.VMEM((nvec, rows_dev), F32),
            pltpu.VMEM((WIDE, 2 * WIDE), jnp.int16),
            pltpu.SMEM((2 * items,), jnp.int32),
            pltpu.SMEM((items,), jnp.int32),
            pltpu.SemaphoreType.DMA((11,)),
        ],
        compiler_params=params,
        name="far",
    )(
        sub_pos.astype(jnp.int32).reshape(1),
        leaf_src,
        leaf_count,
        node_src,
        node_count,
        *given,
    )


def solution(mesh):
    placed = (
        P(None, ("leaf", "grp")),
        P(None, ("leaf", "grp")),
        P(("leaf", "grp")),
        P(("leaf", "grp"), None, None),
        P(("leaf", "grp"), None, None),
        P(("leaf", "grp"), None, None),
        P(("leaf", "grp"), None, None),
        P(("leaf", "grp"), None, None),
        P("leaf", None, None),
        P(("leaf", "grp"), None),
        P(("leaf", "grp")),
        P(("leaf", "grp"), None),
        P(("leaf", "grp")),
    )
    return jax.shard_map(
        shards, mesh=mesh, in_specs=placed, out_specs=P(None, ("leaf", "grp")), check_vma=False
    )
```

```python
import functools
import math

import jax
import jax.numpy as jnp
import numpy as np
from jax import lax
from jax.experimental import pallas as pl
from jax.experimental.pallas import tpu as pltpu
from jax.sharding import PartitionSpec as P

F32 = jnp.float32
BF16 = jnp.bfloat16
WIDE = 256
SHIFT = 8
LOG2E = math.log2(math.e)
TINY = 1e-37
PACK_ROWS = 24
PART = 32
AT_ONCE = 4


def make_tables(norm):
    smooth = [0, 2, 4]
    sigmas = [1.0, 0.8, 1.2]
    rho = [[1.0, 0.5, 0.3], [0.5, 1.0, 0.4], [0.3, 0.4, 1.0]]
    scale = np.zeros((3, 3))
    poly = np.zeros((5, 3, 3))
    for first in range(3):
        for second in range(3):
            order = (smooth[first] + smooth[second]) // 2
            scale[first, second] = -(2.0 * order + 1.0) * (LOG2E / 0.3) ** 2
            amp = sigmas[first] * sigmas[second] * rho[first][second] * norm
            for power in range(order + 1):
                kterm = order - power
                coeff = math.factorial(order) / math.factorial(2 * order)
                coeff = (
                    coeff
                    * math.factorial(order + kterm)
                    / (math.factorial(kterm) * math.factorial(order - kterm))
                )
                poly[power, first, second] = amp * coeff * 2.0**power * (-1.0 / LOG2E) ** power
    return scale, poly


def dot(one, two, turned=False):
    dims = (((1,), (1 if turned else 0,)), ((), ()))
    return lax.dot_general(one, two, dims, preferred_element_type=F32)


def parts(value):
    high = value.astype(BF16)
    return high, (value - high.astype(F32)).astype(BF16)


def product(one, two, turned=False):
    rows = one.shape[0]
    one_hi, one_lo = parts(one)
    two_hi, two_lo = parts(two)
    both = dot(jnp.concatenate([one_hi, one_lo], axis=0), two_hi, turned)
    return both[:rows] + both[rows:] + dot(one_hi, two_lo, turned)


def count_rows(rows):
    rows[...] = lax.broadcasted_iota(jnp.int32, rows.shape, 0).astype(jnp.int16)


def one_hot(rows, low):
    count = low.shape[1]
    low = jnp.broadcast_to(low, (16, count)).astype(jnp.int16)[None]
    same = rows[:, :count].reshape(WIDE // 16, 16, count) == low
    return jnp.where(same, jnp.bfloat16(1), jnp.bfloat16(0)).reshape(WIDE, count)


def fill(source, value, at, nvec):
    high, low = parts(value)
    source[pl.ds(at, nvec), :WIDE] = high
    source[pl.ds(at, nvec), WIDE:] = low


def pick(rows, source, index, nvec):
    count = index.shape[1]
    hot = one_hot(rows, index & (WIDE - 1))
    hot = jnp.concatenate([hot, hot], axis=0)
    chunk = jnp.broadcast_to(index >> SHIFT, (8, count))[None]
    out = jnp.zeros((nvec // 8, 8, count), F32)
    chunks = source.shape[0] // nvec
    found = dot(source[...], hot).reshape(chunks, nvec // 8, 8, count)
    for each in range(chunks):
        out = jnp.where(chunk == each, found[each], out)
    return out.reshape(nvec, count)


def leaf_index(perm, leaf, block):
    rows = block // 128
    return jnp.concatenate([perm[pl.ds(leaf * rows + each, 1), :] for each in range(rows)], axis=1)


def fetch(pairs, sems):
    copies = [pltpu.make_async_copy(src, dst, sems.at[each]) for each, (src, dst) in enumerate(pairs)]
    for copy in copies:
        copy.start()
    return copies


def up_kernel(*refs):
    given, (tree_out, leaf_pack, tree_pack) = refs[:8], refs[8:11]
    held = refs[11:19]
    tree_vec, source, rows, sems = refs[19:]
    count_rows(rows)
    copies = fetch(list(zip(given, held)), sems)
    vec, perm, bases, leaf_maps, node_maps, leaf_skel, node_skel, sub_skel = held
    leaves, nvec, block = tree_vec.shape
    rank = bases.shape[1]
    copies[0].wait()
    for each in range(vec.shape[1] // WIDE):
        fill(source, vec[:, each * WIDE : (each + 1) * WIDE], each * nvec, nvec)
    copies[1].wait()

    def gather(leaf, carry):
        tree_vec[leaf] = pick(rows, source, leaf_index(perm, leaf, block), nvec)
        return carry

    lax.fori_loop(0, leaves, gather, 0, unroll=2)
    leave = pltpu.make_async_copy(tree_vec, tree_out, sems.at[len(copies)])
    leave.start()
    for copy in copies[2:]:
        copy.wait()
    up_node = jnp.zeros((nvec, rank), F32)
    blank = jnp.zeros((PACK_ROWS - nvec - 2, 2 * rank), F32)
    for leaf in range(0, leaves, 2):
        up = [product(tree_vec[leaf + each], bases[leaf + each], True) for each in range(2)]
        leaf_pack[leaf // 2] = jnp.concatenate(
            [
                jnp.concatenate(up, axis=1),
                jnp.concatenate([leaf_skel[leaf], leaf_skel[leaf + 1]], axis=1),
                blank,
            ],
            axis=0,
        )
        for each in range(2):
            up_node = up_node + product(up[each], leaf_maps[leaf + each])
    up_sub = product(up_node, node_maps[0])
    packed = jnp.concatenate(
        [
            jnp.concatenate([up_node, up_sub], axis=1),
            jnp.concatenate([node_skel[0], sub_skel[0]], axis=1),
            blank,
        ],
        axis=0,
    )

    def spread(each, carry):
        tree_pack[each] = packed
        return carry

    lax.fori_loop(0, tree_pack.shape[0], spread, 0)
    leave.wait()


def near_kernel(shift, *refs):
    given, (near_out, inverse_out) = refs[:3], refs[3:5]
    held = refs[5:8]
    near, inverse, flat, source, rows, across, down, slots, sems = refs[8:]
    copies = fetch(list(zip(given, held)), sems)
    crd, perm, tree_vec = held
    count_rows(rows)
    leaves, nvec, block = tree_vec.shape
    chunks = crd.shape[1] // WIDE
    scale, poly = make_tables(1.0 / math.sqrt(block))
    slope = scale[0, 1] - scale[0, 0]
    copies[0].wait()
    for axis in range(2):
        for each in range(chunks):
            row = axis * chunks + each
            flat[row : row + 1, :] = crd[axis : axis + 1, each * WIDE : (each + 1) * WIDE]
    rest = flat[...]
    for piece in range(3):
        rounded = rest.astype(BF16)
        source[piece * 2 * chunks : (piece + 1) * 2 * chunks, :] = rounded
        rest = rest - rounded.astype(F32)
    slots[...] = jnp.zeros_like(slots)
    copies[1].wait()
    side = 128
    tiles = block // side

    def place_leaf(leaf, carry):
        index = leaf_index(perm, leaf, block)
        hot = one_hot(rows, index & (WIDE - 1))
        found = dot(source[...], hot)
        found = (
            found[: 2 * chunks] + found[2 * chunks : 4 * chunks] + found[4 * chunks :]
        )
        mine = lax.broadcasted_iota(jnp.int32, (chunks, block), 0) == index >> SHIFT
        lane = lax.broadcasted_iota(jnp.int32, (chunks, block), 1) + leaf * block
        lane_low = (lane & (WIDE - 1)).astype(F32)
        lane_high = (lane >> SHIFT).astype(F32)
        marks = jnp.concatenate(
            [jnp.where(mine, lane_low, 0.0), jnp.where(mine, lane_high, 0.0)], axis=0
        ).astype(BF16)
        slots[...] += dot(marks, hot, True)
        row_x = jnp.sum(jnp.where(mine, found[:chunks], 0.0), axis=0, keepdims=True)
        row_y = jnp.sum(jnp.where(mine, found[chunks:], 0.0), axis=0, keepdims=True)
        moved = index + shift[0]
        kind = moved - 3 * ((moved * 43691) >> 17)
        row_w = kind.astype(F32) * slope
        for place, row in enumerate((row_x, row_y, row_w)):
            across[leaf, place] = jnp.broadcast_to(row, (8, block))
            turned = jnp.transpose(jnp.broadcast_to(row, (side, block)))
            down[leaf, place] = turned.reshape(block // 8, 8, side)
        return carry

    lax.fori_loop(0, leaves, place_leaf, 0, unroll=2)
    inverse[...] = (slots[:chunks] + slots[chunks:] * WIDE).astype(jnp.int32)
    leave = pltpu.make_async_copy(inverse, inverse_out, sems.at[3])
    leave.start()
    copies[2].wait()

    def one_leaf(leaf, carry):
        vec_hi, vec_lo = parts(tree_vec[leaf])
        vec_both = jnp.concatenate([vec_hi, vec_lo], axis=0)
        total = [0.0] * tiles
        for col in reversed(range(tiles)):
            cols = slice(col * side, (col + 1) * side)
            over_x, over_y, over_w = [across[leaf, each, :, cols] for each in range(3)]
            over_zero, over_one = over_w > 0.5 * slope, over_w > 1.5 * slope

            def across_table(power, first):
                zero, one, two = [float(each) for each in poly[power, first]]
                return jnp.where(over_zero, zero, jnp.where(over_one, one, two))[None]

            table = [[across_table(power, first) for first in range(3)] for power in range(5)]
            over_w = (over_w + float(scale[0, 0]))[None]
            over_x, over_y = over_x[None], over_y[None]
            high, low = [], []
            for row in range((col + 1) * side // PART):
                at = slice(row * PART // 8, (row + 1) * PART // 8)
                diff_x = down[leaf, 0, at] - over_x
                diff_y = down[leaf, 1, at] - over_y
                down_w = down[leaf, 2, at]
                var_zero, var_one = down_w > 0.5 * slope, down_w > 1.5 * slope
                square = (diff_x * diff_x + diff_y * diff_y) * (down_w + over_w)
                arg = square * lax.rsqrt(TINY - square)
                value = jnp.where(var_one, 0.0, table[4][2])
                value = value * arg + jnp.where(
                    var_zero, 0.0, jnp.where(var_one, table[3][1], table[3][2])
                )
                for power in (2, 1, 0):
                    a, b, c = table[power]
                    value = value * arg + jnp.where(var_zero, a, jnp.where(var_one, b, c))
                value = (value * jnp.exp2(arg)).reshape(PART, side)
                value_hi, value_lo = parts(value)
                high.append(value_hi)
                low.append(value_lo)
            high = jnp.concatenate(high, axis=0)
            low = jnp.concatenate(low, axis=0)
            upto = (col + 1) * side
            both = dot(vec_both[:, :upto], high)
            direct = both[:nvec] + both[nvec:] + dot(vec_hi[:, :upto], low)
            total[col] = total[col] + direct
            if col > 0:
                both = dot(vec_both[:, cols], high[: col * side], True)
                back = both[:nvec] + both[nvec:] + dot(vec_hi[:, cols], low[: col * side], True)
                for row in range(col):
                    total[row] = total[row] + back[:, row * side : (row + 1) * side]
        for col in range(tiles):
            near[leaf, :, col * side : (col + 1) * side] = total[col]
        return carry

    lax.fori_loop(0, leaves, one_leaf, 0)
    leave.wait()
    leave = pltpu.make_async_copy(near, near_out, sems.at[3])
    leave.start()
    leave.wait()


def far_kernel(groups, subtrees, *refs):
    place, leaf_src, leaf_count, node_src, node_count = refs[:5]
    given, out_at = refs[5:16], refs[16]
    held = refs[17:28]
    source, coef, twice, cols, out, rows, srcs, dsts, sems = refs[28:]
    copies = fetch(list(zip(given, held)), sems)
    leaf_all, tree_all, leaf_skel, node_skel, sub_skel, tables = held[:6]
    leaf_maps, node_maps, bases, near, inverse = held[6:]
    count_rows(rows)
    leaves, nvec, block = near.shape
    rank = bases.shape[1]
    nodes = tree_all.shape[0]
    pairs = leaf_all.shape[0]
    node_at = 2 * pairs
    beside = 3 * groups
    sub_at = node_at + beside
    blank = sub_at + subtrees
    sub_pos = place[0]
    left = lax.broadcasted_iota(jnp.int32, (PACK_ROWS, 2 * rank), 1) < rank

    def list_leaf(leaf, at):
        count = leaf_count[leaf]

        def one(step, carry):
            srcs[2 * (at + step)] = leaf_src[leaf, 2 * step]
            second = jnp.where(2 * step + 1 < count, leaf_src[leaf, 2 * step + 1], blank)
            srcs[2 * (at + step) + 1] = second
            dsts[at + step] = leaf
            return carry

        steps = (count + 1) // 2
        lax.fori_loop(0, steps, one, 0)
        return at + steps

    size = lax.fori_loop(0, leaves, list_leaf, 0)
    count = node_count[0]

    def list_node(step, carry):
        srcs[2 * (size + step)] = node_at + node_src[0, 2 * step]
        second = jnp.where(2 * step + 1 < count, node_at + node_src[0, 2 * step + 1], blank)
        srcs[2 * (size + step) + 1] = second
        dsts[size + step] = leaves
        return carry

    steps = (count + 1) // 2
    lax.fori_loop(0, steps, list_node, 0)

    def list_sub(sub, at):
        srcs[at] = sub_at + sub
        dsts[at // 2] = leaves + 1
        return at + jnp.where(jnp.abs(sub - sub_pos) >= 2, 1, 0)

    ends = lax.fori_loop(0, subtrees, list_sub, 2 * (size + steps))
    srcs[ends] = blank
    dsts[ends // 2] = leaves + 1
    ends = (ends + 1) // 2
    for each in range(AT_ONCE):
        srcs[2 * (ends + each)] = blank
        srcs[2 * (ends + each) + 1] = blank
        dsts[ends + each] = leaves + 1

    copies[0].wait()

    def both_leaves(pair, carry):
        packs = leaf_all[pair]
        turned = pltpu.roll(packs, rank, 1)
        twice[2 * pair] = jnp.where(left, packs, turned)
        twice[2 * pair + 1] = jnp.where(left, turned, packs)
        return carry

    lax.fori_loop(0, pairs, both_leaves, 0, unroll=4)
    copies[1].wait()

    def both_node(each, carry):
        packs = tree_all[jnp.clip((sub_pos - 1) * groups + each, 0, nodes - 1)]
        twice[node_at + each] = jnp.where(left, packs, pltpu.roll(packs, rank, 1))
        return carry

    lax.fori_loop(0, beside, both_node, 0, unroll=4)

    def both_sub(sub, carry):
        total = tree_all[sub * groups, :nvec]
        for each in range(1, groups):
            total = total + tree_all[sub * groups + each, :nvec]
        packs = jnp.concatenate([total, tree_all[sub * groups, nvec:]], axis=0)
        twice[sub_at + sub] = jnp.where(left, pltpu.roll(packs, rank, 1), packs)
        return carry

    lax.fori_loop(0, subtrees, both_sub, 0, unroll=2)
    twice[blank] = jnp.zeros_like(twice[blank])
    coef[...] = jnp.zeros_like(coef)
    for copy in copies[2:6]:
        copy.wait()

    def upright(skel, at):
        for axis in range(2):
            row = jnp.broadcast_to(skel[axis : axis + 1], (2 * rank, rank))
            cols[at, axis] = jnp.transpose(row)

    def upright_leaf(leaf, carry):
        upright(leaf_skel[leaf], leaf)
        return carry

    lax.fori_loop(0, leaves, upright_leaf, 0, unroll=4)
    upright(node_skel[0], leaves)
    upright(sub_skel[0], leaves + 1)

    def couple(step, carry):
        terms = []
        for each in range(AT_ONCE):
            item = step * AT_ONCE + each
            packs = jnp.where(left, twice[srcs[2 * item]], twice[srcs[2 * item + 1]])
            target = dsts[item]
            diff_x = cols[target, 0] - packs[nvec : nvec + 1]
            diff_y = cols[target, 1] - packs[nvec + 1 : nvec + 2]
            square = (diff_x * diff_x + diff_y * diff_y) * tables[0]
            arg = square * lax.rsqrt(TINY - square)
            value = tables[5]
            for power in (4, 3, 2, 1):
                value = value * arg + tables[power]
            value = value * jnp.exp2(arg)
            terms.append((target, product(packs[:nvec], value, True)))
        for target, total in terms:
            coef[target] += total
        return carry

    lax.fori_loop(0, (ends + AT_ONCE - 1) // AT_ONCE, couple, 0)
    for copy in copies[6:]:
        copy.wait()
    down_node = coef[leaves] + product(coef[leaves + 1], node_maps[0], True)
    for leaf in range(leaves):
        down_leaf = coef[leaf] + product(down_node, leaf_maps[leaf], True)
        whole = near[leaf] + product(down_leaf, bases[leaf])
        for each in range(block // WIDE):
            fill(
                source,
                whole[:, each * WIDE : (each + 1) * WIDE],
                (leaf * (block // WIDE) + each) * nvec,
                nvec,
            )

    def scatter(each, carry):
        at = pl.multiple_of(each * 2 * WIDE, 2 * WIDE)
        index = jnp.concatenate(
            [inverse[pl.ds(2 * each, 1), :], inverse[pl.ds(2 * each + 1, 1), :]], axis=1
        )
        out[:, pl.ds(at, 2 * WIDE)] = pick(rows, source, index, nvec)
        return carry

    steps = inverse.shape[0] // 2
    segments = 4
    leaving = []
    for each in range(segments):
        start, stop = each * steps // segments, (each + 1) * steps // segments
        lax.fori_loop(start, stop, scatter, 0, unroll=2)
        span = slice(start * 2 * WIDE, stop * 2 * WIDE)
        leaving.append(pltpu.make_async_copy(out.at[:, span], out_at.at[:, span], sems.at[each]))
        leaving[-1].start()
    for copy in leaving:
        copy.wait()


def skeleton_tables(rank):
    scale, poly = make_tables(1.0 / math.sqrt(rank))
    var = np.arange(rank) % 3
    rows, cols = var[:, None], np.tile(var, 2)[None, :]
    return np.stack([scale[rows, cols]] + [poly[power][rows, cols] for power in range(5)]).astype(
        np.float32
    )


def shards(
    vectors,
    coords,
    perm,
    bases,
    leaf_maps,
    node_maps,
    leaf_skel,
    node_skel,
    sub_skel,
    leaf_src,
    leaf_count,
    node_src,
    node_count,
):
    nvec, rows_dev = vectors.shape
    leaves, rank, block = bases.shape
    groups = lax.axis_size("grp")
    subtrees = lax.axis_size("leaf")
    nodes = groups * subtrees
    sub_pos = lax.axis_index("leaf")
    device_pos = sub_pos * groups + lax.axis_index("grp")
    chunks = rows_dev // WIDE
    vmem = pl.BlockSpec(memory_space=pltpu.VMEM)
    smem = pl.BlockSpec(memory_space=pltpu.SMEM)
    hbm = pl.BlockSpec(memory_space=pltpu.HBM)
    anywhere = pl.BlockSpec(memory_space=pl.ANY)
    params = pltpu.CompilerParams(vmem_limit_bytes=60 * 1024 * 1024)
    order = perm.reshape(rows_dev // 128, 128)

    def like(*arrays):
        return [pltpu.VMEM(each.shape, each.dtype) for each in arrays]

    given = (vectors, order, bases, leaf_maps, node_maps, leaf_skel, node_skel, sub_skel)
    tree_vec, leaf_pack, tree_pack = pl.pallas_call(
        up_kernel,
        out_shape=(
            jax.ShapeDtypeStruct((leaves, nvec, block), F32),
            jax.ShapeDtypeStruct((leaves // 2, PACK_ROWS, 2 * rank), F32),
            jax.ShapeDtypeStruct((nodes, PACK_ROWS, 2 * rank), F32),
        ),
        in_specs=[hbm] * 8,
        out_specs=(hbm, vmem, vmem),
        scratch_shapes=like(*given)
        + [
            pltpu.VMEM((leaves, nvec, block), F32),
            pltpu.VMEM((chunks * nvec, 2 * WIDE), BF16),
            pltpu.VMEM((WIDE, block), jnp.int16),
            pltpu.SemaphoreType.DMA((9,)),
        ],
        compiler_params=params,
        name="up",
    )(*given)
    tree_all = lax.all_to_all(tree_pack, ("leaf", "grp"), 0, 0, tiled=True)
    leaf_all = lax.all_gather(leaf_pack, "grp", axis=0, tiled=True)
    shift = (device_pos * (rows_dev % 3) % 3).astype(jnp.int32).reshape(1)
    near, inverse = pl.pallas_call(
        near_kernel,
        out_shape=(
            jax.ShapeDtypeStruct((leaves, nvec, block), F32),
            jax.ShapeDtypeStruct((chunks, WIDE), jnp.int32),
        ),
        in_specs=[smem, hbm, hbm, hbm],
        out_specs=(hbm,) * 2,
        scratch_shapes=like(coords, order, tree_vec)
        + [
            pltpu.VMEM((leaves, nvec, block), F32),
            pltpu.VMEM((chunks, WIDE), jnp.int32),
            pltpu.VMEM((2 * chunks, WIDE), F32),
            pltpu.VMEM((6 * chunks, WIDE), BF16),
            pltpu.VMEM((WIDE, block), jnp.int16),
            pltpu.VMEM((leaves, 3, 8, block), F32),
            pltpu.VMEM((leaves, 3, block // 8, 8, 128), F32),
            pltpu.VMEM((2 * chunks, WIDE), F32),
            pltpu.SemaphoreType.DMA((4,)),
        ],
        compiler_params=params,
        cost_estimate=pl.CostEstimate(
            flops=128 * leaves * block * block,
            bytes_accessed=8 * leaves * nvec * block,
            transcendentals=leaves * block * block,
        ),
        name="near",
    )(shift, coords, order, tree_vec)
    tables = jnp.asarray(skeleton_tables(rank))
    given = (leaf_all, tree_all, leaf_skel, node_skel, sub_skel, tables)
    given = given + (leaf_maps, node_maps, bases, near, inverse)
    items = (leaf_src.size + node_src.size + subtrees + 2) // 2 + AT_ONCE
    sources = groups * leaves + 3 * groups + subtrees + 1
    return pl.pallas_call(
        functools.partial(far_kernel, groups, subtrees),
        out_shape=jax.ShapeDtypeStruct((nvec, rows_dev), F32),
        in_specs=[smem] * 5 + [hbm, anywhere] + [hbm] * 9,
        out_specs=hbm,
        scratch_shapes=like(*given)
        + [
            pltpu.VMEM((chunks * nvec, 2 * WIDE), BF16),
            pltpu.VMEM((leaves + 2, nvec, rank), F32),
            pltpu.VMEM((sources, PACK_ROWS, 2 * rank), F32),
            pltpu.VMEM((leaves + 2, 2, rank, 2 * rank), F32),
            pltpu.VMEM((nvec, rows_dev), F32),
            pltpu.VMEM((WIDE, 2 * WIDE), jnp.int16),
            pltpu.SMEM((2 * items,), jnp.int32),
            pltpu.SMEM((items,), jnp.int32),
            pltpu.SemaphoreType.DMA((11,)),
        ],
        compiler_params=params,
        name="far",
    )(
        sub_pos.astype(jnp.int32).reshape(1),
        leaf_src,
        leaf_count,
        node_src,
        node_count,
        *given,
    )


def solution(mesh):
    placed = (
        P(None, ("leaf", "grp")),
        P(None, ("leaf", "grp")),
        P(("leaf", "grp")),
        P(("leaf", "grp"), None, None),
        P(("leaf", "grp"), None, None),
        P(("leaf", "grp"), None, None),
        P(("leaf", "grp"), None, None),
        P(("leaf", "grp"), None, None),
        P("leaf", None, None),
        P(("leaf", "grp"), None),
        P(("leaf", "grp")),
        P(("leaf", "grp"), None),
        P(("leaf", "grp")),
    )
    return jax.shard_map(
        shards, mesh=mesh, in_specs=placed, out_specs=P(None, ("leaf", "grp")), check_vma=False
    )
```

```python
import functools
import math

import jax
import jax.numpy as jnp
import numpy as np
from jax import lax
from jax.experimental import pallas as pl
from jax.experimental.pallas import tpu as pltpu
from jax.sharding import PartitionSpec as P

F32 = jnp.float32
BF16 = jnp.bfloat16
WIDE = 256
SHIFT = 8
LOG2E = math.log2(math.e)
TINY = 1e-37
PACK_ROWS = 24
AT_ONCE = 4


def make_tables(norm):
    smooth = [0, 2, 4]
    sigmas = [1.0, 0.8, 1.2]
    rho = [[1.0, 0.5, 0.3], [0.5, 1.0, 0.4], [0.3, 0.4, 1.0]]
    scale = np.zeros((3, 3))
    poly = np.zeros((5, 3, 3))
    for first in range(3):
        for second in range(3):
            order = (smooth[first] + smooth[second]) // 2
            scale[first, second] = -(2.0 * order + 1.0) * (LOG2E / 0.3) ** 2
            amp = sigmas[first] * sigmas[second] * rho[first][second] * norm
            for power in range(order + 1):
                kterm = order - power
                coeff = math.factorial(order) / math.factorial(2 * order)
                coeff = (
                    coeff
                    * math.factorial(order + kterm)
                    / (math.factorial(kterm) * math.factorial(order - kterm))
                )
                poly[power, first, second] = amp * coeff * 2.0**power * (-1.0 / LOG2E) ** power
    return scale, poly


def dot(one, two, turned=False):
    dims = (((1,), (1 if turned else 0,)), ((), ()))
    return lax.dot_general(one, two, dims, preferred_element_type=F32)


def parts(value):
    high = value.astype(BF16)
    return high, (value - high.astype(F32)).astype(BF16)


def product(one, two, turned=False):
    rows = one.shape[0]
    one_hi, one_lo = parts(one)
    two_hi, two_lo = parts(two)
    both = dot(jnp.concatenate([one_hi, one_lo], axis=0), two_hi, turned)
    return both[:rows] + both[rows:] + dot(one_hi, two_lo, turned)


def count_rows(rows):
    rows[...] = lax.broadcasted_iota(jnp.int32, rows.shape, 0).astype(jnp.int16)


def one_hot(rows, low):
    count = low.shape[1]
    low = jnp.broadcast_to(low, (16, count)).astype(jnp.int16)[None]
    same = rows[:, :count].reshape(WIDE // 16, 16, count) == low
    return jnp.where(same, jnp.bfloat16(1), jnp.bfloat16(0)).reshape(WIDE, count)


def fill(source, value, at, nvec):
    high, low = parts(value)
    source[pl.ds(at, nvec), :WIDE] = high
    source[pl.ds(at, nvec), WIDE:] = low


def pick(rows, source, index, nvec):
    count = index.shape[1]
    hot = one_hot(rows, index & (WIDE - 1))
    hot = jnp.concatenate([hot, hot], axis=0)
    chunk = jnp.broadcast_to(index >> SHIFT, (8, count))[None]
    out = jnp.zeros((nvec // 8, 8, count), F32)
    chunks = source.shape[0] // nvec
    found = dot(source[...], hot).reshape(chunks, nvec // 8, 8, count)
    for each in range(chunks):
        out = jnp.where(chunk == each, found[each], out)
    return out.reshape(nvec, count)


def leaf_index(perm, leaf, block):
    rows = block // 128
    return jnp.concatenate([perm[pl.ds(leaf * rows + each, 1), :] for each in range(rows)], axis=1)


def fetch(pairs, sems):
    copies = [pltpu.make_async_copy(src, dst, sems.at[each]) for each, (src, dst) in enumerate(pairs)]
    for copy in copies:
        copy.start()
    return copies


def up_kernel(*refs):
    given, (tree_out, leaf_pack, tree_pack) = refs[:8], refs[8:11]
    held = refs[11:19]
    tree_vec, source, rows, sems = refs[19:]
    count_rows(rows)
    copies = fetch(list(zip(given, held)), sems)
    vec, perm, bases, leaf_maps, node_maps, leaf_skel, node_skel, sub_skel = held
    leaves, nvec, block = tree_vec.shape
    rank = bases.shape[1]
    copies[0].wait()
    for each in range(vec.shape[1] // WIDE):
        fill(source, vec[:, each * WIDE : (each + 1) * WIDE], each * nvec, nvec)
    copies[1].wait()

    def gather(leaf, carry):
        tree_vec[leaf] = pick(rows, source, leaf_index(perm, leaf, block), nvec)
        return carry

    lax.fori_loop(0, leaves, gather, 0, unroll=2)
    leave = pltpu.make_async_copy(tree_vec, tree_out, sems.at[len(copies)])
    leave.start()
    for copy in copies[2:]:
        copy.wait()
    up_node = jnp.zeros((nvec, rank), F32)
    blank = jnp.zeros((PACK_ROWS - nvec - 2, 2 * rank), F32)
    for leaf in range(0, leaves, 2):
        up = [product(tree_vec[leaf + each], bases[leaf + each], True) for each in range(2)]
        leaf_pack[leaf // 2] = jnp.concatenate(
            [
                jnp.concatenate(up, axis=1),
                jnp.concatenate([leaf_skel[leaf], leaf_skel[leaf + 1]], axis=1),
                blank,
            ],
            axis=0,
        )
        for each in range(2):
            up_node = up_node + product(up[each], leaf_maps[leaf + each])
    up_sub = product(up_node, node_maps[0])
    packed = jnp.concatenate(
        [
            jnp.concatenate([up_node, up_sub], axis=1),
            jnp.concatenate([node_skel[0], sub_skel[0]], axis=1),
            blank,
        ],
        axis=0,
    )

    def spread(each, carry):
        tree_pack[each] = packed
        return carry

    lax.fori_loop(0, tree_pack.shape[0], spread, 0)
    leave.wait()


def near_kernel(shift, *refs):
    given, (near_out, inverse_out) = refs[:3], refs[3:5]
    held = refs[5:8]
    near, inverse, flat, source, rows, across, down, slots, order, sorts, sorted_vec = refs[8:19]
    tables, marks_vmem, marks, sems = refs[19:]
    copies = fetch(list(zip(given, held)), sems)
    crd, perm, tree_vec = held
    count_rows(rows)
    leaves, nvec, block = tree_vec.shape
    chunks = crd.shape[1] // WIDE
    scale, poly = make_tables(1.0 / math.sqrt(block))
    slope = float(scale[0, 1] - scale[0, 0])
    spread = np.concatenate([scale[None], poly], axis=0)
    copies[0].wait()
    for axis in range(2):
        for each in range(chunks):
            row = axis * chunks + each
            flat[row : row + 1, :] = crd[axis : axis + 1, each * WIDE : (each + 1) * WIDE]
    rest = flat[...]
    for piece in range(3):
        rounded = rest.astype(BF16)
        source[piece * 2 * chunks : (piece + 1) * 2 * chunks, :] = rounded
        rest = rest - rounded.astype(F32)
    slots[...] = jnp.zeros_like(slots)
    copies[1].wait()

    index = jnp.concatenate([leaf_index(perm, leaf, block) for leaf in range(leaves)], axis=0)
    moved = index + shift[0]
    kind = moved - 3 * ((moved * 43691) >> 17)
    ones = [jnp.where(kind == each, 1.0, 0.0) for each in range(2)]
    before = lax.broadcasted_iota(jnp.int32, (block, block), 0) < lax.broadcasted_iota(
        jnp.int32, (block, block), 1
    )
    before = jnp.where(before, 1.0, 0.0).astype(BF16)
    seen = dot(jnp.concatenate(ones, axis=0).astype(BF16), before)
    seen_zero, seen_one = seen[:leaves], seen[leaves:]
    size_zero, size_one = [jnp.sum(each, axis=1, keepdims=True) for each in ones]
    lane = lax.broadcasted_iota(jnp.int32, (leaves, block), 1)
    rank = jnp.where(
        kind == 0,
        seen_zero,
        jnp.where(
            kind == 1,
            size_zero + seen_one,
            size_zero + size_one + lane.astype(F32) - seen_zero - seen_one,
        ),
    )
    order[...] = rank.astype(jnp.int32)
    last = block // 8 - 1
    border_zero = jnp.broadcast_to(size_zero.astype(jnp.int32), (leaves, 128))
    border_one = jnp.broadcast_to((size_zero + size_one).astype(jnp.int32), (leaves, 128))
    tile = lax.broadcasted_iota(jnp.int32, (leaves, 128), 1)
    tile_zero = jnp.minimum(border_zero >> 3, last)
    tile_one = jnp.minimum(border_one >> 3, last)
    which = jnp.where(8 * tile >= border_zero, 1, 0) + jnp.where(8 * tile >= border_one, 1, 0)
    which = jnp.where(tile == tile_zero, 3, jnp.where(tile == tile_one, 4, which))
    which = jnp.where(tile == last + 1, border_zero, which)
    which = jnp.where(tile == last + 2, border_one, which)
    marks_vmem[...] = which
    tell = pltpu.make_async_copy(marks_vmem, marks, sems.at[4])
    tell.start()
    copies[2].wait()
    side = 128

    def place_leaf(leaf, carry):
        index = leaf_index(perm, leaf, block)
        hot = one_hot(rows, index & (WIDE - 1))
        found = dot(source[...], hot)
        found = (
            found[: 2 * chunks] + found[2 * chunks : 4 * chunks] + found[4 * chunks :]
        )
        mine = lax.broadcasted_iota(jnp.int32, (chunks, block), 0) == index >> SHIFT
        lane = lax.broadcasted_iota(jnp.int32, (chunks, block), 1) + leaf * block
        lane_low = (lane & (WIDE - 1)).astype(F32)
        lane_high = (lane >> SHIFT).astype(F32)
        own = jnp.concatenate(
            [jnp.where(mine, lane_low, 0.0), jnp.where(mine, lane_high, 0.0)], axis=0
        ).astype(BF16)
        slots[...] += dot(own, hot, True)
        row_x = jnp.sum(jnp.where(mine, found[:chunks], 0.0), axis=0, keepdims=True)
        row_y = jnp.sum(jnp.where(mine, found[chunks:], 0.0), axis=0, keepdims=True)
        rest = jnp.concatenate([row_x, row_y, jnp.zeros((6, block), F32)], axis=0)
        pieces = []
        for piece in range(2):
            rounded = rest.astype(BF16).astype(F32)
            pieces.append(rounded)
            rest = rest - rounded
        pieces = jnp.concatenate(pieces + [rest, jnp.zeros((8, block), F32)], axis=0).astype(BF16)
        vec_hi, vec_lo = parts(tree_vec[leaf])
        place = order[pl.ds(leaf, 1), :]
        sort = jnp.concatenate([one_hot(rows, place), one_hot(rows, place - WIDE)], axis=0)
        sorts[leaf] = sort
        moved = dot(jnp.concatenate([vec_hi, vec_lo, pieces], axis=0), sort, True)
        sorted_vec[leaf] = moved[: 2 * nvec].astype(BF16)
        moved = moved[2 * nvec :]
        moved = moved[:8] + moved[8:16] + moved[16:24]
        for axis in range(2):
            row = moved[axis : axis + 1]
            across[leaf, axis] = jnp.broadcast_to(row, (8, block))
            turned = jnp.transpose(jnp.broadcast_to(row, (side, block)))
            down[leaf, axis] = turned.reshape(block // 8, 8, side)
        return carry

    lax.fori_loop(0, leaves, place_leaf, 0, unroll=2)
    inverse[...] = (slots[:chunks] + slots[chunks:] * WIDE).astype(jnp.int32)
    leave = pltpu.make_async_copy(inverse, inverse_out, sems.at[3])
    leave.start()
    tell.wait()

    def one_leaf(leaf, carry):
        border_zero, border_one = marks[leaf, last + 1], marks[leaf, last + 2]
        lane = lax.broadcasted_iota(jnp.int32, (8, block), 1)
        over_zero, over_one = lane < border_zero, lane < border_one
        mixes = []
        for border in (border_zero, border_one):
            row = lax.broadcasted_iota(jnp.int32, (8, block), 0) + jnp.minimum(border >> 3, last) * 8
            mixes.append((row < border_zero, row < border_one))
        for power in range(6):
            table = []
            for first in range(3):
                zero, one, two = [float(each) for each in spread[power, first]]
                table.append(jnp.where(over_zero, zero, jnp.where(over_one, one, two)))
                tables[first, power] = table[first]
            for each, (row_zero, row_one) in enumerate(mixes):
                tables[3 + each, power] = jnp.where(
                    row_zero, table[0], jnp.where(row_one, table[1], table[2])
                )
        vec_both = sorted_vec[leaf]
        vec_hi = vec_both[:nvec]
        total = [0.0] * (block // side)

        def add(first, terms):
            for each in range(terms.shape[1] // side):
                total[first + each] = total[first + each] + terms[:, each * side : (each + 1) * side]

        def apply(cols, high, low, turned):
            both = dot(vec_both[:, cols], high, turned)
            return both[:nvec] + both[nvec:] + dot(vec_hi[:, cols], low, turned)

        for pair in reversed(range(block // WIDE)):
            at = [slice((2 * pair + each) * side, (2 * pair + each + 1) * side) for each in range(2)]
            over = [[across[leaf, axis, :, cols] for axis in range(2)] for cols in at]
            high, low = [], []
            for step in range((pair + 1) * WIDE // 16):
                halves = []
                for half in range(2):
                    if half == 0 and step * 16 >= pair * WIDE + side:
                        halves.append(jnp.zeros((16, side), F32))
                        continue
                    values = []
                    for each in (2 * step, 2 * step + 1):
                        which = marks[leaf, each]
                        diff_x = down[leaf, 0, each] - over[half][0]
                        diff_y = down[leaf, 1, each] - over[half][1]
                        square = (diff_x * diff_x + diff_y * diff_y) * tables[which, 0, :, at[half]]
                        arg = square * lax.rsqrt(TINY - square)
                        value = tables[which, 5, :, at[half]]
                        for power in (4, 3, 2, 1):
                            value = value * arg + tables[which, power, :, at[half]]
                        values.append(value * jnp.exp2(arg))
                    halves.append(jnp.concatenate(values, axis=0))
                value_hi, value_lo = parts(jnp.concatenate(halves, axis=1))
                high.append(value_hi)
                low.append(value_lo)
            high = jnp.concatenate(high, axis=0)
            low = jnp.concatenate(low, axis=0)
            start = pair * WIDE
            add(2 * pair, apply(slice(0, start + WIDE), high, low, False))
            if pair > 0:
                add(0, apply(slice(start, start + WIDE), high[:start], low[:start], True))
            corner = slice(start, start + side)
            add(2 * pair, apply(at[1], high[corner, side:], low[corner, side:], True))
        whole = jnp.concatenate(total, axis=1)
        whole_hi, whole_lo = parts(whole)
        both = dot(jnp.concatenate([whole_hi, whole_lo], axis=0), sorts[leaf])
        near[leaf] = both[:nvec] + both[nvec:]
        return carry

    lax.fori_loop(0, leaves, one_leaf, 0)
    leave.wait()
    leave = pltpu.make_async_copy(near, near_out, sems.at[3])
    leave.start()
    leave.wait()


def far_kernel(groups, subtrees, *refs):
    place, leaf_src, leaf_count, node_src, node_count = refs[:5]
    given, out_at = refs[5:16], refs[16]
    held = refs[17:28]
    source, coef, twice, cols, out, rows, srcs, dsts, sems = refs[28:]
    copies = fetch(list(zip(given, held)), sems)
    leaf_all, tree_all, leaf_skel, node_skel, sub_skel, tables = held[:6]
    leaf_maps, node_maps, bases, near, inverse = held[6:]
    count_rows(rows)
    leaves, nvec, block = near.shape
    rank = bases.shape[1]
    nodes = tree_all.shape[0]
    pairs = leaf_all.shape[0]
    node_at = 2 * pairs
    beside = 3 * groups
    sub_at = node_at + beside
    blank = sub_at + subtrees
    sub_pos = place[0]
    left = lax.broadcasted_iota(jnp.int32, (PACK_ROWS, 2 * rank), 1) < rank

    def list_leaf(leaf, at):
        count = leaf_count[leaf]

        def one(step, carry):
            srcs[2 * (at + step)] = leaf_src[leaf, 2 * step]
            second = jnp.where(2 * step + 1 < count, leaf_src[leaf, 2 * step + 1], blank)
            srcs[2 * (at + step) + 1] = second
            dsts[at + step] = leaf
            return carry

        steps = (count + 1) // 2
        lax.fori_loop(0, steps, one, 0)
        return at + steps

    size = lax.fori_loop(0, leaves, list_leaf, 0)
    count = node_count[0]

    def list_node(step, carry):
        srcs[2 * (size + step)] = node_at + node_src[0, 2 * step]
        second = jnp.where(2 * step + 1 < count, node_at + node_src[0, 2 * step + 1], blank)
        srcs[2 * (size + step) + 1] = second
        dsts[size + step] = leaves
        return carry

    steps = (count + 1) // 2
    lax.fori_loop(0, steps, list_node, 0)

    def list_sub(sub, at):
        srcs[at] = sub_at + sub
        dsts[at // 2] = leaves + 1
        return at + jnp.where(jnp.abs(sub - sub_pos) >= 2, 1, 0)

    ends = lax.fori_loop(0, subtrees, list_sub, 2 * (size + steps))
    srcs[ends] = blank
    dsts[ends // 2] = leaves + 1
    ends = (ends + 1) // 2
    for each in range(AT_ONCE):
        srcs[2 * (ends + each)] = blank
        srcs[2 * (ends + each) + 1] = blank
        dsts[ends + each] = leaves + 1

    copies[0].wait()

    def both_leaves(pair, carry):
        packs = leaf_all[pair]
        turned = pltpu.roll(packs, rank, 1)
        twice[2 * pair] = jnp.where(left, packs, turned)
        twice[2 * pair + 1] = jnp.where(left, turned, packs)
        return carry

    lax.fori_loop(0, pairs, both_leaves, 0, unroll=4)
    copies[1].wait()

    def both_node(each, carry):
        packs = tree_all[jnp.clip((sub_pos - 1) * groups + each, 0, nodes - 1)]
        twice[node_at + each] = jnp.where(left, packs, pltpu.roll(packs, rank, 1))
        return carry

    lax.fori_loop(0, beside, both_node, 0, unroll=4)

    def both_sub(sub, carry):
        total = tree_all[sub * groups, :nvec]
        for each in range(1, groups):
            total = total + tree_all[sub * groups + each, :nvec]
        packs = jnp.concatenate([total, tree_all[sub * groups, nvec:]], axis=0)
        twice[sub_at + sub] = jnp.where(left, pltpu.roll(packs, rank, 1), packs)
        return carry

    lax.fori_loop(0, subtrees, both_sub, 0, unroll=2)
    twice[blank] = jnp.zeros_like(twice[blank])
    coef[...] = jnp.zeros_like(coef)
    for copy in copies[2:6]:
        copy.wait()

    def upright(skel, at):
        for axis in range(2):
            row = jnp.broadcast_to(skel[axis : axis + 1], (2 * rank, rank))
            cols[at, axis] = jnp.transpose(row)

    def upright_leaf(leaf, carry):
        upright(leaf_skel[leaf], leaf)
        return carry

    lax.fori_loop(0, leaves, upright_leaf, 0, unroll=4)
    upright(node_skel[0], leaves)
    upright(sub_skel[0], leaves + 1)

    def couple(step, carry):
        terms = []
        for each in range(AT_ONCE):
            item = step * AT_ONCE + each
            packs = jnp.where(left, twice[srcs[2 * item]], twice[srcs[2 * item + 1]])
            target = dsts[item]
            diff_x = cols[target, 0] - packs[nvec : nvec + 1]
            diff_y = cols[target, 1] - packs[nvec + 1 : nvec + 2]
            square = (diff_x * diff_x + diff_y * diff_y) * tables[0]
            arg = square * lax.rsqrt(TINY - square)
            value = tables[5]
            for power in (4, 3, 2, 1):
                value = value * arg + tables[power]
            value = value * jnp.exp2(arg)
            terms.append((target, product(packs[:nvec], value, True)))
        for target, total in terms:
            coef[target] += total
        return carry

    lax.fori_loop(0, (ends + AT_ONCE - 1) // AT_ONCE, couple, 0)
    for copy in copies[6:]:
        copy.wait()
    down_node = coef[leaves] + product(coef[leaves + 1], node_maps[0], True)
    for leaf in range(leaves):
        down_leaf = coef[leaf] + product(down_node, leaf_maps[leaf], True)
        whole = near[leaf] + product(down_leaf, bases[leaf])
        for each in range(block // WIDE):
            fill(
                source,
                whole[:, each * WIDE : (each + 1) * WIDE],
                (leaf * (block // WIDE) + each) * nvec,
                nvec,
            )

    def scatter(each, carry):
        at = pl.multiple_of(each * 2 * WIDE, 2 * WIDE)
        index = jnp.concatenate(
            [inverse[pl.ds(2 * each, 1), :], inverse[pl.ds(2 * each + 1, 1), :]], axis=1
        )
        out[:, pl.ds(at, 2 * WIDE)] = pick(rows, source, index, nvec)
        return carry

    steps = inverse.shape[0] // 2
    segments = 4
    leaving = []
    for each in range(segments):
        start, stop = each * steps // segments, (each + 1) * steps // segments
        lax.fori_loop(start, stop, scatter, 0, unroll=2)
        span = slice(start * 2 * WIDE, stop * 2 * WIDE)
        leaving.append(pltpu.make_async_copy(out.at[:, span], out_at.at[:, span], sems.at[each]))
        leaving[-1].start()
    for copy in leaving:
        copy.wait()


def skeleton_tables(rank):
    scale, poly = make_tables(1.0 / math.sqrt(rank))
    var = np.arange(rank) % 3
    rows, cols = var[:, None], np.tile(var, 2)[None, :]
    return np.stack([scale[rows, cols]] + [poly[power][rows, cols] for power in range(5)]).astype(
        np.float32
    )


def shards(
    vectors,
    coords,
    perm,
    bases,
    leaf_maps,
    node_maps,
    leaf_skel,
    node_skel,
    sub_skel,
    leaf_src,
    leaf_count,
    node_src,
    node_count,
):
    nvec, rows_dev = vectors.shape
    leaves, rank, block = bases.shape
    groups = lax.axis_size("grp")
    subtrees = lax.axis_size("leaf")
    nodes = groups * subtrees
    sub_pos = lax.axis_index("leaf")
    device_pos = sub_pos * groups + lax.axis_index("grp")
    chunks = rows_dev // WIDE
    vmem = pl.BlockSpec(memory_space=pltpu.VMEM)
    smem = pl.BlockSpec(memory_space=pltpu.SMEM)
    hbm = pl.BlockSpec(memory_space=pltpu.HBM)
    anywhere = pl.BlockSpec(memory_space=pl.ANY)
    params = pltpu.CompilerParams(vmem_limit_bytes=60 * 1024 * 1024)
    order = perm.reshape(rows_dev // 128, 128)

    def like(*arrays):
        return [pltpu.VMEM(each.shape, each.dtype) for each in arrays]

    given = (vectors, order, bases, leaf_maps, node_maps, leaf_skel, node_skel, sub_skel)
    tree_vec, leaf_pack, tree_pack = pl.pallas_call(
        up_kernel,
        out_shape=(
            jax.ShapeDtypeStruct((leaves, nvec, block), F32),
            jax.ShapeDtypeStruct((leaves // 2, PACK_ROWS, 2 * rank), F32),
            jax.ShapeDtypeStruct((nodes, PACK_ROWS, 2 * rank), F32),
        ),
        in_specs=[hbm] * 8,
        out_specs=(hbm, vmem, vmem),
        scratch_shapes=like(*given)
        + [
            pltpu.VMEM((leaves, nvec, block), F32),
            pltpu.VMEM((chunks * nvec, 2 * WIDE), BF16),
            pltpu.VMEM((WIDE, block), jnp.int16),
            pltpu.SemaphoreType.DMA((9,)),
        ],
        compiler_params=params,
        name="up",
    )(*given)
    tree_all = lax.all_to_all(tree_pack, ("leaf", "grp"), 0, 0, tiled=True)
    leaf_all = lax.all_gather(leaf_pack, "grp", axis=0, tiled=True)
    shift = (device_pos * (rows_dev % 3) % 3).astype(jnp.int32).reshape(1)
    near, inverse = pl.pallas_call(
        near_kernel,
        out_shape=(
            jax.ShapeDtypeStruct((leaves, nvec, block), F32),
            jax.ShapeDtypeStruct((chunks, WIDE), jnp.int32),
        ),
        in_specs=[smem, hbm, hbm, hbm],
        out_specs=(hbm,) * 2,
        scratch_shapes=like(coords, order, tree_vec)
        + [
            pltpu.VMEM((leaves, nvec, block), F32),
            pltpu.VMEM((chunks, WIDE), jnp.int32),
            pltpu.VMEM((2 * chunks, WIDE), F32),
            pltpu.VMEM((6 * chunks, WIDE), BF16),
            pltpu.VMEM((WIDE, block), jnp.int16),
            pltpu.VMEM((leaves, 2, 8, block), F32),
            pltpu.VMEM((leaves, 2, block // 8, 8, 128), F32),
            pltpu.VMEM((2 * chunks, WIDE), F32),
            pltpu.VMEM((leaves, block), jnp.int32),
            pltpu.VMEM((leaves, block, block), BF16),
            pltpu.VMEM((leaves, 2 * nvec, block), BF16),
            pltpu.VMEM((5, 6, 8, block), F32),
            pltpu.VMEM((leaves, 128), jnp.int32),
            pltpu.SMEM((leaves, 128), jnp.int32),
            pltpu.SemaphoreType.DMA((5,)),
        ],
        compiler_params=params,
        cost_estimate=pl.CostEstimate(
            flops=128 * leaves * block * block,
            bytes_accessed=8 * leaves * nvec * block,
            transcendentals=leaves * block * block,
        ),
        name="near",
    )(shift, coords, order, tree_vec)
    tables = jnp.asarray(skeleton_tables(rank))
    given = (leaf_all, tree_all, leaf_skel, node_skel, sub_skel, tables)
    given = given + (leaf_maps, node_maps, bases, near, inverse)
    items = (leaf_src.size + node_src.size + subtrees + 2) // 2 + AT_ONCE
    sources = groups * leaves + 3 * groups + subtrees + 1
    return pl.pallas_call(
        functools.partial(far_kernel, groups, subtrees),
        out_shape=jax.ShapeDtypeStruct((nvec, rows_dev), F32),
        in_specs=[smem] * 5 + [hbm, anywhere] + [hbm] * 9,
        out_specs=hbm,
        scratch_shapes=like(*given)
        + [
            pltpu.VMEM((chunks * nvec, 2 * WIDE), BF16),
            pltpu.VMEM((leaves + 2, nvec, rank), F32),
            pltpu.VMEM((sources, PACK_ROWS, 2 * rank), F32),
            pltpu.VMEM((leaves + 2, 2, rank, 2 * rank), F32),
            pltpu.VMEM((nvec, rows_dev), F32),
            pltpu.VMEM((WIDE, 2 * WIDE), jnp.int16),
            pltpu.SMEM((2 * items,), jnp.int32),
            pltpu.SMEM((items,), jnp.int32),
            pltpu.SemaphoreType.DMA((11,)),
        ],
        compiler_params=params,
        name="far",
    )(
        sub_pos.astype(jnp.int32).reshape(1),
        leaf_src,
        leaf_count,
        node_src,
        node_count,
        *given,
    )


def solution(mesh):
    placed = (
        P(None, ("leaf", "grp")),
        P(None, ("leaf", "grp")),
        P(("leaf", "grp")),
        P(("leaf", "grp"), None, None),
        P(("leaf", "grp"), None, None),
        P(("leaf", "grp"), None, None),
        P(("leaf", "grp"), None, None),
        P(("leaf", "grp"), None, None),
        P("leaf", None, None),
        P(("leaf", "grp"), None),
        P(("leaf", "grp")),
        P(("leaf", "grp"), None),
        P(("leaf", "grp")),
    )
    return jax.shard_map(
        shards, mesh=mesh, in_specs=placed, out_specs=P(None, ("leaf", "grp")), check_vma=False
    )
```

```python
import functools
import math

import jax
import jax.numpy as jnp
import numpy as np
from jax import lax
from jax.experimental import pallas as pl
from jax.experimental.pallas import tpu as pltpu
from jax.sharding import PartitionSpec as P

F32 = jnp.float32
BF16 = jnp.bfloat16
WIDE = 128
SHIFT = 7
LOG2E = math.log2(math.e)
TINY = 1e-37
PACK_ROWS = 24
PART = 32
AT_ONCE = 4


def make_tables(norm):
    smooth = [0, 2, 4]
    sigmas = [1.0, 0.8, 1.2]
    rho = [[1.0, 0.5, 0.3], [0.5, 1.0, 0.4], [0.3, 0.4, 1.0]]
    scale = np.zeros((3, 3))
    poly = np.zeros((5, 3, 3))
    for first in range(3):
        for second in range(3):
            order = (smooth[first] + smooth[second]) // 2
            scale[first, second] = -(2.0 * order + 1.0) * (LOG2E / 0.3) ** 2
            amp = sigmas[first] * sigmas[second] * rho[first][second] * norm
            for power in range(order + 1):
                kterm = order - power
                coeff = math.factorial(order) / math.factorial(2 * order)
                coeff = (
                    coeff
                    * math.factorial(order + kterm)
                    / (math.factorial(kterm) * math.factorial(order - kterm))
                )
                poly[power, first, second] = amp * coeff * 2.0**power * (-1.0 / LOG2E) ** power
    return scale, poly


def dot(one, two, turned=False):
    dims = (((1,), (1 if turned else 0,)), ((), ()))
    return lax.dot_general(one, two, dims, preferred_element_type=F32)


def parts(value):
    high = value.astype(BF16)
    return high, (value - high.astype(F32)).astype(BF16)


def product(one, two, turned=False):
    rows = one.shape[0]
    one_hi, one_lo = parts(one)
    two_hi, two_lo = parts(two)
    both = dot(jnp.concatenate([one_hi, one_lo], axis=0), two_hi, turned)
    return both[:rows] + both[rows:] + dot(one_hi, two_lo, turned)


def count_rows(rows):
    rows[...] = lax.broadcasted_iota(jnp.int32, rows.shape, 0).astype(jnp.int16)


def one_hot(rows, low):
    count = low.shape[1]
    low = jnp.broadcast_to(low, (16, count)).astype(jnp.int16)[None]
    same = rows[:, :count].reshape(WIDE // 16, 16, count) == low
    return jnp.where(same, jnp.bfloat16(1), jnp.bfloat16(0)).reshape(WIDE, count)


def fill(source, value, at, nvec):
    high, low = parts(value)
    source[pl.ds(at, nvec), :WIDE] = high
    source[pl.ds(at, nvec), WIDE:] = low


def pick(rows, source, index, nvec):
    count = index.shape[1]
    hot = one_hot(rows, index & (WIDE - 1))
    hot = jnp.concatenate([hot, hot], axis=0)
    chunk = jnp.broadcast_to(index >> SHIFT, (8, count))[None]
    out = jnp.zeros((nvec // 8, 8, count), F32)
    chunks = source.shape[0] // nvec
    found = dot(source[...], hot).reshape(chunks, nvec // 8, 8, count)
    for each in range(chunks):
        out = jnp.where(chunk == each, found[each], out)
    return out.reshape(nvec, count)


def leaf_index(perm, leaf, block):
    rows = block // 128
    return jnp.concatenate([perm[pl.ds(leaf * rows + each, 1), :] for each in range(rows)], axis=1)


def fetch(pairs, sems):
    copies = [pltpu.make_async_copy(src, dst, sems.at[each]) for each, (src, dst) in enumerate(pairs)]
    for copy in copies:
        copy.start()
    return copies


def up_kernel(*refs):
    given, (tree_out, leaf_pack, tree_pack) = refs[:8], refs[8:11]
    held = refs[11:19]
    tree_vec, source, rows, sems = refs[19:]
    count_rows(rows)
    copies = fetch(list(zip(given, held)), sems)
    vec, perm, bases, leaf_maps, node_maps, leaf_skel, node_skel, sub_skel = held
    leaves, nvec, block = tree_vec.shape
    rank = bases.shape[1]
    copies[0].wait()
    for each in range(vec.shape[1] // WIDE):
        fill(source, vec[:, each * WIDE : (each + 1) * WIDE], each * nvec, nvec)
    copies[1].wait()

    def gather(leaf, carry):
        tree_vec[leaf] = pick(rows, source, leaf_index(perm, leaf, block), nvec)
        return carry

    lax.fori_loop(0, leaves, gather, 0, unroll=2)
    leave = pltpu.make_async_copy(tree_vec, tree_out, sems.at[len(copies)])
    leave.start()
    for copy in copies[2:]:
        copy.wait()
    up_node = jnp.zeros((nvec, rank), F32)
    blank = jnp.zeros((PACK_ROWS - nvec - 2, 2 * rank), F32)
    for leaf in range(0, leaves, 2):
        up = [product(tree_vec[leaf + each], bases[leaf + each], True) for each in range(2)]
        leaf_pack[leaf // 2] = jnp.concatenate(
            [
                jnp.concatenate(up, axis=1),
                jnp.concatenate([leaf_skel[leaf], leaf_skel[leaf + 1]], axis=1),
                blank,
            ],
            axis=0,
        )
        for each in range(2):
            up_node = up_node + product(up[each], leaf_maps[leaf + each])
    up_sub = product(up_node, node_maps[0])
    packed = jnp.concatenate(
        [
            jnp.concatenate([up_node, up_sub], axis=1),
            jnp.concatenate([node_skel[0], sub_skel[0]], axis=1),
            blank,
        ],
        axis=0,
    )

    def spread(each, carry):
        tree_pack[each] = packed
        return carry

    lax.fori_loop(0, tree_pack.shape[0], spread, 0)
    leave.wait()


def near_kernel(shift, *refs):
    given, (near_out, inverse_out) = refs[:3], refs[3:5]
    held = refs[5:8]
    near, inverse, flat, source, rows, across, down, slots = refs[8:16]
    sooner, later, sems = refs[16:18], refs[18:20], refs[20]
    copies = fetch(list(zip(given, held)), sems)
    crd, perm, tree_vec = held
    count_rows(rows)
    leaves, nvec, block = tree_vec.shape
    chunks = crd.shape[1] // WIDE
    scale, poly = make_tables(1.0 / math.sqrt(block))
    slope = scale[0, 1] - scale[0, 0]
    copies[0].wait()
    for axis in range(2):
        for each in range(chunks):
            row = axis * chunks + each
            flat[row : row + 1, :] = crd[axis : axis + 1, each * WIDE : (each + 1) * WIDE]
    rest = flat[...]
    for piece in range(3):
        rounded = rest.astype(BF16)
        source[piece * 2 * chunks : (piece + 1) * 2 * chunks, :] = rounded
        rest = rest - rounded.astype(F32)
    slots[...] = jnp.zeros_like(slots)
    copies[1].wait()
    side = 128
    tiles = block // side

    def place_leaf(leaf, carry):
        index = leaf_index(perm, leaf, block)
        hot = one_hot(rows, index & (WIDE - 1))
        found = dot(source[...], hot)
        found = (
            found[: 2 * chunks] + found[2 * chunks : 4 * chunks] + found[4 * chunks :]
        )
        mine = lax.broadcasted_iota(jnp.int32, (chunks, block), 0) == index >> SHIFT
        lane = lax.broadcasted_iota(jnp.int32, (chunks, block), 1) + leaf * block
        lane_low = (lane & (WIDE - 1)).astype(F32)
        lane_high = (lane >> SHIFT).astype(F32)
        marks = jnp.concatenate(
            [jnp.where(mine, lane_low, 0.0), jnp.where(mine, lane_high, 0.0)], axis=0
        ).astype(BF16)
        slots[...] += dot(marks, hot, True)
        row_x = jnp.sum(jnp.where(mine, found[:chunks], 0.0), axis=0, keepdims=True)
        row_y = jnp.sum(jnp.where(mine, found[chunks:], 0.0), axis=0, keepdims=True)
        moved = index + shift[0]
        kind = moved - 3 * ((moved * 43691) >> 17)
        row_w = kind.astype(F32) * slope
        for place, row in enumerate((row_x, row_y, row_w)):
            across[leaf, place] = jnp.broadcast_to(row, (8, block))
            turned = jnp.transpose(jnp.broadcast_to(row, (side, block)))
            down[leaf, place] = turned.reshape(block // 8, 8, side)
        return carry

    lax.fori_loop(0, leaves, place_leaf, 0, unroll=2)
    inverse[...] = (slots[:chunks] + slots[chunks:] * WIDE).astype(jnp.int32)
    leave = pltpu.make_async_copy(inverse, inverse_out, sems.at[3])
    leave.start()
    copies[2].wait()

    def values(leaf, high, low):
        for col in range(tiles):
            cols = slice(col * side, (col + 1) * side)
            over_x, over_y, over_w = [across[leaf, each, :, cols] for each in range(3)]
            over_zero, over_one = over_w > 0.5 * slope, over_w > 1.5 * slope

            def across_table(power, first):
                zero, one, two = [float(each) for each in poly[power, first]]
                return jnp.where(over_zero, zero, jnp.where(over_one, one, two))[None]

            table = [[across_table(power, first) for first in range(3)] for power in range(5)]
            over_w = (over_w + float(scale[0, 0]))[None]
            over_x, over_y = over_x[None], over_y[None]
            for row in range(col + 1):
                pieces = []
                for part in range(side // PART):
                    first = row * side + part * PART
                    at = slice(first // 8, (first + PART) // 8)
                    diff_x = down[leaf, 0, at] - over_x
                    diff_y = down[leaf, 1, at] - over_y
                    down_w = down[leaf, 2, at]
                    var_zero, var_one = down_w > 0.5 * slope, down_w > 1.5 * slope
                    square = (diff_x * diff_x + diff_y * diff_y) * (down_w + over_w)
                    arg = square * lax.rsqrt(TINY - square)
                    value = jnp.where(var_one, 0.0, table[4][2])
                    value = value * arg + jnp.where(
                        var_zero, 0.0, jnp.where(var_one, table[3][1], table[3][2])
                    )
                    for power in (2, 1, 0):
                        a, b, c = table[power]
                        value = value * arg + jnp.where(var_zero, a, jnp.where(var_one, b, c))
                    pieces.append(parts((value * jnp.exp2(arg)).reshape(PART, side)))
                rows = slice(row * side, (row + 1) * side)
                for each, out in enumerate((high, low)):
                    tile = jnp.concatenate([piece[each] for piece in pieces], axis=0)
                    out[rows, cols] = tile
                    if row < col:
                        out[cols, rows] = jnp.transpose(tile)

    def apply(leaf, high, low):
        vec_hi, vec_lo = parts(tree_vec[leaf])
        both = dot(jnp.concatenate([vec_hi, vec_lo], axis=0), high[...])
        near[leaf] = both[:nvec] + both[nvec:] + dot(vec_hi, low[...])

    for each in later:
        each[...] = jnp.zeros_like(each)

    def two_leaves(step, carry):
        apply(jnp.maximum(2 * step - 1, 0), *later)
        values(2 * step, *sooner)
        apply(2 * step, *sooner)
        values(2 * step + 1, *later)
        return carry

    lax.fori_loop(0, leaves // 2, two_leaves, 0)
    apply(leaves - 1, *later)
    leave.wait()
    leave = pltpu.make_async_copy(near, near_out, sems.at[3])
    leave.start()
    leave.wait()


def far_kernel(groups, subtrees, *refs):
    place, leaf_src, leaf_count, node_src, node_count = refs[:5]
    given, out_at = refs[5:16], refs[16]
    held = refs[17:28]
    source, coef, twice, cols, out, rows, srcs, dsts, sems = refs[28:]
    copies = fetch(list(zip(given, held)), sems)
    leaf_all, tree_all, leaf_skel, node_skel, sub_skel, tables = held[:6]
    leaf_maps, node_maps, bases, near, inverse = held[6:]
    count_rows(rows)
    leaves, nvec, block = near.shape
    rank = bases.shape[1]
    nodes = tree_all.shape[0]
    pairs = leaf_all.shape[0]
    node_at = 2 * pairs
    beside = 3 * groups
    sub_at = node_at + beside
    blank = sub_at + subtrees
    sub_pos = place[0]
    left = lax.broadcasted_iota(jnp.int32, (PACK_ROWS, 2 * rank), 1) < rank

    def list_leaf(leaf, at):
        count = leaf_count[leaf]

        def one(step, carry):
            srcs[2 * (at + step)] = leaf_src[leaf, 2 * step]
            second = jnp.where(2 * step + 1 < count, leaf_src[leaf, 2 * step + 1], blank)
            srcs[2 * (at + step) + 1] = second
            dsts[at + step] = leaf
            return carry

        steps = (count + 1) // 2
        lax.fori_loop(0, steps, one, 0)
        return at + steps

    size = lax.fori_loop(0, leaves, list_leaf, 0)
    count = node_count[0]

    def list_node(step, carry):
        srcs[2 * (size + step)] = node_at + node_src[0, 2 * step]
        second = jnp.where(2 * step + 1 < count, node_at + node_src[0, 2 * step + 1], blank)
        srcs[2 * (size + step) + 1] = second
        dsts[size + step] = leaves
        return carry

    steps = (count + 1) // 2
    lax.fori_loop(0, steps, list_node, 0)

    def list_sub(sub, at):
        srcs[at] = sub_at + sub
        dsts[at // 2] = leaves + 1
        return at + jnp.where(jnp.abs(sub - sub_pos) >= 2, 1, 0)

    ends = lax.fori_loop(0, subtrees, list_sub, 2 * (size + steps))
    srcs[ends] = blank
    dsts[ends // 2] = leaves + 1
    ends = (ends + 1) // 2
    for each in range(AT_ONCE):
        srcs[2 * (ends + each)] = blank
        srcs[2 * (ends + each) + 1] = blank
        dsts[ends + each] = leaves + 1

    copies[0].wait()

    def both_leaves(pair, carry):
        packs = leaf_all[pair]
        turned = pltpu.roll(packs, rank, 1)
        twice[2 * pair] = jnp.where(left, packs, turned)
        twice[2 * pair + 1] = jnp.where(left, turned, packs)
        return carry

    lax.fori_loop(0, pairs, both_leaves, 0, unroll=4)
    copies[1].wait()

    def both_node(each, carry):
        packs = tree_all[jnp.clip((sub_pos - 1) * groups + each, 0, nodes - 1)]
        twice[node_at + each] = jnp.where(left, packs, pltpu.roll(packs, rank, 1))
        return carry

    lax.fori_loop(0, beside, both_node, 0, unroll=4)

    def both_sub(sub, carry):
        total = tree_all[sub * groups, :nvec]
        for each in range(1, groups):
            total = total + tree_all[sub * groups + each, :nvec]
        packs = jnp.concatenate([total, tree_all[sub * groups, nvec:]], axis=0)
        twice[sub_at + sub] = jnp.where(left, pltpu.roll(packs, rank, 1), packs)
        return carry

    lax.fori_loop(0, subtrees, both_sub, 0, unroll=2)
    twice[blank] = jnp.zeros_like(twice[blank])
    coef[...] = jnp.zeros_like(coef)
    for copy in copies[2:6]:
        copy.wait()

    def upright(skel, at):
        for axis in range(2):
            row = jnp.broadcast_to(skel[axis : axis + 1], (2 * rank, rank))
            cols[at, axis] = jnp.transpose(row)

    def upright_leaf(leaf, carry):
        upright(leaf_skel[leaf], leaf)
        return carry

    lax.fori_loop(0, leaves, upright_leaf, 0, unroll=4)
    upright(node_skel[0], leaves)
    upright(sub_skel[0], leaves + 1)

    def couple(step, carry):
        terms = []
        for each in range(AT_ONCE):
            item = step * AT_ONCE + each
            packs = jnp.where(left, twice[srcs[2 * item]], twice[srcs[2 * item + 1]])
            target = dsts[item]
            diff_x = cols[target, 0] - packs[nvec : nvec + 1]
            diff_y = cols[target, 1] - packs[nvec + 1 : nvec + 2]
            square = (diff_x * diff_x + diff_y * diff_y) * tables[0]
            arg = square * lax.rsqrt(TINY - square)
            value = tables[5]
            for power in (4, 3, 2, 1):
                value = value * arg + tables[power]
            value = value * jnp.exp2(arg)
            terms.append((target, product(packs[:nvec], value, True)))
        for target, total in terms:
            coef[target] += total
        return carry

    lax.fori_loop(0, (ends + AT_ONCE - 1) // AT_ONCE, couple, 0)
    for copy in copies[6:]:
        copy.wait()
    down_node = coef[leaves] + product(coef[leaves + 1], node_maps[0], True)
    for leaf in range(leaves):
        down_leaf = coef[leaf] + product(down_node, leaf_maps[leaf], True)
        whole = near[leaf] + product(down_leaf, bases[leaf])
        for each in range(block // WIDE):
            fill(
                source,
                whole[:, each * WIDE : (each + 1) * WIDE],
                (leaf * (block // WIDE) + each) * nvec,
                nvec,
            )

    def scatter(each, carry):
        at = pl.multiple_of(each * block, block)
        out[:, pl.ds(at, block)] = pick(rows, source, leaf_index(inverse, each, block), nvec)
        return carry

    steps = inverse.shape[0] * WIDE // block
    segments = 4
    leaving = []
    for each in range(segments):
        start, stop = each * steps // segments, (each + 1) * steps // segments
        lax.fori_loop(start, stop, scatter, 0, unroll=2)
        span = slice(start * block, stop * block)
        leaving.append(pltpu.make_async_copy(out.at[:, span], out_at.at[:, span], sems.at[each]))
        leaving[-1].start()
    for copy in leaving:
        copy.wait()


def skeleton_tables(rank):
    scale, poly = make_tables(1.0 / math.sqrt(rank))
    var = np.arange(rank) % 3
    rows, cols = var[:, None], np.tile(var, 2)[None, :]
    return np.stack([scale[rows, cols]] + [poly[power][rows, cols] for power in range(5)]).astype(
        np.float32
    )


def shards(
    vectors,
    coords,
    perm,
    bases,
    leaf_maps,
    node_maps,
    leaf_skel,
    node_skel,
    sub_skel,
    leaf_src,
    leaf_count,
    node_src,
    node_count,
):
    nvec, rows_dev = vectors.shape
    leaves, rank, block = bases.shape
    groups = lax.axis_size("grp")
    subtrees = lax.axis_size("leaf")
    nodes = groups * subtrees
    sub_pos = lax.axis_index("leaf")
    device_pos = sub_pos * groups + lax.axis_index("grp")
    chunks = rows_dev // WIDE
    vmem = pl.BlockSpec(memory_space=pltpu.VMEM)
    smem = pl.BlockSpec(memory_space=pltpu.SMEM)
    hbm = pl.BlockSpec(memory_space=pltpu.HBM)
    anywhere = pl.BlockSpec(memory_space=pl.ANY)
    params = pltpu.CompilerParams(vmem_limit_bytes=60 * 1024 * 1024)
    order = perm.reshape(rows_dev // 128, 128)

    def like(*arrays):
        return [pltpu.VMEM(each.shape, each.dtype) for each in arrays]

    given = (vectors, order, bases, leaf_maps, node_maps, leaf_skel, node_skel, sub_skel)
    tree_vec, leaf_pack, tree_pack = pl.pallas_call(
        up_kernel,
        out_shape=(
            jax.ShapeDtypeStruct((leaves, nvec, block), F32),
            jax.ShapeDtypeStruct((leaves // 2, PACK_ROWS, 2 * rank), F32),
            jax.ShapeDtypeStruct((nodes, PACK_ROWS, 2 * rank), F32),
        ),
        in_specs=[hbm] * 8,
        out_specs=(hbm, vmem, vmem),
        scratch_shapes=like(*given)
        + [
            pltpu.VMEM((leaves, nvec, block), F32),
            pltpu.VMEM((chunks * nvec, 2 * WIDE), BF16),
            pltpu.VMEM((WIDE, block), jnp.int16),
            pltpu.SemaphoreType.DMA((9,)),
        ],
        compiler_params=params,
        name="up",
    )(*given)
    tree_all = lax.all_to_all(tree_pack, ("leaf", "grp"), 0, 0, tiled=True)
    leaf_all = lax.all_gather(leaf_pack, "grp", axis=0, tiled=True)
    shift = (device_pos * (rows_dev % 3) % 3).astype(jnp.int32).reshape(1)
    near, inverse = pl.pallas_call(
        near_kernel,
        out_shape=(
            jax.ShapeDtypeStruct((leaves, nvec, block), F32),
            jax.ShapeDtypeStruct((chunks, WIDE), jnp.int32),
        ),
        in_specs=[smem, hbm, hbm, hbm],
        out_specs=(hbm,) * 2,
        scratch_shapes=like(coords, order, tree_vec)
        + [
            pltpu.VMEM((leaves, nvec, block), F32),
            pltpu.VMEM((chunks, WIDE), jnp.int32),
            pltpu.VMEM((2 * chunks, WIDE), F32),
            pltpu.VMEM((6 * chunks, WIDE), BF16),
            pltpu.VMEM((WIDE, block), jnp.int16),
            pltpu.VMEM((leaves, 3, 8, block), F32),
            pltpu.VMEM((leaves, 3, block // 8, 8, 128), F32),
            pltpu.VMEM((2 * chunks, WIDE), F32),
            *[pltpu.VMEM((block, block), BF16)] * 4,
            pltpu.SemaphoreType.DMA((4,)),
        ],
        compiler_params=params,
        cost_estimate=pl.CostEstimate(
            flops=128 * leaves * block * block,
            bytes_accessed=8 * leaves * nvec * block,
            transcendentals=leaves * block * block,
        ),
        name="near",
    )(shift, coords, order, tree_vec)
    tables = jnp.asarray(skeleton_tables(rank))
    given = (leaf_all, tree_all, leaf_skel, node_skel, sub_skel, tables)
    given = given + (leaf_maps, node_maps, bases, near, inverse)
    items = (leaf_src.size + node_src.size + subtrees + 2) // 2 + AT_ONCE
    sources = groups * leaves + 3 * groups + subtrees + 1
    return pl.pallas_call(
        functools.partial(far_kernel, groups, subtrees),
        out_shape=jax.ShapeDtypeStruct((nvec, rows_dev), F32),
        in_specs=[smem] * 5 + [hbm, anywhere] + [hbm] * 9,
        out_specs=hbm,
        scratch_shapes=like(*given)
        + [
            pltpu.VMEM((chunks * nvec, 2 * WIDE), BF16),
            pltpu.VMEM((leaves + 2, nvec, rank), F32),
            pltpu.VMEM((sources, PACK_ROWS, 2 * rank), F32),
            pltpu.VMEM((leaves + 2, 2, rank, 2 * rank), F32),
            pltpu.VMEM((nvec, rows_dev), F32),
            pltpu.VMEM((WIDE, block), jnp.int16),
            pltpu.SMEM((2 * items,), jnp.int32),
            pltpu.SMEM((items,), jnp.int32),
            pltpu.SemaphoreType.DMA((11,)),
        ],
        compiler_params=params,
        name="far",
    )(
        sub_pos.astype(jnp.int32).reshape(1),
        leaf_src,
        leaf_count,
        node_src,
        node_count,
        *given,
    )


def solution(mesh):
    placed = (
        P(None, ("leaf", "grp")),
        P(None, ("leaf", "grp")),
        P(("leaf", "grp")),
        P(("leaf", "grp"), None, None),
        P(("leaf", "grp"), None, None),
        P(("leaf", "grp"), None, None),
        P(("leaf", "grp"), None, None),
        P(("leaf", "grp"), None, None),
        P("leaf", None, None),
        P(("leaf", "grp"), None),
        P(("leaf", "grp")),
        P(("leaf", "grp"), None),
        P(("leaf", "grp")),
    )
    return jax.shard_map(
        shards, mesh=mesh, in_specs=placed, out_specs=P(None, ("leaf", "grp")), check_vma=False
    )
```

```python
import functools
import math

import jax
import jax.numpy as jnp
import ml_dtypes
import numpy as np
from jax import lax
from jax.experimental import pallas as pl
from jax.experimental.pallas import tpu as pltpu
from jax.sharding import PartitionSpec as P

F32 = jnp.float32
BF16 = jnp.bfloat16
WIDE = 128
SHIFT = 7
LOG2E = math.log2(math.e)
TINY = 1e-37
PACK_ROWS = 24
PART = 32
AT_ONCE = 4


def make_tables(norm):
    smooth = [0, 2, 4]
    sigmas = [1.0, 0.8, 1.2]
    rho = [[1.0, 0.5, 0.3], [0.5, 1.0, 0.4], [0.3, 0.4, 1.0]]
    scale = np.zeros((3, 3))
    poly = np.zeros((5, 3, 3))
    for first in range(3):
        for second in range(3):
            order = (smooth[first] + smooth[second]) // 2
            scale[first, second] = -(2.0 * order + 1.0) * (LOG2E / 0.3) ** 2
            amp = sigmas[first] * sigmas[second] * rho[first][second] * norm
            for power in range(order + 1):
                kterm = order - power
                coeff = math.factorial(order) / math.factorial(2 * order)
                coeff = (
                    coeff
                    * math.factorial(order + kterm)
                    / (math.factorial(kterm) * math.factorial(order - kterm))
                )
                poly[power, first, second] = amp * coeff * 2.0**power * (-1.0 / LOG2E) ** power
    return scale, poly


def dot(one, two, turned=False):
    dims = (((1,), (1 if turned else 0,)), ((), ()))
    return lax.dot_general(one, two, dims, preferred_element_type=F32)


def parts(value):
    high = value.astype(BF16)
    return high, (value - high.astype(F32)).astype(BF16)


def product(one, two, turned=False):
    rows = one.shape[0]
    one_hi, one_lo = parts(one)
    two_hi, two_lo = parts(two)
    both = dot(jnp.concatenate([one_hi, one_lo], axis=0), two_hi, turned)
    return both[:rows] + both[rows:] + dot(one_hi, two_lo, turned)


def count_rows(rows):
    rows[...] = lax.broadcasted_iota(jnp.int32, rows.shape, 0).astype(jnp.int16)


def one_hot(rows, low):
    count = low.shape[1]
    low = jnp.broadcast_to(low, (16, count)).astype(jnp.int16)[None]
    same = rows[:, :count].reshape(WIDE // 16, 16, count) == low
    return jnp.where(same, jnp.bfloat16(1), jnp.bfloat16(0)).reshape(WIDE, count)


def fill(source, value, at, nvec):
    high, low = parts(value)
    source[pl.ds(at, nvec), :WIDE] = high
    source[pl.ds(at, nvec), WIDE:] = low


def pick(rows, source, index, nvec):
    count = index.shape[1]
    hot = one_hot(rows, index & (WIDE - 1))
    hot = jnp.concatenate([hot, hot], axis=0)
    chunk = jnp.broadcast_to(index >> SHIFT, (8, count))[None]
    out = jnp.zeros((nvec // 8, 8, count), F32)
    chunks = source.shape[0] // nvec
    found = dot(source[...], hot).reshape(chunks, nvec // 8, 8, count)
    for each in range(chunks):
        out = jnp.where(chunk == each, found[each], out)
    return out.reshape(nvec, count)


def leaf_index(perm, leaf, block):
    rows = block // 128
    return jnp.concatenate([perm[pl.ds(leaf * rows + each, 1), :] for each in range(rows)], axis=1)


def fetch(pairs, sems):
    copies = [pltpu.make_async_copy(src, dst, sems.at[each]) for each, (src, dst) in enumerate(pairs)]
    for copy in copies:
        copy.start()
    return copies


def up_kernel(*refs):
    given, (tree_out, leaf_pack, tree_pack) = refs[:8], refs[8:11]
    held = refs[11:19]
    tree_vec, source, rows, sems = refs[19:]
    count_rows(rows)
    copies = fetch(list(zip(given, held)), sems)
    vec, perm, bases, leaf_maps, node_maps, leaf_skel, node_skel, sub_skel = held
    leaves, nvec, block = tree_vec.shape
    rank = bases.shape[1]
    copies[0].wait()
    for each in range(vec.shape[1] // WIDE):
        fill(source, vec[:, each * WIDE : (each + 1) * WIDE], each * nvec, nvec)
    copies[1].wait()

    def gather(leaf, carry):
        tree_vec[leaf] = pick(rows, source, leaf_index(perm, leaf, block), nvec)
        return carry

    lax.fori_loop(0, leaves, gather, 0, unroll=2)
    leave = pltpu.make_async_copy(tree_vec, tree_out, sems.at[len(copies)])
    leave.start()
    for copy in copies[2:]:
        copy.wait()
    up_node = jnp.zeros((nvec, rank), F32)
    blank = jnp.zeros((PACK_ROWS - nvec - 2, 2 * rank), F32)
    for leaf in range(0, leaves, 2):
        up = [product(tree_vec[leaf + each], bases[leaf + each], True) for each in range(2)]
        leaf_pack[leaf // 2] = jnp.concatenate(
            [
                jnp.concatenate(up, axis=1),
                jnp.concatenate([leaf_skel[leaf], leaf_skel[leaf + 1]], axis=1),
                blank,
            ],
            axis=0,
        )
        for each in range(2):
            up_node = up_node + product(up[each], leaf_maps[leaf + each])
    up_sub = product(up_node, node_maps[0])
    packed = jnp.concatenate(
        [
            jnp.concatenate([up_node, up_sub], axis=1),
            jnp.concatenate([node_skel[0], sub_skel[0]], axis=1),
            blank,
        ],
        axis=0,
    )

    def spread(each, carry):
        tree_pack[each] = packed
        return carry

    lax.fori_loop(0, tree_pack.shape[0], spread, 0)
    leave.wait()


def near_kernel(shift, *refs):
    given, (near_out, inverse_out) = refs[:3], refs[3:5]
    held = refs[5:8]
    near, inverse, flat, source, rows, across, down, slots = refs[8:16]
    sooner, later, sems = refs[16:18], refs[18:20], refs[20]
    copies = fetch(list(zip(given, held)), sems)
    crd, perm, tree_vec = held
    count_rows(rows)
    leaves, nvec, block = tree_vec.shape
    chunks = crd.shape[1] // WIDE
    scale, poly = make_tables(1.0 / math.sqrt(block))
    slope = scale[0, 1] - scale[0, 0]
    copies[0].wait()
    for axis in range(2):
        for each in range(chunks):
            row = axis * chunks + each
            flat[row : row + 1, :] = crd[axis : axis + 1, each * WIDE : (each + 1) * WIDE]
    rest = flat[...]
    for piece in range(3):
        rounded = rest.astype(BF16)
        source[piece * 2 * chunks : (piece + 1) * 2 * chunks, :] = rounded
        rest = rest - rounded.astype(F32)
    slots[...] = jnp.zeros_like(slots)
    copies[1].wait()
    side = 128
    tiles = block // side

    def three(row):
        pieces = []
        for _ in range(3):
            pieces.append(row.astype(BF16).astype(F32))
            row = row - pieces[-1]
        return pieces

    part = lax.broadcasted_iota(jnp.int32, (16, 3 * side), 0)
    third = lax.broadcasted_iota(jnp.int32, (16, 3 * side), 1) // side
    widen = jnp.where((part < 6) & (part // 3 == third), 1.0, 0.0)
    left = np.float32(slope)
    for each in range(3):
        piece = np.float32(left.astype(ml_dtypes.bfloat16))
        widen = jnp.where((part == 6 + each) & (third == 2), float(piece), widen)
        left = left - piece
    widen = widen.astype(BF16)

    def place_leaf(leaf, carry):
        index = leaf_index(perm, leaf, block)
        hot = one_hot(rows, index & (WIDE - 1))
        found = dot(source[...], hot)
        found = (
            found[: 2 * chunks] + found[2 * chunks : 4 * chunks] + found[4 * chunks :]
        )
        mine = lax.broadcasted_iota(jnp.int32, (chunks, block), 0) == index >> SHIFT
        lane = lax.broadcasted_iota(jnp.int32, (chunks, block), 1) + leaf * block
        lane_low = (lane & (WIDE - 1)).astype(F32)
        lane_high = (lane >> SHIFT).astype(F32)
        marks = jnp.concatenate(
            [jnp.where(mine, lane_low, 0.0), jnp.where(mine, lane_high, 0.0)], axis=0
        ).astype(BF16)
        slots[...] += dot(marks, hot, True)
        row_x = jnp.sum(jnp.where(mine, found[:chunks], 0.0), axis=0, keepdims=True)
        row_y = jnp.sum(jnp.where(mine, found[chunks:], 0.0), axis=0, keepdims=True)
        moved = index + shift[0]
        kind = moved - 3 * ((moved * 43691) >> 17)
        row_w = kind.astype(F32) * slope
        for place, row in enumerate((row_x, row_y, row_w)):
            across[leaf, place] = jnp.broadcast_to(row, (8, block))
        stack = three(row_x) + three(row_y) + [kind.astype(F32)] * 3
        stack = jnp.concatenate(stack + [jnp.zeros((7, block), F32)], axis=0).astype(BF16)
        columns = dot(jnp.transpose(stack), widen)
        for place in range(3):
            column = columns[:, place * side : (place + 1) * side]
            down[leaf, place] = column.reshape(block // 8, 8, side)
        return carry

    lax.fori_loop(0, leaves, place_leaf, 0, unroll=4)
    inverse[...] = (slots[:chunks] + slots[chunks:] * WIDE).astype(jnp.int32)
    leave = pltpu.make_async_copy(inverse, inverse_out, sems.at[3])
    leave.start()
    copies[2].wait()

    def values(leaf, high, low):
        for col in range(tiles):
            cols = slice(col * side, (col + 1) * side)
            over_x, over_y, over_w = [across[leaf, each, :, cols] for each in range(3)]
            over_zero, over_one = over_w > 0.5 * slope, over_w > 1.5 * slope

            def across_table(power, first):
                zero, one, two = [float(each) for each in poly[power, first]]
                return jnp.where(over_zero, zero, jnp.where(over_one, one, two))[None]

            table = [[across_table(power, first) for first in range(3)] for power in range(5)]
            over_w = (over_w + float(scale[0, 0]))[None]
            over_x, over_y = over_x[None], over_y[None]
            for row in range(col + 1):
                pieces = []
                for part in range(side // PART):
                    first = row * side + part * PART
                    at = slice(first // 8, (first + PART) // 8)
                    diff_x = down[leaf, 0, at] - over_x
                    diff_y = down[leaf, 1, at] - over_y
                    down_w = down[leaf, 2, at]
                    var_zero, var_one = down_w > 0.5 * slope, down_w > 1.5 * slope
                    square = (diff_x * diff_x + diff_y * diff_y) * (down_w + over_w)
                    arg = square * lax.rsqrt(TINY - square)
                    value = jnp.where(var_one, 0.0, table[4][2])
                    value = value * arg + jnp.where(
                        var_zero, 0.0, jnp.where(var_one, table[3][1], table[3][2])
                    )
                    for power in (2, 1, 0):
                        a, b, c = table[power]
                        value = value * arg + jnp.where(var_zero, a, jnp.where(var_one, b, c))
                    pieces.append(parts((value * jnp.exp2(arg)).reshape(PART, side)))
                rows = slice(row * side, (row + 1) * side)
                for each, out in enumerate((high, low)):
                    tile = jnp.concatenate([piece[each] for piece in pieces], axis=0)
                    out[rows, cols] = tile
                    if row < col:
                        out[cols, rows] = jnp.transpose(tile)

    def apply(leaf, high, low):
        vec_hi, vec_lo = parts(tree_vec[leaf])
        both = dot(jnp.concatenate([vec_hi, vec_lo], axis=0), high[...])
        near[leaf] = both[:nvec] + both[nvec:] + dot(vec_hi, low[...])

    for each in later:
        each[...] = jnp.zeros_like(each)

    def two_leaves(step, carry):
        apply(jnp.maximum(2 * step - 1, 0), *later)
        values(2 * step, *sooner)
        apply(2 * step, *sooner)
        values(2 * step + 1, *later)
        return carry

    lax.fori_loop(0, leaves // 4, two_leaves, 0)
    half = slice(0, leaves // 2 - 1)
    first = pltpu.make_async_copy(near.at[half], near_out.at[half], sems.at[0])
    first.start()
    lax.fori_loop(leaves // 4, leaves // 2, two_leaves, 0)
    apply(leaves - 1, *later)
    half = slice(leaves // 2 - 1, leaves)
    second = pltpu.make_async_copy(near.at[half], near_out.at[half], sems.at[1])
    second.start()
    for copy in (leave, first, second):
        copy.wait()


def far_kernel(groups, subtrees, *refs):
    place, leaf_src, leaf_count, node_src, node_count = refs[:5]
    leaf_packs, refs = refs[5 : 5 + groups], refs[5 + groups :]
    given, out_at, held = refs[:10], refs[10], refs[11:21]
    leaf_all, source, coef, twice, cols, out, rows, srcs, dsts, sems = refs[21:]
    own = leaf_packs[0].shape[0]
    owner = [lax.rem(place[1] - shift + groups, groups) for shift in range(groups)]
    arrive = [leaf_all.at[pl.ds(each * own, own)] for each in owner]
    copies = fetch(list(zip(leaf_packs + given, arrive + list(held))), sems)
    leaf_copies, copies = copies[:groups], [None] + copies[groups:]
    tree_all, leaf_skel, node_skel, sub_skel, tables = held[:5]
    leaf_maps, node_maps, bases, near, inverse = held[5:]
    count_rows(rows)
    leaves, nvec, block = near.shape
    rank = bases.shape[1]
    nodes = tree_all.shape[0]
    pairs = leaf_all.shape[0]
    node_at = 2 * pairs
    beside = 3 * groups
    sub_at = node_at + beside
    blank = sub_at + subtrees
    sub_pos = place[0]
    left = lax.broadcasted_iota(jnp.int32, (PACK_ROWS, 2 * rank), 1) < rank

    def list_leaf(leaf, at):
        count = leaf_count[leaf]

        def one(step, carry):
            srcs[2 * (at + step)] = leaf_src[leaf, 2 * step]
            second = jnp.where(2 * step + 1 < count, leaf_src[leaf, 2 * step + 1], blank)
            srcs[2 * (at + step) + 1] = second
            dsts[at + step] = leaf
            return carry

        steps = (count + 1) // 2
        lax.fori_loop(0, steps, one, 0)
        return at + steps

    size = lax.fori_loop(0, leaves, list_leaf, 0)
    count = node_count[0]

    def list_node(step, carry):
        srcs[2 * (size + step)] = node_at + node_src[0, 2 * step]
        second = jnp.where(2 * step + 1 < count, node_at + node_src[0, 2 * step + 1], blank)
        srcs[2 * (size + step) + 1] = second
        dsts[size + step] = leaves
        return carry

    steps = (count + 1) // 2
    lax.fori_loop(0, steps, list_node, 0)

    def list_sub(sub, at):
        srcs[at] = sub_at + sub
        dsts[at // 2] = leaves + 1
        return at + jnp.where(jnp.abs(sub - sub_pos) >= 2, 1, 0)

    ends = lax.fori_loop(0, subtrees, list_sub, 2 * (size + steps))
    srcs[ends] = blank
    dsts[ends // 2] = leaves + 1
    ends = (ends + 1) // 2
    for each in range(AT_ONCE):
        srcs[2 * (ends + each)] = blank
        srcs[2 * (ends + each) + 1] = blank
        dsts[ends + each] = leaves + 1

    for copy in leaf_copies:
        copy.wait()

    def both_leaves(pair, carry):
        packs = leaf_all[pair]
        turned = pltpu.roll(packs, rank, 1)
        twice[2 * pair] = jnp.where(left, packs, turned)
        twice[2 * pair + 1] = jnp.where(left, turned, packs)
        return carry

    lax.fori_loop(0, pairs, both_leaves, 0, unroll=4)
    copies[1].wait()

    def both_node(each, carry):
        packs = tree_all[jnp.clip((sub_pos - 1) * groups + each, 0, nodes - 1)]
        twice[node_at + each] = jnp.where(left, packs, pltpu.roll(packs, rank, 1))
        return carry

    lax.fori_loop(0, beside, both_node, 0, unroll=4)

    def both_sub(sub, carry):
        total = tree_all[sub * groups, :nvec]
        for each in range(1, groups):
            total = total + tree_all[sub * groups + each, :nvec]
        packs = jnp.concatenate([total, tree_all[sub * groups, nvec:]], axis=0)
        twice[sub_at + sub] = jnp.where(left, pltpu.roll(packs, rank, 1), packs)
        return carry

    lax.fori_loop(0, subtrees, both_sub, 0, unroll=2)
    twice[blank] = jnp.zeros_like(twice[blank])
    coef[...] = jnp.zeros_like(coef)
    for copy in copies[2:6]:
        copy.wait()

    def upright(skel, at):
        for axis in range(2):
            row = jnp.broadcast_to(skel[axis : axis + 1], (2 * rank, rank))
            cols[at, axis] = jnp.transpose(row)

    def upright_leaf(leaf, carry):
        upright(leaf_skel[leaf], leaf)
        return carry

    lax.fori_loop(0, leaves, upright_leaf, 0, unroll=4)
    upright(node_skel[0], leaves)
    upright(sub_skel[0], leaves + 1)

    def couple(step, carry):
        terms = []
        for each in range(AT_ONCE):
            item = step * AT_ONCE + each
            packs = jnp.where(left, twice[srcs[2 * item]], twice[srcs[2 * item + 1]])
            target = dsts[item]
            diff_x = cols[target, 0] - packs[nvec : nvec + 1]
            diff_y = cols[target, 1] - packs[nvec + 1 : nvec + 2]
            square = (diff_x * diff_x + diff_y * diff_y) * tables[0]
            arg = square * lax.rsqrt(TINY - square)
            value = tables[5]
            for power in (4, 3, 2, 1):
                value = value * arg + tables[power]
            value = value * jnp.exp2(arg)
            terms.append((target, product(packs[:nvec], value, True)))
        for target, total in terms:
            coef[target] += total
        return carry

    lax.fori_loop(0, (ends + AT_ONCE - 1) // AT_ONCE, couple, 0)
    for copy in copies[6:]:
        copy.wait()
    down_node = coef[leaves] + product(coef[leaves + 1], node_maps[0], True)
    for leaf in range(leaves):
        down_leaf = coef[leaf] + product(down_node, leaf_maps[leaf], True)
        whole = near[leaf] + product(down_leaf, bases[leaf])
        for each in range(block // WIDE):
            fill(
                source,
                whole[:, each * WIDE : (each + 1) * WIDE],
                (leaf * (block // WIDE) + each) * nvec,
                nvec,
            )

    def scatter(each, carry):
        at = pl.multiple_of(each * block, block)
        out[:, pl.ds(at, block)] = pick(rows, source, leaf_index(inverse, each, block), nvec)
        return carry

    steps = inverse.shape[0] * WIDE // block
    segments = 4
    leaving = []
    for each in range(segments):
        start, stop = each * steps // segments, (each + 1) * steps // segments
        lax.fori_loop(start, stop, scatter, 0, unroll=2)
        span = slice(start * block, stop * block)
        leaving.append(pltpu.make_async_copy(out.at[:, span], out_at.at[:, span], sems.at[each]))
        leaving[-1].start()
    for copy in leaving:
        copy.wait()


def skeleton_tables(rank):
    scale, poly = make_tables(1.0 / math.sqrt(rank))
    var = np.arange(rank) % 3
    rows, cols = var[:, None], np.tile(var, 2)[None, :]
    return np.stack([scale[rows, cols]] + [poly[power][rows, cols] for power in range(5)]).astype(
        np.float32
    )


def shards(
    vectors,
    coords,
    perm,
    bases,
    leaf_maps,
    node_maps,
    leaf_skel,
    node_skel,
    sub_skel,
    leaf_src,
    leaf_count,
    node_src,
    node_count,
):
    nvec, rows_dev = vectors.shape
    leaves, rank, block = bases.shape
    groups = lax.axis_size("grp")
    subtrees = lax.axis_size("leaf")
    nodes = groups * subtrees
    sub_pos = lax.axis_index("leaf")
    device_pos = sub_pos * groups + lax.axis_index("grp")
    chunks = rows_dev // WIDE
    vmem = pl.BlockSpec(memory_space=pltpu.VMEM)
    smem = pl.BlockSpec(memory_space=pltpu.SMEM)
    hbm = pl.BlockSpec(memory_space=pltpu.HBM)
    anywhere = pl.BlockSpec(memory_space=pl.ANY)
    params = pltpu.CompilerParams(vmem_limit_bytes=60 * 1024 * 1024)
    order = perm.reshape(rows_dev // 128, 128)

    def like(*arrays):
        return [pltpu.VMEM(each.shape, each.dtype) for each in arrays]

    given = (vectors, order, bases, leaf_maps, node_maps, leaf_skel, node_skel, sub_skel)
    tree_vec, leaf_pack, tree_pack = pl.pallas_call(
        up_kernel,
        out_shape=(
            jax.ShapeDtypeStruct((leaves, nvec, block), F32),
            jax.ShapeDtypeStruct((leaves // 2, PACK_ROWS, 2 * rank), F32),
            jax.ShapeDtypeStruct((nodes, PACK_ROWS, 2 * rank), F32),
        ),
        in_specs=[hbm] * 8,
        out_specs=(hbm, vmem, vmem),
        scratch_shapes=like(*given)
        + [
            pltpu.VMEM((leaves, nvec, block), F32),
            pltpu.VMEM((chunks * nvec, 2 * WIDE), BF16),
            pltpu.VMEM((WIDE, block), jnp.int16),
            pltpu.SemaphoreType.DMA((9,)),
        ],
        compiler_params=params,
        name="up",
    )(*given)
    tree_all = lax.all_to_all(tree_pack, ("leaf", "grp"), 0, 0, tiled=True)
    leaf_all = [leaf_pack] + [
        lax.ppermute(leaf_pack, "grp", [(each, (each + shift) % groups) for each in range(groups)])
        for shift in range(1, groups)
    ]
    shift = (device_pos * (rows_dev % 3) % 3).astype(jnp.int32).reshape(1)
    near, inverse = pl.pallas_call(
        near_kernel,
        out_shape=(
            jax.ShapeDtypeStruct((leaves, nvec, block), F32),
            jax.ShapeDtypeStruct((chunks, WIDE), jnp.int32),
        ),
        in_specs=[smem, hbm, hbm, hbm],
        out_specs=(hbm,) * 2,
        scratch_shapes=like(coords, order, tree_vec)
        + [
            pltpu.VMEM((leaves, nvec, block), F32),
            pltpu.VMEM((chunks, WIDE), jnp.int32),
            pltpu.VMEM((2 * chunks, WIDE), F32),
            pltpu.VMEM((6 * chunks, WIDE), BF16),
            pltpu.VMEM((WIDE, block), jnp.int16),
            pltpu.VMEM((leaves, 3, 8, block), F32),
            pltpu.VMEM((leaves, 3, block // 8, 8, 128), F32),
            pltpu.VMEM((2 * chunks, WIDE), F32),
            *[pltpu.VMEM((block, block), BF16)] * 4,
            pltpu.SemaphoreType.DMA((4,)),
        ],
        compiler_params=params,
        cost_estimate=pl.CostEstimate(
            flops=128 * leaves * block * block,
            bytes_accessed=8 * leaves * nvec * block,
            transcendentals=leaves * block * block,
        ),
        name="near",
    )(shift, coords, order, tree_vec)
    tables = jnp.asarray(skeleton_tables(rank))
    given = (tree_all, leaf_skel, node_skel, sub_skel, tables)
    given = given + (leaf_maps, node_maps, bases, near, inverse)
    items = (leaf_src.size + node_src.size + subtrees + 2) // 2 + AT_ONCE
    sources = groups * leaves + 3 * groups + subtrees + 1
    return pl.pallas_call(
        functools.partial(far_kernel, groups, subtrees),
        out_shape=jax.ShapeDtypeStruct((nvec, rows_dev), F32),
        in_specs=[smem] * 5 + [anywhere] * (groups + 1) + [hbm] * 9,
        out_specs=hbm,
        scratch_shapes=like(*given)
        + [
            pltpu.VMEM((groups * leaf_pack.shape[0],) + leaf_pack.shape[1:], F32),
            pltpu.VMEM((chunks * nvec, 2 * WIDE), BF16),
            pltpu.VMEM((leaves + 2, nvec, rank), F32),
            pltpu.VMEM((sources, PACK_ROWS, 2 * rank), F32),
            pltpu.VMEM((leaves + 2, 2, rank, 2 * rank), F32),
            pltpu.VMEM((nvec, rows_dev), F32),
            pltpu.VMEM((WIDE, block), jnp.int16),
            pltpu.SMEM((2 * items,), jnp.int32),
            pltpu.SMEM((items,), jnp.int32),
            pltpu.SemaphoreType.DMA((10 + groups,)),
        ],
        compiler_params=params,
        name="far",
    )(
        jnp.stack([sub_pos, lax.axis_index("grp")]).astype(jnp.int32),
        leaf_src,
        leaf_count,
        node_src,
        node_count,
        *leaf_all,
        *given,
    )


def solution(mesh):
    placed = (
        P(None, ("leaf", "grp")),
        P(None, ("leaf", "grp")),
        P(("leaf", "grp")),
        P(("leaf", "grp"), None, None),
        P(("leaf", "grp"), None, None),
        P(("leaf", "grp"), None, None),
        P(("leaf", "grp"), None, None),
        P(("leaf", "grp"), None, None),
        P("leaf", None, None),
        P(("leaf", "grp"), None),
        P(("leaf", "grp")),
        P(("leaf", "grp"), None),
        P(("leaf", "grp")),
    )
    return jax.shard_map(
        shards, mesh=mesh, in_specs=placed, out_specs=P(None, ("leaf", "grp")), check_vma=False
    )
```

```python
import functools
import math

import jax
import jax.numpy as jnp
import numpy as np
from jax import lax
from jax.experimental import pallas as pl
from jax.experimental.pallas import tpu as pltpu
from jax.sharding import PartitionSpec as P

F32 = jnp.float32
BF16 = jnp.bfloat16
WIDE = 128
SHIFT = 7
LOG2E = math.log2(math.e)
TINY = 1e-37
PACK_ROWS = 24
PART = 32
AT_ONCE = 8


def make_tables(norm):
    smooth = [0, 2, 4]
    sigmas = [1.0, 0.8, 1.2]
    rho = [[1.0, 0.5, 0.3], [0.5, 1.0, 0.4], [0.3, 0.4, 1.0]]
    scale = np.zeros((3, 3))
    poly = np.zeros((5, 3, 3))
    for first in range(3):
        for second in range(3):
            order = (smooth[first] + smooth[second]) // 2
            scale[first, second] = -(2.0 * order + 1.0) * (LOG2E / 0.3) ** 2
            amp = sigmas[first] * sigmas[second] * rho[first][second] * norm
            for power in range(order + 1):
                kterm = order - power
                coeff = math.factorial(order) / math.factorial(2 * order)
                coeff = (
                    coeff
                    * math.factorial(order + kterm)
                    / (math.factorial(kterm) * math.factorial(order - kterm))
                )
                poly[power, first, second] = amp * coeff * 2.0**power * (-1.0 / LOG2E) ** power
    return scale, poly


def dot(one, two, turned=False):
    dims = (((1,), (1 if turned else 0,)), ((), ()))
    return lax.dot_general(one, two, dims, preferred_element_type=F32)


def parts(value):
    high = value.astype(BF16)
    return high, (value - high.astype(F32)).astype(BF16)


def product(one, two, turned=False):
    rows = one.shape[0]
    one_hi, one_lo = parts(one)
    two_hi, two_lo = parts(two)
    both = dot(jnp.concatenate([one_hi, one_lo], axis=0), two_hi, turned)
    return both[:rows] + both[rows:] + dot(one_hi, two_lo, turned)


def count_rows(rows):
    rows[...] = lax.broadcasted_iota(jnp.int32, rows.shape, 0).astype(jnp.int16)


def one_hot(rows, low):
    count = low.shape[1]
    low = jnp.broadcast_to(low, (16, count)).astype(jnp.int16)[None]
    same = rows[:, :count].reshape(WIDE // 16, 16, count) == low
    return jnp.where(same, jnp.bfloat16(1), jnp.bfloat16(0)).reshape(WIDE, count)


def fill(source, value, at, nvec):
    high, low = parts(value)
    source[pl.ds(at, nvec), :WIDE] = high
    source[pl.ds(at, nvec), WIDE:] = low


def pick(rows, source, index, nvec):
    count = index.shape[1]
    hot = one_hot(rows, index & (WIDE - 1))
    hot = jnp.concatenate([hot, hot], axis=0)
    chunk = jnp.broadcast_to(index >> SHIFT, (8, count))[None]
    out = jnp.zeros((nvec // 8, 8, count), F32)
    chunks = source.shape[0] // nvec
    found = dot(source[...], hot).reshape(chunks, nvec // 8, 8, count)
    for each in range(chunks):
        out = jnp.where(chunk == each, found[each], out)
    return out.reshape(nvec, count)


def leaf_index(perm, leaf, block):
    rows = block // 128
    return jnp.concatenate([perm[pl.ds(leaf * rows + each, 1), :] for each in range(rows)], axis=1)


def fetch(pairs, sems):
    copies = [pltpu.make_async_copy(src, dst, sems.at[each]) for each, (src, dst) in enumerate(pairs)]
    for copy in copies:
        copy.start()
    return copies


def up_kernel(*refs):
    given, (tree_out, leaf_pack, tree_pack) = refs[:8], refs[8:11]
    held = refs[11:19]
    tree_vec, source, rows, sems = refs[19:]
    count_rows(rows)
    copies = fetch(list(zip(given, held)), sems)
    vec, perm, bases, leaf_maps, node_maps, leaf_skel, node_skel, sub_skel = held
    leaves, nvec, block = tree_vec.shape
    rank = bases.shape[1]
    copies[0].wait()
    for each in range(vec.shape[1] // WIDE):
        fill(source, vec[:, each * WIDE : (each + 1) * WIDE], each * nvec, nvec)
    copies[1].wait()

    def gather(leaf, carry):
        tree_vec[leaf] = pick(rows, source, leaf_index(perm, leaf, block), nvec)
        return carry

    lax.fori_loop(0, leaves, gather, 0, unroll=2)
    leave = pltpu.make_async_copy(tree_vec, tree_out, sems.at[len(copies)])
    leave.start()
    for copy in copies[2:]:
        copy.wait()
    up_node = jnp.zeros((nvec, rank), F32)
    blank = jnp.zeros((PACK_ROWS - nvec - 2, 2 * rank), F32)
    for leaf in range(0, leaves, 2):
        up = [product(tree_vec[leaf + each], bases[leaf + each], True) for each in range(2)]
        leaf_pack[leaf // 2] = jnp.concatenate(
            [
                jnp.concatenate(up, axis=1),
                jnp.concatenate([leaf_skel[leaf], leaf_skel[leaf + 1]], axis=1),
                blank,
            ],
            axis=0,
        )
        for each in range(2):
            up_node = up_node + product(up[each], leaf_maps[leaf + each])
    up_sub = product(up_node, node_maps[0])
    packed = jnp.concatenate(
        [
            jnp.concatenate([up_node, up_sub], axis=1),
            jnp.concatenate([node_skel[0], sub_skel[0]], axis=1),
            blank,
        ],
        axis=0,
    )

    def spread(each, carry):
        tree_pack[each] = packed
        return carry

    lax.fori_loop(0, tree_pack.shape[0], spread, 0)
    leave.wait()


def near_kernel(shift, *refs):
    given, (near_out, inverse_out) = refs[:3], refs[3:5]
    held = refs[5:8]
    near, inverse, flat, source, rows, across, down, slots = refs[8:16]
    sooner, later, sems = refs[16:18], refs[18:20], refs[20]
    copies = fetch(list(zip(given, held)), sems)
    crd, perm, tree_vec = held
    count_rows(rows)
    leaves, nvec, block = tree_vec.shape
    chunks = crd.shape[1] // WIDE
    scale, poly = make_tables(1.0 / math.sqrt(block))
    slope = scale[0, 1] - scale[0, 0]
    copies[0].wait()
    for axis in range(2):
        for each in range(chunks):
            row = axis * chunks + each
            flat[row : row + 1, :] = crd[axis : axis + 1, each * WIDE : (each + 1) * WIDE]
    rest = flat[...]
    for piece in range(3):
        rounded = rest.astype(BF16)
        source[piece * 2 * chunks : (piece + 1) * 2 * chunks, :] = rounded
        rest = rest - rounded.astype(F32)
    slots[...] = jnp.zeros_like(slots)
    copies[1].wait()
    side = 128
    tiles = block // side

    def place_leaf(leaf, carry):
        index = leaf_index(perm, leaf, block)
        hot = one_hot(rows, index & (WIDE - 1))
        found = dot(source[...], hot)
        found = (
            found[: 2 * chunks] + found[2 * chunks : 4 * chunks] + found[4 * chunks :]
        )
        mine = lax.broadcasted_iota(jnp.int32, (chunks, block), 0) == index >> SHIFT
        lane = lax.broadcasted_iota(jnp.int32, (chunks, block), 1) + leaf * block
        lane_low = (lane & (WIDE - 1)).astype(F32)
        lane_high = (lane >> SHIFT).astype(F32)
        marks = jnp.concatenate(
            [jnp.where(mine, lane_low, 0.0), jnp.where(mine, lane_high, 0.0)], axis=0
        ).astype(BF16)
        slots[...] += dot(marks, hot, True)
        row_x = jnp.sum(jnp.where(mine, found[:chunks], 0.0), axis=0, keepdims=True)
        row_y = jnp.sum(jnp.where(mine, found[chunks:], 0.0), axis=0, keepdims=True)
        moved = index + shift[0]
        kind = moved - 3 * ((moved * 43691) >> 17)
        row_w = kind.astype(F32) * slope
        for place, row in enumerate((row_x, row_y, row_w)):
            across[leaf, place] = jnp.broadcast_to(row, (8, block))
            turned = jnp.transpose(jnp.broadcast_to(row, (side, block)))
            down[leaf, place] = turned.reshape(block // 8, 8, side)
        return carry

    lax.fori_loop(0, leaves, place_leaf, 0, unroll=2)
    inverse[...] = (slots[:chunks] + slots[chunks:] * WIDE).astype(jnp.int32)
    leave = pltpu.make_async_copy(inverse, inverse_out, sems.at[3])
    leave.start()
    copies[2].wait()

    def values(leaf, high, low):
        for col in range(tiles):
            cols = slice(col * side, (col + 1) * side)
            over_x, over_y, over_w = [across[leaf, each, :, cols] for each in range(3)]
            over_zero, over_one = over_w > 0.5 * slope, over_w > 1.5 * slope

            def across_table(power, first):
                zero, one, two = [float(each) for each in poly[power, first]]
                return jnp.where(over_zero, zero, jnp.where(over_one, one, two))[None]

            table = [[across_table(power, first) for first in range(3)] for power in range(5)]
            over_w = (over_w + float(scale[0, 0]))[None]
            over_x, over_y = over_x[None], over_y[None]
            for row in range(col + 1):
                pieces = []
                for part in range(side // PART):
                    first = row * side + part * PART
                    at = slice(first // 8, (first + PART) // 8)
                    diff_x = down[leaf, 0, at] - over_x
                    diff_y = down[leaf, 1, at] - over_y
                    down_w = down[leaf, 2, at]
                    var_zero, var_one = down_w > 0.5 * slope, down_w > 1.5 * slope
                    square = (diff_x * diff_x + diff_y * diff_y) * (down_w + over_w)
                    arg = square * lax.rsqrt(TINY - square)
                    value = jnp.where(var_one, 0.0, table[4][2])
                    value = value * arg + jnp.where(
                        var_zero, 0.0, jnp.where(var_one, table[3][1], table[3][2])
                    )
                    for power in (2, 1, 0):
                        a, b, c = table[power]
                        value = value * arg + jnp.where(var_zero, a, jnp.where(var_one, b, c))
                    pieces.append(parts((value * jnp.exp2(arg)).reshape(PART, side)))
                rows = slice(row * side, (row + 1) * side)
                for each, out in enumerate((high, low)):
                    tile = jnp.concatenate([piece[each] for piece in pieces], axis=0)
                    out[rows, cols] = tile
                    if row < col:
                        out[cols, rows] = jnp.transpose(tile)

    def apply(leaf, high, low):
        vec_hi, vec_lo = parts(tree_vec[leaf])
        both = dot(jnp.concatenate([vec_hi, vec_lo], axis=0), high[...])
        near[leaf] = both[:nvec] + both[nvec:] + dot(vec_hi, low[...])

    for each in later:
        each[...] = jnp.zeros_like(each)

    def two_leaves(step, carry):
        apply(jnp.maximum(2 * step - 1, 0), *later)
        values(2 * step, *sooner)
        apply(2 * step, *sooner)
        values(2 * step + 1, *later)
        return carry

    lax.fori_loop(0, leaves // 4, two_leaves, 0)
    half = slice(0, leaves // 2 - 1)
    first = pltpu.make_async_copy(near.at[half], near_out.at[half], sems.at[0])
    first.start()
    lax.fori_loop(leaves // 4, leaves // 2, two_leaves, 0)
    apply(leaves - 1, *later)
    half = slice(leaves // 2 - 1, leaves)
    second = pltpu.make_async_copy(near.at[half], near_out.at[half], sems.at[1])
    second.start()
    for copy in (leave, first, second):
        copy.wait()


def far_kernel(groups, subtrees, *refs):
    place, leaf_src, leaf_count, node_src, node_count = refs[:5]
    leaf_packs, refs = refs[5 : 5 + groups], refs[5 + groups :]
    given, out_at, held = refs[:10], refs[10], refs[11:21]
    leaf_all, source, coef, twice, cols, out, rows, srcs, dsts, sems = refs[21:]
    own = leaf_packs[0].shape[0]
    grp_pos = lax.rem(place[0], groups)
    owner = [lax.rem(grp_pos - shift + groups, groups) for shift in range(groups)]
    arrive = [leaf_all.at[pl.ds(each * own, own)] for each in owner]
    copies = fetch(list(zip(leaf_packs + given, arrive + list(held))), sems)
    leaf_copies, copies = copies[:groups], [None] + copies[groups:]
    tree_all, leaf_skel, node_skel, sub_skel, tables = held[:5]
    leaf_maps, node_maps, bases, near, inverse = held[5:]
    count_rows(rows)
    leaves, nvec, block = near.shape
    rank = bases.shape[1]
    nodes = tree_all.shape[0]
    pairs = leaf_all.shape[0]
    node_at = 2 * pairs
    beside = 3 * groups
    sub_at = node_at + beside
    blank = sub_at + subtrees
    sub_pos = lax.div(place[0], groups)
    left = lax.broadcasted_iota(jnp.int32, (PACK_ROWS, 2 * rank), 1) < rank

    def list_leaf(leaf, at):
        count = leaf_count[leaf]

        def one(step, carry):
            srcs[2 * (at + step)] = leaf_src[leaf, 2 * step]
            second = jnp.where(2 * step + 1 < count, leaf_src[leaf, 2 * step + 1], blank)
            srcs[2 * (at + step) + 1] = second
            dsts[at + step] = leaf
            return carry

        steps = (count + 1) // 2
        lax.fori_loop(0, steps, one, 0)
        return at + steps

    size = lax.fori_loop(0, leaves, list_leaf, 0)
    count = node_count[0]

    def list_node(step, carry):
        srcs[2 * (size + step)] = node_at + node_src[0, 2 * step]
        second = jnp.where(2 * step + 1 < count, node_at + node_src[0, 2 * step + 1], blank)
        srcs[2 * (size + step) + 1] = second
        dsts[size + step] = leaves
        return carry

    steps = (count + 1) // 2
    lax.fori_loop(0, steps, list_node, 0)

    def list_sub(sub, at):
        srcs[at] = sub_at + sub
        dsts[at // 2] = leaves + 1
        return at + jnp.where(jnp.abs(sub - sub_pos) >= 2, 1, 0)

    ends = lax.fori_loop(0, subtrees, list_sub, 2 * (size + steps))
    srcs[ends] = blank
    dsts[ends // 2] = leaves + 1
    ends = (ends + 1) // 2
    for each in range(AT_ONCE):
        srcs[2 * (ends + each)] = blank
        srcs[2 * (ends + each) + 1] = blank
        dsts[ends + each] = leaves + 1

    for copy in leaf_copies:
        copy.wait()

    def both_leaves(pair, carry):
        packs = leaf_all[pair]
        turned = pltpu.roll(packs, rank, 1)
        twice[2 * pair] = jnp.where(left, packs, turned)
        twice[2 * pair + 1] = jnp.where(left, turned, packs)
        return carry

    lax.fori_loop(0, pairs, both_leaves, 0, unroll=4)
    copies[1].wait()

    def both_node(each, carry):
        packs = tree_all[jnp.clip((sub_pos - 1) * groups + each, 0, nodes - 1)]
        twice[node_at + each] = jnp.where(left, packs, pltpu.roll(packs, rank, 1))
        return carry

    lax.fori_loop(0, beside, both_node, 0, unroll=4)

    def both_sub(sub, carry):
        total = tree_all[sub * groups, :nvec]
        for each in range(1, groups):
            total = total + tree_all[sub * groups + each, :nvec]
        packs = jnp.concatenate([total, tree_all[sub * groups, nvec:]], axis=0)
        twice[sub_at + sub] = jnp.where(left, pltpu.roll(packs, rank, 1), packs)
        return carry

    lax.fori_loop(0, subtrees, both_sub, 0, unroll=2)
    twice[blank] = jnp.zeros_like(twice[blank])
    coef[...] = jnp.zeros_like(coef)
    for copy in copies[2:6]:
        copy.wait()

    def upright(skel, at):
        for axis in range(2):
            row = jnp.broadcast_to(skel[axis : axis + 1], (2 * rank, rank))
            cols[at, axis] = jnp.transpose(row)

    def upright_leaf(leaf, carry):
        upright(leaf_skel[leaf], leaf)
        return carry

    lax.fori_loop(0, leaves, upright_leaf, 0, unroll=4)
    upright(node_skel[0], leaves)
    upright(sub_skel[0], leaves + 1)

    def couple(step, carry):
        terms = []
        for each in range(AT_ONCE):
            item = step * AT_ONCE + each
            packs = jnp.where(left, twice[srcs[2 * item]], twice[srcs[2 * item + 1]])
            target = dsts[item]
            diff_x = cols[target, 0] - packs[nvec : nvec + 1]
            diff_y = cols[target, 1] - packs[nvec + 1 : nvec + 2]
            square = (diff_x * diff_x + diff_y * diff_y) * tables[0]
            arg = square * lax.rsqrt(TINY - square)
            value = tables[5]
            for power in (4, 3, 2, 1):
                value = value * arg + tables[power]
            value = value * jnp.exp2(arg)
            terms.append((target, product(packs[:nvec], value, True)))
        for target, total in terms:
            coef[target] += total
        return carry

    lax.fori_loop(0, (ends + AT_ONCE - 1) // AT_ONCE, couple, 0)
    for copy in copies[6:]:
        copy.wait()
    down_node = coef[leaves] + product(coef[leaves + 1], node_maps[0], True)
    for leaf in range(leaves):
        down_leaf = coef[leaf] + product(down_node, leaf_maps[leaf], True)
        whole = near[leaf] + product(down_leaf, bases[leaf])
        for each in range(block // WIDE):
            fill(
                source,
                whole[:, each * WIDE : (each + 1) * WIDE],
                (leaf * (block // WIDE) + each) * nvec,
                nvec,
            )

    def scatter(each, carry):
        at = pl.multiple_of(each * block, block)
        out[:, pl.ds(at, block)] = pick(rows, source, leaf_index(inverse, each, block), nvec)
        return carry

    steps = inverse.shape[0] * WIDE // block
    segments = 4
    leaving = []
    for each in range(segments):
        start, stop = each * steps // segments, (each + 1) * steps // segments
        lax.fori_loop(start, stop, scatter, 0, unroll=2)
        span = slice(start * block, stop * block)
        leaving.append(pltpu.make_async_copy(out.at[:, span], out_at.at[:, span], sems.at[each]))
        leaving[-1].start()
    for copy in leaving:
        copy.wait()


def skeleton_tables(rank):
    scale, poly = make_tables(1.0 / math.sqrt(rank))
    var = np.arange(rank) % 3
    rows, cols = var[:, None], np.tile(var, 2)[None, :]
    return np.stack([scale[rows, cols]] + [poly[power][rows, cols] for power in range(5)]).astype(
        np.float32
    )


def shards(
    vectors,
    coords,
    perm,
    bases,
    leaf_maps,
    node_maps,
    leaf_skel,
    node_skel,
    sub_skel,
    leaf_src,
    leaf_count,
    node_src,
    node_count,
):
    nvec, rows_dev = vectors.shape
    leaves, rank, block = bases.shape
    groups = lax.axis_size("grp")
    subtrees = lax.axis_size("leaf")
    nodes = groups * subtrees
    sub_pos = lax.axis_index("leaf")
    device_pos = sub_pos * groups + lax.axis_index("grp")
    chunks = rows_dev // WIDE
    vmem = pl.BlockSpec(memory_space=pltpu.VMEM)
    smem = pl.BlockSpec(memory_space=pltpu.SMEM)
    hbm = pl.BlockSpec(memory_space=pltpu.HBM)
    anywhere = pl.BlockSpec(memory_space=pl.ANY)
    params = pltpu.CompilerParams(vmem_limit_bytes=60 * 1024 * 1024)
    order = perm.reshape(rows_dev // 128, 128)

    def like(*arrays):
        return [pltpu.VMEM(each.shape, each.dtype) for each in arrays]

    given = (vectors, order, bases, leaf_maps, node_maps, leaf_skel, node_skel, sub_skel)
    tree_vec, leaf_pack, tree_pack = pl.pallas_call(
        up_kernel,
        out_shape=(
            jax.ShapeDtypeStruct((leaves, nvec, block), F32),
            jax.ShapeDtypeStruct((leaves // 2, PACK_ROWS, 2 * rank), F32),
            jax.ShapeDtypeStruct((nodes, PACK_ROWS, 2 * rank), F32),
        ),
        in_specs=[hbm] * 8,
        out_specs=(hbm, vmem, vmem),
        scratch_shapes=like(*given)
        + [
            pltpu.VMEM((leaves, nvec, block), F32),
            pltpu.VMEM((chunks * nvec, 2 * WIDE), BF16),
            pltpu.VMEM((WIDE, block), jnp.int16),
            pltpu.SemaphoreType.DMA((9,)),
        ],
        compiler_params=params,
        name="up",
    )(*given)
    tree_all = lax.all_to_all(tree_pack, ("leaf", "grp"), 0, 0, tiled=True)
    leaf_all = [leaf_pack] + [
        lax.ppermute(leaf_pack, "grp", [(each, (each + shift) % groups) for each in range(groups)])
        for shift in range(1, groups)
    ]
    shift = (device_pos * (rows_dev % 3) % 3).astype(jnp.int32).reshape(1)
    near, inverse = pl.pallas_call(
        near_kernel,
        out_shape=(
            jax.ShapeDtypeStruct((leaves, nvec, block), F32),
            jax.ShapeDtypeStruct((chunks, WIDE), jnp.int32),
        ),
        in_specs=[smem, hbm, hbm, hbm],
        out_specs=(hbm,) * 2,
        scratch_shapes=like(coords, order, tree_vec)
        + [
            pltpu.VMEM((leaves, nvec, block), F32),
            pltpu.VMEM((chunks, WIDE), jnp.int32),
            pltpu.VMEM((2 * chunks, WIDE), F32),
            pltpu.VMEM((6 * chunks, WIDE), BF16),
            pltpu.VMEM((WIDE, block), jnp.int16),
            pltpu.VMEM((leaves, 3, 8, block), F32),
            pltpu.VMEM((leaves, 3, block // 8, 8, 128), F32),
            pltpu.VMEM((2 * chunks, WIDE), F32),
            *[pltpu.VMEM((block, block), BF16)] * 4,
            pltpu.SemaphoreType.DMA((4,)),
        ],
        compiler_params=params,
        cost_estimate=pl.CostEstimate(
            flops=128 * leaves * block * block,
            bytes_accessed=8 * leaves * nvec * block,
            transcendentals=leaves * block * block,
        ),
        name="near",
    )(shift, coords, order, tree_vec)
    tables = jnp.asarray(skeleton_tables(rank))
    given = (tree_all, leaf_skel, node_skel, sub_skel, tables)
    given = given + (leaf_maps, node_maps, bases, near, inverse)
    items = (leaf_src.size + node_src.size + subtrees + 2) // 2 + AT_ONCE
    sources = groups * leaves + 3 * groups + subtrees + 1
    return pl.pallas_call(
        functools.partial(far_kernel, groups, subtrees),
        out_shape=jax.ShapeDtypeStruct((nvec, rows_dev), F32),
        in_specs=[smem] * 5 + [anywhere] * (groups + 1) + [hbm] * 9,
        out_specs=hbm,
        scratch_shapes=like(*given)
        + [
            pltpu.VMEM((groups * leaf_pack.shape[0],) + leaf_pack.shape[1:], F32),
            pltpu.VMEM((chunks * nvec, 2 * WIDE), BF16),
            pltpu.VMEM((leaves + 2, nvec, rank), F32),
            pltpu.VMEM((sources, PACK_ROWS, 2 * rank), F32),
            pltpu.VMEM((leaves + 2, 2, rank, 2 * rank), F32),
            pltpu.VMEM((nvec, rows_dev), F32),
            pltpu.VMEM((WIDE, block), jnp.int16),
            pltpu.SMEM((2 * items,), jnp.int32),
            pltpu.SMEM((items,), jnp.int32),
            pltpu.SemaphoreType.DMA((10 + groups,)),
        ],
        compiler_params=params,
        name="far",
    )(
        device_pos.astype(jnp.int32).reshape(1),
        leaf_src,
        leaf_count,
        node_src,
        node_count,
        *leaf_all,
        *given,
    )


def solution(mesh):
    placed = (
        P(None, ("leaf", "grp")),
        P(None, ("leaf", "grp")),
        P(("leaf", "grp")),
        P(("leaf", "grp"), None, None),
        P(("leaf", "grp"), None, None),
        P(("leaf", "grp"), None, None),
        P(("leaf", "grp"), None, None),
        P(("leaf", "grp"), None, None),
        P("leaf", None, None),
        P(("leaf", "grp"), None),
        P(("leaf", "grp")),
        P(("leaf", "grp"), None),
        P(("leaf", "grp")),
    )
    return jax.shard_map(
        shards, mesh=mesh, in_specs=placed, out_specs=P(None, ("leaf", "grp")), check_vma=False
    )
```

```python
import functools
import math

import jax
import jax.numpy as jnp
import numpy as np
from jax import lax
from jax.experimental import pallas as pl
from jax.experimental.pallas import tpu as pltpu
from jax.sharding import PartitionSpec as P

F32 = jnp.float32
BF16 = jnp.bfloat16
WIDE = 128
SHIFT = 7
LOG2E = math.log2(math.e)
TINY = 1e-37
PACK_ROWS = 24
PART = 32
AT_ONCE = 8


def make_tables(norm):
    smooth = [0, 2, 4]
    sigmas = [1.0, 0.8, 1.2]
    rho = [[1.0, 0.5, 0.3], [0.5, 1.0, 0.4], [0.3, 0.4, 1.0]]
    scale = np.zeros((3, 3))
    poly = np.zeros((5, 3, 3))
    for first in range(3):
        for second in range(3):
            order = (smooth[first] + smooth[second]) // 2
            scale[first, second] = -(2.0 * order + 1.0) * (LOG2E / 0.3) ** 2
            amp = sigmas[first] * sigmas[second] * rho[first][second] * norm
            for power in range(order + 1):
                kterm = order - power
                coeff = math.factorial(order) / math.factorial(2 * order)
                coeff = (
                    coeff
                    * math.factorial(order + kterm)
                    / (math.factorial(kterm) * math.factorial(order - kterm))
                )
                poly[power, first, second] = amp * coeff * 2.0**power * (-1.0 / LOG2E) ** power
    return scale, poly


def dot(one, two, turned=False):
    dims = (((1,), (1 if turned else 0,)), ((), ()))
    return lax.dot_general(one, two, dims, preferred_element_type=F32)


def parts(value):
    high = value.astype(BF16)
    return high, (value - high.astype(F32)).astype(BF16)


def product(one, two, turned=False):
    rows = one.shape[0]
    one_hi, one_lo = parts(one)
    two_hi, two_lo = parts(two)
    both = dot(jnp.concatenate([one_hi, one_lo], axis=0), two_hi, turned)
    return both[:rows] + both[rows:] + dot(one_hi, two_lo, turned)


def count_rows(rows):
    rows[...] = lax.broadcasted_iota(jnp.int32, rows.shape, 0).astype(jnp.int16)


def one_hot(rows, low):
    count = low.shape[1]
    low = jnp.broadcast_to(low, (16, count)).astype(jnp.int16)[None]
    same = rows[:, :count].reshape(WIDE // 16, 16, count) == low
    return jnp.where(same, jnp.bfloat16(1), jnp.bfloat16(0)).reshape(WIDE, count)


def fill(source, value, at, nvec):
    high, low = parts(value)
    source[pl.ds(at, nvec), :WIDE] = high
    source[pl.ds(at, nvec), WIDE:] = low


def pick(rows, source, index, nvec):
    count = index.shape[1]
    hot = one_hot(rows, index & (WIDE - 1))
    hot = jnp.concatenate([hot, hot], axis=0)
    chunk = jnp.broadcast_to(index >> SHIFT, (8, count))[None]
    out = jnp.zeros((nvec // 8, 8, count), F32)
    chunks = source.shape[0] // nvec
    found = dot(source[...], hot).reshape(chunks, nvec // 8, 8, count)
    for each in range(chunks):
        out = jnp.where(chunk == each, found[each], out)
    return out.reshape(nvec, count)


def leaf_index(perm, leaf, block):
    rows = block // 128
    return jnp.concatenate([perm[pl.ds(leaf * rows + each, 1), :] for each in range(rows)], axis=1)


def fetch(pairs, sems):
    copies = [pltpu.make_async_copy(src, dst, sems.at[each]) for each, (src, dst) in enumerate(pairs)]
    for copy in copies:
        copy.start()
    return copies


def up_kernel(*refs):
    given, (tree_out, leaf_pack, tree_pack) = refs[:8], refs[8:11]
    held = refs[11:19]
    tree_vec, source, rows, sems = refs[19:]
    count_rows(rows)
    copies = fetch(list(zip(given, held)), sems)
    vec, perm, bases, leaf_maps, node_maps, leaf_skel, node_skel, sub_skel = held
    leaves, nvec, block = tree_vec.shape
    rank = bases.shape[1]
    copies[0].wait()
    for each in range(vec.shape[1] // WIDE):
        fill(source, vec[:, each * WIDE : (each + 1) * WIDE], each * nvec, nvec)
    copies[1].wait()

    def gather(leaf, carry):
        tree_vec[leaf] = pick(rows, source, leaf_index(perm, leaf, block), nvec)
        return carry

    lax.fori_loop(0, leaves, gather, 0, unroll=2)
    leave = pltpu.make_async_copy(tree_vec, tree_out, sems.at[len(copies)])
    leave.start()
    for copy in copies[2:]:
        copy.wait()
    up_node = jnp.zeros((nvec, rank), F32)
    blank = jnp.zeros((PACK_ROWS - nvec - 2, 2 * rank), F32)
    for leaf in range(0, leaves, 2):
        up = [product(tree_vec[leaf + each], bases[leaf + each], True) for each in range(2)]
        leaf_pack[leaf // 2] = jnp.concatenate(
            [
                jnp.concatenate(up, axis=1),
                jnp.concatenate([leaf_skel[leaf], leaf_skel[leaf + 1]], axis=1),
                blank,
            ],
            axis=0,
        )
        for each in range(2):
            up_node = up_node + product(up[each], leaf_maps[leaf + each])
    up_sub = product(up_node, node_maps[0])
    packed = jnp.concatenate(
        [
            jnp.concatenate([up_node, up_sub], axis=1),
            jnp.concatenate([node_skel[0], sub_skel[0]], axis=1),
            blank,
        ],
        axis=0,
    )

    def spread(each, carry):
        tree_pack[each] = packed
        return carry

    lax.fori_loop(0, tree_pack.shape[0], spread, 0)
    leave.wait()


def near_kernel(shift, *refs):
    given, (near_out, inverse_out) = refs[:3], refs[3:5]
    held = refs[5:8]
    near, inverse, flat, source, rows, slots = refs[8:14]
    even, odd, sooner, later, sems = refs[14:16], refs[16:18], refs[18:20], refs[20:22], refs[22]
    copies = fetch(list(zip(given, held)), sems)
    crd, perm, tree_vec = held
    count_rows(rows)
    leaves, nvec, block = tree_vec.shape
    chunks = crd.shape[1] // WIDE
    scale, poly = make_tables(1.0 / math.sqrt(block))
    slope = scale[0, 1] - scale[0, 0]
    copies[0].wait()
    for axis in range(2):
        for each in range(chunks):
            row = axis * chunks + each
            flat[row : row + 1, :] = crd[axis : axis + 1, each * WIDE : (each + 1) * WIDE]
    rest = flat[...]
    for piece in range(3):
        rounded = rest.astype(BF16)
        source[piece * 2 * chunks : (piece + 1) * 2 * chunks, :] = rounded
        rest = rest - rounded.astype(F32)
    slots[...] = jnp.zeros_like(slots)
    copies[1].wait()
    side = 128
    tiles = block // side

    def place_leaf(leaf, across, down):
        live = jnp.where(leaf < leaves, 1.0, 0.0)
        leaf = jnp.minimum(leaf, leaves - 1)
        index = leaf_index(perm, leaf, block)
        hot = one_hot(rows, index & (WIDE - 1))
        found = dot(source[...], hot)
        found = (
            found[: 2 * chunks] + found[2 * chunks : 4 * chunks] + found[4 * chunks :]
        )
        mine = lax.broadcasted_iota(jnp.int32, (chunks, block), 0) == index >> SHIFT
        lane = lax.broadcasted_iota(jnp.int32, (chunks, block), 1) + leaf * block
        lane_low = (lane & (WIDE - 1)).astype(F32) * live
        lane_high = (lane >> SHIFT).astype(F32) * live
        marks = jnp.concatenate(
            [jnp.where(mine, lane_low, 0.0), jnp.where(mine, lane_high, 0.0)], axis=0
        ).astype(BF16)
        slots[...] += dot(marks, hot, True)
        row_x = jnp.sum(jnp.where(mine, found[:chunks], 0.0), axis=0, keepdims=True)
        row_y = jnp.sum(jnp.where(mine, found[chunks:], 0.0), axis=0, keepdims=True)
        moved = index + shift[0]
        kind = moved - 3 * ((moved * 43691) >> 17)
        row_w = kind.astype(F32) * slope
        for place, row in enumerate((row_x, row_y, row_w)):
            across[place] = jnp.broadcast_to(row, (8, block))
            turned = jnp.transpose(jnp.broadcast_to(row, (side, block)))
            down[place] = turned.reshape(block // 8, 8, side)

    copies[2].wait()

    def values(across, down, high, low):
        for col in range(tiles):
            cols = slice(col * side, (col + 1) * side)
            over_x, over_y, over_w = [across[each, :, cols] for each in range(3)]
            over_zero, over_one = over_w > 0.5 * slope, over_w > 1.5 * slope

            def across_table(power, first):
                zero, one, two = [float(each) for each in poly[power, first]]
                return jnp.where(over_zero, zero, jnp.where(over_one, one, two))[None]

            table = [[across_table(power, first) for first in range(3)] for power in range(5)]
            over_w = (over_w + float(scale[0, 0]))[None]
            over_x, over_y = over_x[None], over_y[None]
            for row in range(col + 1):
                pieces = []
                for part in range(side // PART):
                    first = row * side + part * PART
                    at = slice(first // 8, (first + PART) // 8)
                    diff_x = down[0, at] - over_x
                    diff_y = down[1, at] - over_y
                    down_w = down[2, at]
                    var_zero, var_one = down_w > 0.5 * slope, down_w > 1.5 * slope
                    square = (diff_x * diff_x + diff_y * diff_y) * (down_w + over_w)
                    arg = square * lax.rsqrt(TINY - square)
                    value = jnp.where(var_one, 0.0, table[4][2])
                    value = value * arg + jnp.where(
                        var_zero, 0.0, jnp.where(var_one, table[3][1], table[3][2])
                    )
                    for power in (2, 1, 0):
                        a, b, c = table[power]
                        value = value * arg + jnp.where(var_zero, a, jnp.where(var_one, b, c))
                    pieces.append(parts((value * jnp.exp2(arg)).reshape(PART, side)))
                rows = slice(row * side, (row + 1) * side)
                for each, out in enumerate((high, low)):
                    tile = jnp.concatenate([piece[each] for piece in pieces], axis=0)
                    out[rows, cols] = tile
                    if row < col:
                        out[cols, rows] = jnp.transpose(tile)

    def apply(leaf, high, low):
        vec_hi, vec_lo = parts(tree_vec[leaf])
        both = dot(jnp.concatenate([vec_hi, vec_lo], axis=0), high[...])
        near[leaf] = both[:nvec] + both[nvec:] + dot(vec_hi, low[...])

    for each in later:
        each[...] = jnp.zeros_like(each)

    def two_leaves(step, carry):
        apply(jnp.maximum(2 * step - 1, 0), *later)
        values(*even, *sooner)
        place_leaf(2 * step + 1, *odd)
        apply(2 * step, *sooner)
        values(*odd, *later)
        place_leaf(2 * step + 2, *even)
        return carry

    place_leaf(0, *even)

    lax.fori_loop(0, leaves // 4, two_leaves, 0)
    half = slice(0, leaves // 2 - 1)
    first = pltpu.make_async_copy(near.at[half], near_out.at[half], sems.at[0])
    first.start()
    lax.fori_loop(leaves // 4, leaves // 2, two_leaves, 0)
    inverse[...] = (slots[:chunks] + slots[chunks:] * WIDE).astype(jnp.int32)
    leave = pltpu.make_async_copy(inverse, inverse_out, sems.at[3])
    leave.start()
    apply(leaves - 1, *later)
    half = slice(leaves // 2 - 1, leaves)
    second = pltpu.make_async_copy(near.at[half], near_out.at[half], sems.at[1])
    second.start()
    for copy in (leave, first, second):
        copy.wait()


def far_kernel(groups, subtrees, *refs):
    place, leaf_src, leaf_count, node_src, node_count = refs[:5]
    leaf_packs, refs = refs[5 : 5 + groups], refs[5 + groups :]
    given, out_at, held = refs[:10], refs[10], refs[11:21]
    leaf_all, source, coef, twice, cols, out, rows, srcs, dsts, sems = refs[21:]
    own = leaf_packs[0].shape[0]
    grp_pos = lax.rem(place[0], groups)
    owner = [lax.rem(grp_pos - shift + groups, groups) for shift in range(groups)]
    arrive = [leaf_all.at[pl.ds(each * own, own)] for each in owner]
    copies = fetch(list(zip(leaf_packs + given, arrive + list(held))), sems)
    leaf_copies, copies = copies[:groups], [None] + copies[groups:]
    tree_all, leaf_skel, node_skel, sub_skel, tables = held[:5]
    leaf_maps, node_maps, bases, near, inverse = held[5:]
    count_rows(rows)
    leaves, nvec, block = near.shape
    rank = bases.shape[1]
    nodes = tree_all.shape[0]
    pairs = leaf_all.shape[0]
    node_at = 2 * pairs
    beside = 3 * groups
    sub_at = node_at + beside
    blank = sub_at + subtrees
    sub_pos = lax.div(place[0], groups)
    left = lax.broadcasted_iota(jnp.int32, (PACK_ROWS, 2 * rank), 1) < rank

    def list_leaf(leaf, at):
        count = leaf_count[leaf]

        def one(step, carry):
            srcs[2 * (at + step)] = leaf_src[leaf, 2 * step]
            second = jnp.where(2 * step + 1 < count, leaf_src[leaf, 2 * step + 1], blank)
            srcs[2 * (at + step) + 1] = second
            dsts[at + step] = leaf
            return carry

        steps = (count + 1) // 2
        lax.fori_loop(0, steps, one, 0)
        return at + steps

    size = lax.fori_loop(0, leaves, list_leaf, 0)
    count = node_count[0]

    def list_node(step, carry):
        srcs[2 * (size + step)] = node_at + node_src[0, 2 * step]
        second = jnp.where(2 * step + 1 < count, node_at + node_src[0, 2 * step + 1], blank)
        srcs[2 * (size + step) + 1] = second
        dsts[size + step] = leaves
        return carry

    steps = (count + 1) // 2
    lax.fori_loop(0, steps, list_node, 0)

    def list_sub(sub, at):
        srcs[at] = sub_at + sub
        dsts[at // 2] = leaves + 1
        return at + jnp.where(jnp.abs(sub - sub_pos) >= 2, 1, 0)

    ends = lax.fori_loop(0, subtrees, list_sub, 2 * (size + steps))
    srcs[ends] = blank
    dsts[ends // 2] = leaves + 1
    ends = (ends + 1) // 2
    for each in range(AT_ONCE):
        srcs[2 * (ends + each)] = blank
        srcs[2 * (ends + each) + 1] = blank
        dsts[ends + each] = leaves + 1

    for copy in leaf_copies:
        copy.wait()

    def both_leaves(pair, carry):
        packs = leaf_all[pair]
        turned = pltpu.roll(packs, rank, 1)
        twice[2 * pair] = jnp.where(left, packs, turned)
        twice[2 * pair + 1] = jnp.where(left, turned, packs)
        return carry

    lax.fori_loop(0, pairs, both_leaves, 0, unroll=4)
    copies[1].wait()

    def both_node(each, carry):
        packs = tree_all[jnp.clip((sub_pos - 1) * groups + each, 0, nodes - 1)]
        twice[node_at + each] = jnp.where(left, packs, pltpu.roll(packs, rank, 1))
        return carry

    lax.fori_loop(0, beside, both_node, 0, unroll=4)

    def both_sub(sub, carry):
        total = tree_all[sub * groups, :nvec]
        for each in range(1, groups):
            total = total + tree_all[sub * groups + each, :nvec]
        packs = jnp.concatenate([total, tree_all[sub * groups, nvec:]], axis=0)
        twice[sub_at + sub] = jnp.where(left, pltpu.roll(packs, rank, 1), packs)
        return carry

    lax.fori_loop(0, subtrees, both_sub, 0, unroll=2)
    twice[blank] = jnp.zeros_like(twice[blank])
    coef[...] = jnp.zeros_like(coef)
    for copy in copies[2:6]:
        copy.wait()

    def upright(skel, at):
        for axis in range(2):
            row = jnp.broadcast_to(skel[axis : axis + 1], (2 * rank, rank))
            cols[at, axis] = jnp.transpose(row)

    def upright_leaf(leaf, carry):
        upright(leaf_skel[leaf], leaf)
        return carry

    lax.fori_loop(0, leaves, upright_leaf, 0, unroll=4)
    upright(node_skel[0], leaves)
    upright(sub_skel[0], leaves + 1)

    def couple(step, carry):
        terms = []
        for each in range(AT_ONCE):
            item = step * AT_ONCE + each
            packs = jnp.where(left, twice[srcs[2 * item]], twice[srcs[2 * item + 1]])
            target = dsts[item]
            diff_x = cols[target, 0] - packs[nvec : nvec + 1]
            diff_y = cols[target, 1] - packs[nvec + 1 : nvec + 2]
            square = (diff_x * diff_x + diff_y * diff_y) * tables[0]
            arg = square * lax.rsqrt(TINY - square)
            value = tables[5]
            for power in (4, 3, 2, 1):
                value = value * arg + tables[power]
            value = value * jnp.exp2(arg)
            terms.append((target, product(packs[:nvec], value, True)))
        for target, total in terms:
            coef[target] += total
        return carry

    lax.fori_loop(0, (ends + AT_ONCE - 1) // AT_ONCE, couple, 0)
    for copy in copies[6:]:
        copy.wait()
    down_node = coef[leaves] + product(coef[leaves + 1], node_maps[0], True)
    for leaf in range(leaves):
        down_leaf = coef[leaf] + product(down_node, leaf_maps[leaf], True)
        whole = near[leaf] + product(down_leaf, bases[leaf])
        for each in range(block // WIDE):
            fill(
                source,
                whole[:, each * WIDE : (each + 1) * WIDE],
                (leaf * (block // WIDE) + each) * nvec,
                nvec,
            )

    def scatter(each, carry):
        at = pl.multiple_of(each * block, block)
        out[:, pl.ds(at, block)] = pick(rows, source, leaf_index(inverse, each, block), nvec)
        return carry

    steps = inverse.shape[0] * WIDE // block
    segments = 4
    leaving = []
    for each in range(segments):
        start, stop = each * steps // segments, (each + 1) * steps // segments
        lax.fori_loop(start, stop, scatter, 0, unroll=2)
        span = slice(start * block, stop * block)
        leaving.append(pltpu.make_async_copy(out.at[:, span], out_at.at[:, span], sems.at[each]))
        leaving[-1].start()
    for copy in leaving:
        copy.wait()


def skeleton_tables(rank):
    scale, poly = make_tables(1.0 / math.sqrt(rank))
    var = np.arange(rank) % 3
    rows, cols = var[:, None], np.tile(var, 2)[None, :]
    return np.stack([scale[rows, cols]] + [poly[power][rows, cols] for power in range(5)]).astype(
        np.float32
    )


def shards(
    vectors,
    coords,
    perm,
    bases,
    leaf_maps,
    node_maps,
    leaf_skel,
    node_skel,
    sub_skel,
    leaf_src,
    leaf_count,
    node_src,
    node_count,
):
    nvec, rows_dev = vectors.shape
    leaves, rank, block = bases.shape
    groups = lax.axis_size("grp")
    subtrees = lax.axis_size("leaf")
    nodes = groups * subtrees
    sub_pos = lax.axis_index("leaf")
    device_pos = sub_pos * groups + lax.axis_index("grp")
    chunks = rows_dev // WIDE
    vmem = pl.BlockSpec(memory_space=pltpu.VMEM)
    smem = pl.BlockSpec(memory_space=pltpu.SMEM)
    hbm = pl.BlockSpec(memory_space=pltpu.HBM)
    anywhere = pl.BlockSpec(memory_space=pl.ANY)
    params = pltpu.CompilerParams(vmem_limit_bytes=60 * 1024 * 1024)
    order = perm.reshape(rows_dev // 128, 128)

    def like(*arrays):
        return [pltpu.VMEM(each.shape, each.dtype) for each in arrays]

    given = (vectors, order, bases, leaf_maps, node_maps, leaf_skel, node_skel, sub_skel)
    tree_vec, leaf_pack, tree_pack = pl.pallas_call(
        up_kernel,
        out_shape=(
            jax.ShapeDtypeStruct((leaves, nvec, block), F32),
            jax.ShapeDtypeStruct((leaves // 2, PACK_ROWS, 2 * rank), F32),
            jax.ShapeDtypeStruct((nodes, PACK_ROWS, 2 * rank), F32),
        ),
        in_specs=[hbm] * 8,
        out_specs=(hbm, vmem, vmem),
        scratch_shapes=like(*given)
        + [
            pltpu.VMEM((leaves, nvec, block), F32),
            pltpu.VMEM((chunks * nvec, 2 * WIDE), BF16),
            pltpu.VMEM((WIDE, block), jnp.int16),
            pltpu.SemaphoreType.DMA((9,)),
        ],
        compiler_params=params,
        name="up",
    )(*given)
    tree_all = lax.all_to_all(tree_pack, ("leaf", "grp"), 0, 0, tiled=True)
    leaf_all = [leaf_pack] + [
        lax.ppermute(leaf_pack, "grp", [(each, (each + shift) % groups) for each in range(groups)])
        for shift in range(1, groups)
    ]
    shift = (device_pos * (rows_dev % 3) % 3).astype(jnp.int32).reshape(1)
    near, inverse = pl.pallas_call(
        near_kernel,
        out_shape=(
            jax.ShapeDtypeStruct((leaves, nvec, block), F32),
            jax.ShapeDtypeStruct((chunks, WIDE), jnp.int32),
        ),
        in_specs=[smem, hbm, hbm, hbm],
        out_specs=(hbm,) * 2,
        scratch_shapes=like(coords, order, tree_vec)
        + [
            pltpu.VMEM((leaves, nvec, block), F32),
            pltpu.VMEM((chunks, WIDE), jnp.int32),
            pltpu.VMEM((2 * chunks, WIDE), F32),
            pltpu.VMEM((6 * chunks, WIDE), BF16),
            pltpu.VMEM((WIDE, block), jnp.int16),
            pltpu.VMEM((2 * chunks, WIDE), F32),
            *[
                pltpu.VMEM((3, 8, block), F32),
                pltpu.VMEM((3, block // 8, 8, 128), F32),
            ]
            * 2,
            *[pltpu.VMEM((block, block), BF16)] * 4,
            pltpu.SemaphoreType.DMA((4,)),
        ],
        compiler_params=params,
        cost_estimate=pl.CostEstimate(
            flops=128 * leaves * block * block,
            bytes_accessed=8 * leaves * nvec * block,
            transcendentals=leaves * block * block,
        ),
        name="near",
    )(shift, coords, order, tree_vec)
    tables = jnp.asarray(skeleton_tables(rank))
    given = (tree_all, leaf_skel, node_skel, sub_skel, tables)
    given = given + (leaf_maps, node_maps, bases, near, inverse)
    items = (leaf_src.size + node_src.size + subtrees + 2) // 2 + AT_ONCE
    sources = groups * leaves + 3 * groups + subtrees + 1
    return pl.pallas_call(
        functools.partial(far_kernel, groups, subtrees),
        out_shape=jax.ShapeDtypeStruct((nvec, rows_dev), F32),
        in_specs=[smem] * 5 + [anywhere] * (groups + 1) + [hbm] * 9,
        out_specs=hbm,
        scratch_shapes=like(*given)
        + [
            pltpu.VMEM((groups * leaf_pack.shape[0],) + leaf_pack.shape[1:], F32),
            pltpu.VMEM((chunks * nvec, 2 * WIDE), BF16),
            pltpu.VMEM((leaves + 2, nvec, rank), F32),
            pltpu.VMEM((sources, PACK_ROWS, 2 * rank), F32),
            pltpu.VMEM((leaves + 2, 2, rank, 2 * rank), F32),
            pltpu.VMEM((nvec, rows_dev), F32),
            pltpu.VMEM((WIDE, block), jnp.int16),
            pltpu.SMEM((2 * items,), jnp.int32),
            pltpu.SMEM((items,), jnp.int32),
            pltpu.SemaphoreType.DMA((10 + groups,)),
        ],
        compiler_params=params,
        name="far",
    )(
        device_pos.astype(jnp.int32).reshape(1),
        leaf_src,
        leaf_count,
        node_src,
        node_count,
        *leaf_all,
        *given,
    )


def solution(mesh):
    placed = (
        P(None, ("leaf", "grp")),
        P(None, ("leaf", "grp")),
        P(("leaf", "grp")),
        P(("leaf", "grp"), None, None),
        P(("leaf", "grp"), None, None),
        P(("leaf", "grp"), None, None),
        P(("leaf", "grp"), None, None),
        P(("leaf", "grp"), None, None),
        P("leaf", None, None),
        P(("leaf", "grp"), None),
        P(("leaf", "grp")),
        P(("leaf", "grp"), None),
        P(("leaf", "grp")),
    )
    return jax.shard_map(
        shards, mesh=mesh, in_specs=placed, out_specs=P(None, ("leaf", "grp")), check_vma=False
    )
```

```python
import functools
import math

import jax
import jax.numpy as jnp
import numpy as np
from jax import lax
from jax.experimental import pallas as pl
from jax.experimental.pallas import tpu as pltpu
from jax.sharding import PartitionSpec as P

F32 = jnp.float32
BF16 = jnp.bfloat16
WIDE = 128
SHIFT = 7
LOG2E = math.log2(math.e)
TINY = 1e-37
PACK_ROWS = 24
PART = 32
AT_ONCE = 8


def make_tables(norm):
    smooth = [0, 2, 4]
    sigmas = [1.0, 0.8, 1.2]
    rho = [[1.0, 0.5, 0.3], [0.5, 1.0, 0.4], [0.3, 0.4, 1.0]]
    scale = np.zeros((3, 3))
    poly = np.zeros((5, 3, 3))
    for first in range(3):
        for second in range(3):
            order = (smooth[first] + smooth[second]) // 2
            scale[first, second] = -(2.0 * order + 1.0) * (LOG2E / 0.3) ** 2
            amp = sigmas[first] * sigmas[second] * rho[first][second] * norm
            for power in range(order + 1):
                kterm = order - power
                coeff = math.factorial(order) / math.factorial(2 * order)
                coeff = (
                    coeff
                    * math.factorial(order + kterm)
                    / (math.factorial(kterm) * math.factorial(order - kterm))
                )
                poly[power, first, second] = amp * coeff * 2.0**power * (-1.0 / LOG2E) ** power
    return scale, poly


def dot(one, two, turned=False):
    dims = (((1,), (1 if turned else 0,)), ((), ()))
    return lax.dot_general(one, two, dims, preferred_element_type=F32)


def parts(value):
    high = value.astype(BF16)
    return high, (value - high.astype(F32)).astype(BF16)


def product(one, two, turned=False):
    rows = one.shape[0]
    one_hi, one_lo = parts(one)
    two_hi, two_lo = parts(two)
    both = dot(jnp.concatenate([one_hi, one_lo], axis=0), two_hi, turned)
    return both[:rows] + both[rows:] + dot(one_hi, two_lo, turned)


def count_rows(rows):
    rows[...] = lax.broadcasted_iota(jnp.int32, rows.shape, 0).astype(jnp.int16)


def one_hot(rows, low):
    count = low.shape[1]
    low = jnp.broadcast_to(low, (16, count)).astype(jnp.int16)[None]
    same = rows[:, :count].reshape(WIDE // 16, 16, count) == low
    return jnp.where(same, jnp.bfloat16(1), jnp.bfloat16(0)).reshape(WIDE, count)


def fill(source, value, at, nvec):
    high, low = parts(value)
    source[pl.ds(at, nvec), :WIDE] = high
    source[pl.ds(at, nvec), WIDE:] = low


def pick(rows, source, index, nvec):
    count = index.shape[1]
    hot = one_hot(rows, index & (WIDE - 1))
    hot = jnp.concatenate([hot, hot], axis=0)
    chunk = jnp.broadcast_to(index >> SHIFT, (8, count))[None]
    out = jnp.zeros((nvec // 8, 8, count), F32)
    chunks = source.shape[0] // nvec
    found = dot(source[...], hot).reshape(chunks, nvec // 8, 8, count)
    for each in range(chunks):
        out = jnp.where(chunk == each, found[each], out)
    return out.reshape(nvec, count)


def leaf_index(perm, leaf, block):
    rows = block // 128
    return jnp.concatenate([perm[pl.ds(leaf * rows + each, 1), :] for each in range(rows)], axis=1)


def fetch(pairs, sems):
    copies = [pltpu.make_async_copy(src, dst, sems.at[each]) for each, (src, dst) in enumerate(pairs)]
    for copy in copies:
        copy.start()
    return copies


def up_kernel(*refs):
    given, (tree_out, leaf_pack, tree_pack) = refs[:8], refs[8:11]
    held = refs[11:19]
    tree_vec, source, rows, sems = refs[19:]
    count_rows(rows)
    copies = fetch(list(zip(given, held)), sems)
    vec, perm, bases, leaf_maps, node_maps, leaf_skel, node_skel, sub_skel = held
    leaves, nvec, block = tree_vec.shape
    rank = bases.shape[1]
    copies[0].wait()
    for each in range(vec.shape[1] // WIDE):
        fill(source, vec[:, each * WIDE : (each + 1) * WIDE], each * nvec, nvec)
    copies[1].wait()

    def gather(leaf, carry):
        tree_vec[leaf] = pick(rows, source, leaf_index(perm, leaf, block), nvec)
        return carry

    lax.fori_loop(0, leaves, gather, 0, unroll=4)
    leave = pltpu.make_async_copy(tree_vec, tree_out, sems.at[len(copies)])
    leave.start()
    for copy in copies[2:]:
        copy.wait()
    up_node = jnp.zeros((nvec, rank), F32)
    blank = jnp.zeros((PACK_ROWS - nvec - 2, 2 * rank), F32)
    for leaf in range(0, leaves, 2):
        up = [product(tree_vec[leaf + each], bases[leaf + each], True) for each in range(2)]
        leaf_pack[leaf // 2] = jnp.concatenate(
            [
                jnp.concatenate(up, axis=1),
                jnp.concatenate([leaf_skel[leaf], leaf_skel[leaf + 1]], axis=1),
                blank,
            ],
            axis=0,
        )
        for each in range(2):
            up_node = up_node + product(up[each], leaf_maps[leaf + each])
    up_sub = product(up_node, node_maps[0])
    packed = jnp.concatenate(
        [
            jnp.concatenate([up_node, up_sub], axis=1),
            jnp.concatenate([node_skel[0], sub_skel[0]], axis=1),
            blank,
        ],
        axis=0,
    )

    def spread(each, carry):
        tree_pack[each] = packed
        return carry

    lax.fori_loop(0, tree_pack.shape[0], spread, 0)
    leave.wait()


def near_kernel(shift, *refs):
    given, (near_out, inverse_out) = refs[:3], refs[3:5]
    held = refs[5:8]
    near, inverse, flat, source, rows, slots = refs[8:14]
    even, odd, sooner, later, sems = refs[14:16], refs[16:18], refs[18:20], refs[20:22], refs[22]
    copies = fetch(list(zip(given, held)), sems)
    crd, perm, tree_vec = held
    count_rows(rows)
    leaves, nvec, block = tree_vec.shape
    chunks = crd.shape[1] // WIDE
    scale, poly = make_tables(1.0 / math.sqrt(block))
    slope = scale[0, 1] - scale[0, 0]
    copies[0].wait()
    for axis in range(2):
        for each in range(chunks):
            row = axis * chunks + each
            flat[row : row + 1, :] = crd[axis : axis + 1, each * WIDE : (each + 1) * WIDE]
    rest = flat[...]
    for piece in range(3):
        rounded = rest.astype(BF16)
        source[piece * 2 * chunks : (piece + 1) * 2 * chunks, :] = rounded
        rest = rest - rounded.astype(F32)
    slots[...] = jnp.zeros_like(slots)
    copies[1].wait()
    side = 128
    tiles = block // side

    def place_leaf(leaf, across, down):
        live = jnp.where(leaf < leaves, 1.0, 0.0)
        leaf = jnp.minimum(leaf, leaves - 1)
        index = leaf_index(perm, leaf, block)
        hot = one_hot(rows, index & (WIDE - 1))
        found = dot(source[...], hot)
        found = (
            found[: 2 * chunks] + found[2 * chunks : 4 * chunks] + found[4 * chunks :]
        )
        mine = lax.broadcasted_iota(jnp.int32, (chunks, block), 0) == index >> SHIFT
        lane = lax.broadcasted_iota(jnp.int32, (chunks, block), 1) + leaf * block
        lane_low = (lane & (WIDE - 1)).astype(F32) * live
        lane_high = (lane >> SHIFT).astype(F32) * live
        marks = jnp.concatenate(
            [jnp.where(mine, lane_low, 0.0), jnp.where(mine, lane_high, 0.0)], axis=0
        ).astype(BF16)
        slots[...] += dot(marks, hot, True)
        row_x = jnp.sum(jnp.where(mine, found[:chunks], 0.0), axis=0, keepdims=True)
        row_y = jnp.sum(jnp.where(mine, found[chunks:], 0.0), axis=0, keepdims=True)
        moved = index + shift[0]
        kind = moved - 3 * ((moved * 43691) >> 17)
        row_w = kind.astype(F32) * slope
        for place, row in enumerate((row_x, row_y, row_w)):
            across[place] = jnp.broadcast_to(row, (8, block))
            turned = jnp.transpose(jnp.broadcast_to(row, (side, block)))
            down[place] = turned.reshape(block // 8, 8, side)

    copies[2].wait()

    def values(across, down, high, low):
        for col in range(tiles):
            cols = slice(col * side, (col + 1) * side)
            over_x, over_y, over_w = [across[each, :, cols] for each in range(3)]
            over_zero, over_one = over_w > 0.5 * slope, over_w > 1.5 * slope

            def across_table(power, first):
                zero, one, two = [float(each) for each in poly[power, first]]
                return jnp.where(over_zero, zero, jnp.where(over_one, one, two))[None]

            table = [[across_table(power, first) for first in range(3)] for power in range(5)]
            over_w = (over_w + float(scale[0, 0]))[None]
            over_x, over_y = over_x[None], over_y[None]
            for row in range(col + 1):
                pieces = []
                for part in range(side // PART):
                    first = row * side + part * PART
                    at = slice(first // 8, (first + PART) // 8)
                    diff_x = down[0, at] - over_x
                    diff_y = down[1, at] - over_y
                    down_w = down[2, at]
                    var_zero, var_one = down_w > 0.5 * slope, down_w > 1.5 * slope
                    square = (diff_x * diff_x + diff_y * diff_y) * (down_w + over_w)
                    arg = square * lax.rsqrt(TINY - square)
                    value = jnp.where(var_one, table[3][1], table[4][2] * arg + table[3][2])
                    rest = value * arg + jnp.where(var_one, table[2][1], table[2][2])
                    value = jnp.where(var_zero, table[2][0], rest)
                    for power in (1, 0):
                        a, b, c = table[power]
                        value = value * arg + jnp.where(var_zero, a, jnp.where(var_one, b, c))
                    pieces.append(parts((value * jnp.exp2(arg)).reshape(PART, side)))
                rows = slice(row * side, (row + 1) * side)
                for each, out in enumerate((high, low)):
                    tile = jnp.concatenate([piece[each] for piece in pieces], axis=0)
                    out[rows, cols] = tile
                    if row < col:
                        out[cols, rows] = jnp.transpose(tile)

    def apply(leaf, high, low):
        vec_hi, vec_lo = parts(tree_vec[leaf])
        both = dot(jnp.concatenate([vec_hi, vec_lo], axis=0), high[...])
        near[leaf] = both[:nvec] + both[nvec:] + dot(vec_hi, low[...])

    for each in later:
        each[...] = jnp.zeros_like(each)

    def two_leaves(step, carry):
        apply(jnp.maximum(2 * step - 1, 0), *later)
        values(*even, *sooner)
        place_leaf(2 * step + 1, *odd)
        apply(2 * step, *sooner)
        values(*odd, *later)
        place_leaf(2 * step + 2, *even)
        return carry

    place_leaf(0, *even)

    lax.fori_loop(0, leaves // 4, two_leaves, 0)
    half = slice(0, leaves // 2 - 1)
    first = pltpu.make_async_copy(near.at[half], near_out.at[half], sems.at[0])
    first.start()
    lax.fori_loop(leaves // 4, leaves // 2, two_leaves, 0)
    inverse[...] = (slots[:chunks] + slots[chunks:] * WIDE).astype(jnp.int32)
    leave = pltpu.make_async_copy(inverse, inverse_out, sems.at[3])
    leave.start()
    apply(leaves - 1, *later)
    half = slice(leaves // 2 - 1, leaves)
    second = pltpu.make_async_copy(near.at[half], near_out.at[half], sems.at[1])
    second.start()
    for copy in (leave, first, second):
        copy.wait()


def far_kernel(groups, subtrees, *refs):
    place, leaf_src, leaf_count, node_src, node_count = refs[:5]
    leaf_packs, refs = refs[5 : 5 + groups], refs[5 + groups :]
    given, out_at, held = refs[:10], refs[10], refs[11:21]
    leaf_all, source, coef, twice, cols, out, rows, srcs, dsts, sems = refs[21:]
    own = leaf_packs[0].shape[0]
    grp_pos = lax.rem(place[0], groups)
    owner = [lax.rem(grp_pos - shift + groups, groups) for shift in range(groups)]
    arrive = [leaf_all.at[pl.ds(each * own, own)] for each in owner]
    copies = fetch(list(zip(leaf_packs + given, arrive + list(held))), sems)
    leaf_copies, copies = copies[:groups], [None] + copies[groups:]
    tree_all, leaf_skel, node_skel, sub_skel, tables = held[:5]
    leaf_maps, node_maps, bases, near, inverse = held[5:]
    count_rows(rows)
    leaves, nvec, block = near.shape
    rank = bases.shape[1]
    nodes = tree_all.shape[0]
    pairs = leaf_all.shape[0]
    node_at = 2 * pairs
    beside = 3 * groups
    sub_at = node_at + beside
    blank = sub_at + subtrees
    sub_pos = lax.div(place[0], groups)
    left = lax.broadcasted_iota(jnp.int32, (PACK_ROWS, 2 * rank), 1) < rank

    def list_leaf(leaf, at):
        count = leaf_count[leaf]

        def one(step, carry):
            srcs[2 * (at + step)] = leaf_src[leaf, 2 * step]
            second = jnp.where(2 * step + 1 < count, leaf_src[leaf, 2 * step + 1], blank)
            srcs[2 * (at + step) + 1] = second
            dsts[at + step] = leaf
            return carry

        steps = (count + 1) // 2
        lax.fori_loop(0, steps, one, 0)
        return at + steps

    size = lax.fori_loop(0, leaves, list_leaf, 0)
    count = node_count[0]

    def list_node(step, carry):
        srcs[2 * (size + step)] = node_at + node_src[0, 2 * step]
        second = jnp.where(2 * step + 1 < count, node_at + node_src[0, 2 * step + 1], blank)
        srcs[2 * (size + step) + 1] = second
        dsts[size + step] = leaves
        return carry

    steps = (count + 1) // 2
    lax.fori_loop(0, steps, list_node, 0)

    def list_sub(sub, at):
        srcs[at] = sub_at + sub
        dsts[at // 2] = leaves + 1
        return at + jnp.where(jnp.abs(sub - sub_pos) >= 2, 1, 0)

    ends = lax.fori_loop(0, subtrees, list_sub, 2 * (size + steps))
    srcs[ends] = blank
    dsts[ends // 2] = leaves + 1
    ends = (ends + 1) // 2
    for each in range(AT_ONCE):
        srcs[2 * (ends + each)] = blank
        srcs[2 * (ends + each) + 1] = blank
        dsts[ends + each] = leaves + 1

    for copy in leaf_copies:
        copy.wait()

    def both_leaves(pair, carry):
        packs = leaf_all[pair]
        turned = pltpu.roll(packs, rank, 1)
        twice[2 * pair] = jnp.where(left, packs, turned)
        twice[2 * pair + 1] = jnp.where(left, turned, packs)
        return carry

    lax.fori_loop(0, pairs, both_leaves, 0, unroll=4)
    copies[1].wait()

    def both_node(each, carry):
        packs = tree_all[jnp.clip((sub_pos - 1) * groups + each, 0, nodes - 1)]
        twice[node_at + each] = jnp.where(left, packs, pltpu.roll(packs, rank, 1))
        return carry

    lax.fori_loop(0, beside, both_node, 0, unroll=4)

    def both_sub(sub, carry):
        total = tree_all[sub * groups, :nvec]
        for each in range(1, groups):
            total = total + tree_all[sub * groups + each, :nvec]
        packs = jnp.concatenate([total, tree_all[sub * groups, nvec:]], axis=0)
        twice[sub_at + sub] = jnp.where(left, pltpu.roll(packs, rank, 1), packs)
        return carry

    lax.fori_loop(0, subtrees, both_sub, 0, unroll=2)
    twice[blank] = jnp.zeros_like(twice[blank])
    coef[...] = jnp.zeros_like(coef)
    for copy in copies[2:6]:
        copy.wait()

    def upright(skel, at):
        for axis in range(2):
            row = jnp.broadcast_to(skel[axis : axis + 1], (2 * rank, rank))
            cols[at, axis] = jnp.transpose(row)

    def upright_leaf(leaf, carry):
        upright(leaf_skel[leaf], leaf)
        return carry

    lax.fori_loop(0, leaves, upright_leaf, 0, unroll=4)
    upright(node_skel[0], leaves)
    upright(sub_skel[0], leaves + 1)

    def couple(step, carry):
        terms = []
        for each in range(AT_ONCE):
            item = step * AT_ONCE + each
            packs = jnp.where(left, twice[srcs[2 * item]], twice[srcs[2 * item + 1]])
            target = dsts[item]
            diff_x = cols[target, 0] - packs[nvec : nvec + 1]
            diff_y = cols[target, 1] - packs[nvec + 1 : nvec + 2]
            square = (diff_x * diff_x + diff_y * diff_y) * tables[0]
            arg = square * lax.rsqrt(TINY - square)
            value = tables[5]
            for power in (4, 3, 2, 1):
                value = value * arg + tables[power]
            value = value * jnp.exp2(arg)
            terms.append((target, product(packs[:nvec], value, True)))
        for target, total in terms:
            coef[target] += total
        return carry

    lax.fori_loop(0, (ends + AT_ONCE - 1) // AT_ONCE, couple, 0)
    for copy in copies[6:]:
        copy.wait()
    down_node = coef[leaves] + product(coef[leaves + 1], node_maps[0], True)
    for leaf in range(leaves):
        down_leaf = coef[leaf] + product(down_node, leaf_maps[leaf], True)
        whole = near[leaf] + product(down_leaf, bases[leaf])
        for each in range(block // WIDE):
            fill(
                source,
                whole[:, each * WIDE : (each + 1) * WIDE],
                (leaf * (block // WIDE) + each) * nvec,
                nvec,
            )

    def scatter(each, carry):
        at = pl.multiple_of(each * block, block)
        out[:, pl.ds(at, block)] = pick(rows, source, leaf_index(inverse, each, block), nvec)
        return carry

    steps = inverse.shape[0] * WIDE // block
    segments = 4
    leaving = []
    for each in range(segments):
        start, stop = each * steps // segments, (each + 1) * steps // segments
        lax.fori_loop(start, stop, scatter, 0, unroll=4)
        span = slice(start * block, stop * block)
        leaving.append(pltpu.make_async_copy(out.at[:, span], out_at.at[:, span], sems.at[each]))
        leaving[-1].start()
    for copy in leaving:
        copy.wait()


def skeleton_tables(rank):
    scale, poly = make_tables(1.0 / math.sqrt(rank))
    var = np.arange(rank) % 3
    rows, cols = var[:, None], np.tile(var, 2)[None, :]
    return np.stack([scale[rows, cols]] + [poly[power][rows, cols] for power in range(5)]).astype(
        np.float32
    )


def shards(
    vectors,
    coords,
    perm,
    bases,
    leaf_maps,
    node_maps,
    leaf_skel,
    node_skel,
    sub_skel,
    leaf_src,
    leaf_count,
    node_src,
    node_count,
):
    nvec, rows_dev = vectors.shape
    leaves, rank, block = bases.shape
    groups = lax.axis_size("grp")
    subtrees = lax.axis_size("leaf")
    nodes = groups * subtrees
    sub_pos = lax.axis_index("leaf")
    device_pos = sub_pos * groups + lax.axis_index("grp")
    chunks = rows_dev // WIDE
    vmem = pl.BlockSpec(memory_space=pltpu.VMEM)
    smem = pl.BlockSpec(memory_space=pltpu.SMEM)
    hbm = pl.BlockSpec(memory_space=pltpu.HBM)
    anywhere = pl.BlockSpec(memory_space=pl.ANY)
    params = pltpu.CompilerParams(vmem_limit_bytes=60 * 1024 * 1024)
    order = perm.reshape(rows_dev // 128, 128)

    def like(*arrays):
        return [pltpu.VMEM(each.shape, each.dtype) for each in arrays]

    given = (vectors, order, bases, leaf_maps, node_maps, leaf_skel, node_skel, sub_skel)
    tree_vec, leaf_pack, tree_pack = pl.pallas_call(
        up_kernel,
        out_shape=(
            jax.ShapeDtypeStruct((leaves, nvec, block), F32),
            jax.ShapeDtypeStruct((leaves // 2, PACK_ROWS, 2 * rank), F32),
            jax.ShapeDtypeStruct((nodes, PACK_ROWS, 2 * rank), F32),
        ),
        in_specs=[hbm] * 8,
        out_specs=(hbm, vmem, vmem),
        scratch_shapes=like(*given)
        + [
            pltpu.VMEM((leaves, nvec, block), F32),
            pltpu.VMEM((chunks * nvec, 2 * WIDE), BF16),
            pltpu.VMEM((WIDE, block), jnp.int16),
            pltpu.SemaphoreType.DMA((9,)),
        ],
        compiler_params=params,
        name="up",
    )(*given)
    tree_all = lax.all_to_all(tree_pack, ("leaf", "grp"), 0, 0, tiled=True)
    leaf_all = [leaf_pack] + [
        lax.ppermute(leaf_pack, "grp", [(each, (each + shift) % groups) for each in range(groups)])
        for shift in range(1, groups)
    ]
    shift = (device_pos * (rows_dev % 3) % 3).astype(jnp.int32).reshape(1)
    near, inverse = pl.pallas_call(
        near_kernel,
        out_shape=(
            jax.ShapeDtypeStruct((leaves, nvec, block), F32),
            jax.ShapeDtypeStruct((chunks, WIDE), jnp.int32),
        ),
        in_specs=[smem, hbm, hbm, hbm],
        out_specs=(hbm,) * 2,
        scratch_shapes=like(coords, order, tree_vec)
        + [
            pltpu.VMEM((leaves, nvec, block), F32),
            pltpu.VMEM((chunks, WIDE), jnp.int32),
            pltpu.VMEM((2 * chunks, WIDE), F32),
            pltpu.VMEM((6 * chunks, WIDE), BF16),
            pltpu.VMEM((WIDE, block), jnp.int16),
            pltpu.VMEM((2 * chunks, WIDE), F32),
            *[
                pltpu.VMEM((3, 8, block), F32),
                pltpu.VMEM((3, block // 8, 8, 128), F32),
            ]
            * 2,
            *[pltpu.VMEM((block, block), BF16)] * 4,
            pltpu.SemaphoreType.DMA((4,)),
        ],
        compiler_params=params,
        cost_estimate=pl.CostEstimate(
            flops=128 * leaves * block * block,
            bytes_accessed=8 * leaves * nvec * block,
            transcendentals=leaves * block * block,
        ),
        name="near",
    )(shift, coords, order, tree_vec)
    tables = jnp.asarray(skeleton_tables(rank))
    given = (tree_all, leaf_skel, node_skel, sub_skel, tables)
    given = given + (leaf_maps, node_maps, bases, near, inverse)
    items = (leaf_src.size + node_src.size + subtrees + 2) // 2 + AT_ONCE
    sources = groups * leaves + 3 * groups + subtrees + 1
    return pl.pallas_call(
        functools.partial(far_kernel, groups, subtrees),
        out_shape=jax.ShapeDtypeStruct((nvec, rows_dev), F32),
        in_specs=[smem] * 5 + [anywhere] * (groups + 1) + [hbm] * 9,
        out_specs=hbm,
        scratch_shapes=like(*given)
        + [
            pltpu.VMEM((groups * leaf_pack.shape[0],) + leaf_pack.shape[1:], F32),
            pltpu.VMEM((chunks * nvec, 2 * WIDE), BF16),
            pltpu.VMEM((leaves + 2, nvec, rank), F32),
            pltpu.VMEM((sources, PACK_ROWS, 2 * rank), F32),
            pltpu.VMEM((leaves + 2, 2, rank, 2 * rank), F32),
            pltpu.VMEM((nvec, rows_dev), F32),
            pltpu.VMEM((WIDE, block), jnp.int16),
            pltpu.SMEM((2 * items,), jnp.int32),
            pltpu.SMEM((items,), jnp.int32),
            pltpu.SemaphoreType.DMA((10 + groups,)),
        ],
        compiler_params=params,
        name="far",
    )(
        device_pos.astype(jnp.int32).reshape(1),
        leaf_src,
        leaf_count,
        node_src,
        node_count,
        *leaf_all,
        *given,
    )


def solution(mesh):
    placed = (
        P(None, ("leaf", "grp")),
        P(None, ("leaf", "grp")),
        P(("leaf", "grp")),
        P(("leaf", "grp"), None, None),
        P(("leaf", "grp"), None, None),
        P(("leaf", "grp"), None, None),
        P(("leaf", "grp"), None, None),
        P(("leaf", "grp"), None, None),
        P("leaf", None, None),
        P(("leaf", "grp"), None),
        P(("leaf", "grp")),
        P(("leaf", "grp"), None),
        P(("leaf", "grp")),
    )
    return jax.shard_map(
        shards, mesh=mesh, in_specs=placed, out_specs=P(None, ("leaf", "grp")), check_vma=False
    )
```

```python
import functools
import math

import jax
import jax.numpy as jnp
import numpy as np
from jax import lax
from jax.experimental import pallas as pl
from jax.experimental.pallas import tpu as pltpu
from jax.sharding import PartitionSpec as P

F32 = jnp.float32
BF16 = jnp.bfloat16
WIDE = 128
SHIFT = 7
LOG2E = math.log2(math.e)
TINY = 1e-37
PACK_ROWS = 24
PART = 32
AT_ONCE = 8


def make_tables(norm):
    smooth = [0, 2, 4]
    sigmas = [1.0, 0.8, 1.2]
    rho = [[1.0, 0.5, 0.3], [0.5, 1.0, 0.4], [0.3, 0.4, 1.0]]
    scale = np.zeros((3, 3))
    poly = np.zeros((5, 3, 3))
    for first in range(3):
        for second in range(3):
            order = (smooth[first] + smooth[second]) // 2
            scale[first, second] = -(2.0 * order + 1.0) * (LOG2E / 0.3) ** 2
            amp = sigmas[first] * sigmas[second] * rho[first][second] * norm
            for power in range(order + 1):
                kterm = order - power
                coeff = math.factorial(order) / math.factorial(2 * order)
                coeff = (
                    coeff
                    * math.factorial(order + kterm)
                    / (math.factorial(kterm) * math.factorial(order - kterm))
                )
                poly[power, first, second] = amp * coeff * 2.0**power * (-1.0 / LOG2E) ** power
    return scale, poly


def dot(one, two, turned=False):
    dims = (((1,), (1 if turned else 0,)), ((), ()))
    return lax.dot_general(one, two, dims, preferred_element_type=F32)


def parts(value):
    high = value.astype(BF16)
    return high, (value - high.astype(F32)).astype(BF16)


def product(one, two, turned=False):
    rows = one.shape[0]
    one_hi, one_lo = parts(one)
    two_hi, two_lo = parts(two)
    both = dot(jnp.concatenate([one_hi, one_lo], axis=0), two_hi, turned)
    return both[:rows] + both[rows:] + dot(one_hi, two_lo, turned)


def count_rows(rows):
    rows[...] = lax.broadcasted_iota(jnp.int32, rows.shape, 0).astype(jnp.int16)


def one_hot(rows, low):
    count = low.shape[1]
    low = jnp.broadcast_to(low, (16, count)).astype(jnp.int16)[None]
    same = rows[:, :count].reshape(WIDE // 16, 16, count) == low
    return jnp.where(same, jnp.bfloat16(1), jnp.bfloat16(0)).reshape(WIDE, count)


def fill(source, value, at, nvec):
    high, low = parts(value)
    source[pl.ds(at, nvec), :WIDE] = high
    source[pl.ds(at, nvec), WIDE:] = low


def pick(rows, source, index, nvec):
    count = index.shape[1]
    hot = one_hot(rows, index & (WIDE - 1))
    hot = jnp.concatenate([hot, hot], axis=0)
    chunk = jnp.broadcast_to(index >> SHIFT, (8, count))[None]
    out = jnp.zeros((nvec // 8, 8, count), F32)
    chunks = source.shape[0] // nvec
    found = dot(source[...], hot).reshape(chunks, nvec // 8, 8, count)
    for each in range(chunks):
        out = jnp.where(chunk == each, found[each], out)
    return out.reshape(nvec, count)


def leaf_index(perm, leaf, block):
    rows = block // 128
    return jnp.concatenate([perm[pl.ds(leaf * rows + each, 1), :] for each in range(rows)], axis=1)


def fetch(pairs, sems):
    copies = [pltpu.make_async_copy(src, dst, sems.at[each]) for each, (src, dst) in enumerate(pairs)]
    for copy in copies:
        copy.start()
    return copies


def up_kernel(*refs):
    given, (tree_out, leaf_pack, tree_pack) = refs[:8], refs[8:11]
    held = refs[11:19]
    tree_vec, source, rows, sems = refs[19:]
    count_rows(rows)
    copies = fetch(list(zip(given, held)), sems)
    vec, perm, bases, leaf_maps, node_maps, leaf_skel, node_skel, sub_skel = held
    leaves, nvec, block = tree_vec.shape
    rank = bases.shape[1]
    copies[0].wait()
    for each in range(vec.shape[1] // WIDE):
        fill(source, vec[:, each * WIDE : (each + 1) * WIDE], each * nvec, nvec)
    copies[1].wait()

    def gather(leaf, carry):
        tree_vec[leaf] = pick(rows, source, leaf_index(perm, leaf, block), nvec)
        return carry

    lax.fori_loop(0, leaves, gather, 0, unroll=8)
    leave = pltpu.make_async_copy(tree_vec, tree_out, sems.at[len(copies)])
    leave.start()
    for copy in copies[2:]:
        copy.wait()
    up_node = jnp.zeros((nvec, rank), F32)
    blank = jnp.zeros((PACK_ROWS - nvec - 2, 2 * rank), F32)
    for leaf in range(0, leaves, 2):
        up = [product(tree_vec[leaf + each], bases[leaf + each], True) for each in range(2)]
        leaf_pack[leaf // 2] = jnp.concatenate(
            [
                jnp.concatenate(up, axis=1),
                jnp.concatenate([leaf_skel[leaf], leaf_skel[leaf + 1]], axis=1),
                blank,
            ],
            axis=0,
        )
        for each in range(2):
            up_node = up_node + product(up[each], leaf_maps[leaf + each])
    up_sub = product(up_node, node_maps[0])
    packed = jnp.concatenate(
        [
            jnp.concatenate([up_node, up_sub], axis=1),
            jnp.concatenate([node_skel[0], sub_skel[0]], axis=1),
            blank,
        ],
        axis=0,
    )

    def spread(each, carry):
        tree_pack[each] = packed
        return carry

    lax.fori_loop(0, tree_pack.shape[0], spread, 0)
    leave.wait()


def near_kernel(shift, *refs):
    given, (near_out, inverse_out) = refs[:3], refs[3:5]
    held = refs[5:8]
    near, inverse, flat, source, rows, slots = refs[8:14]
    even, odd, sooner, later, sems = refs[14:16], refs[16:18], refs[18:20], refs[20:22], refs[22]
    copies = fetch(list(zip(given, held)), sems)
    crd, perm, tree_vec = held
    count_rows(rows)
    leaves, nvec, block = tree_vec.shape
    chunks = crd.shape[1] // WIDE
    scale, poly = make_tables(1.0 / math.sqrt(block))
    slope = scale[0, 1] - scale[0, 0]
    copies[0].wait()
    for axis in range(2):
        for each in range(chunks):
            row = axis * chunks + each
            flat[row : row + 1, :] = crd[axis : axis + 1, each * WIDE : (each + 1) * WIDE]
    rest = flat[...]
    for piece in range(3):
        rounded = rest.astype(BF16)
        source[piece * 2 * chunks : (piece + 1) * 2 * chunks, :] = rounded
        rest = rest - rounded.astype(F32)
    slots[...] = jnp.zeros_like(slots)
    copies[1].wait()
    side = 128
    tiles = block // side

    def place_leaf(leaf, across, down):
        live = jnp.where(leaf < leaves, 1.0, 0.0)
        leaf = jnp.minimum(leaf, leaves - 1)
        index = leaf_index(perm, leaf, block)
        hot = one_hot(rows, index & (WIDE - 1))
        found = dot(source[...], hot)
        found = (
            found[: 2 * chunks] + found[2 * chunks : 4 * chunks] + found[4 * chunks :]
        )
        mine = lax.broadcasted_iota(jnp.int32, (chunks, block), 0) == index >> SHIFT
        lane = lax.broadcasted_iota(jnp.int32, (chunks, block), 1) + leaf * block
        lane_low = (lane & (WIDE - 1)).astype(F32) * live
        lane_high = (lane >> SHIFT).astype(F32) * live
        marks = jnp.concatenate(
            [jnp.where(mine, lane_low, 0.0), jnp.where(mine, lane_high, 0.0)], axis=0
        ).astype(BF16)
        slots[...] += dot(marks, hot, True)
        row_x = jnp.sum(jnp.where(mine, found[:chunks], 0.0), axis=0, keepdims=True)
        row_y = jnp.sum(jnp.where(mine, found[chunks:], 0.0), axis=0, keepdims=True)
        moved = index + shift[0]
        kind = moved - 3 * ((moved * 43691) >> 17)
        row_w = kind.astype(F32) * slope
        for place, row in enumerate((row_x, row_y, row_w)):
            across[place] = jnp.broadcast_to(row, (8, block))
            turned = jnp.transpose(jnp.broadcast_to(row, (side, block)))
            down[place] = turned.reshape(block // 8, 8, side)

    copies[2].wait()

    def values(across, down, high, low):
        for col in range(tiles):
            cols = slice(col * side, (col + 1) * side)
            over_x, over_y, over_w = [across[each, :, cols] for each in range(3)]
            over_zero, over_one = over_w > 0.5 * slope, over_w > 1.5 * slope

            def across_table(power, first):
                zero, one, two = [float(each) for each in poly[power, first]]
                return jnp.where(over_zero, zero, jnp.where(over_one, one, two))[None]

            table = [[across_table(power, first) for first in range(3)] for power in range(5)]
            over_w = (over_w + float(scale[0, 0]))[None]
            over_x, over_y = over_x[None], over_y[None]
            for row in range(col + 1):
                pieces = []
                for part in range(side // PART):
                    first = row * side + part * PART
                    at = slice(first // 8, (first + PART) // 8)
                    diff_x = down[0, at] - over_x
                    diff_y = down[1, at] - over_y
                    down_w = down[2, at]
                    var_zero, var_one = down_w > 0.5 * slope, down_w > 1.5 * slope
                    square = (diff_x * diff_x + diff_y * diff_y) * (down_w + over_w)
                    arg = square * lax.rsqrt(TINY - square)
                    value = jnp.where(var_one, table[3][1], table[4][2] * arg + table[3][2])
                    rest = value * arg + jnp.where(var_one, table[2][1], table[2][2])
                    value = jnp.where(var_zero, table[2][0], rest)
                    for power in (1, 0):
                        a, b, c = table[power]
                        value = value * arg + jnp.where(var_zero, a, jnp.where(var_one, b, c))
                    pieces.append(parts((value * jnp.exp2(arg)).reshape(PART, side)))
                rows = slice(row * side, (row + 1) * side)
                for each, out in enumerate((high, low)):
                    tile = jnp.concatenate([piece[each] for piece in pieces], axis=0)
                    out[rows, cols] = tile
                    if row < col:
                        out[cols, rows] = jnp.transpose(tile)

    def apply(leaf, high, low):
        vec_hi, vec_lo = parts(tree_vec[leaf])
        both = dot(jnp.concatenate([vec_hi, vec_lo], axis=0), high[...])
        near[leaf] = both[:nvec] + both[nvec:] + dot(vec_hi, low[...])

    for each in later:
        each[...] = jnp.zeros_like(each)

    def two_leaves(step, carry):
        apply(jnp.maximum(2 * step - 1, 0), *later)
        values(*even, *sooner)
        place_leaf(2 * step + 1, *odd)
        apply(2 * step, *sooner)
        values(*odd, *later)
        place_leaf(2 * step + 2, *even)
        return carry

    place_leaf(0, *even)

    lax.fori_loop(0, leaves // 4, two_leaves, 0)
    half = slice(0, leaves // 2 - 1)
    first = pltpu.make_async_copy(near.at[half], near_out.at[half], sems.at[0])
    first.start()
    lax.fori_loop(leaves // 4, leaves // 2, two_leaves, 0)
    inverse[...] = (slots[:chunks] + slots[chunks:] * WIDE).astype(jnp.int32)
    leave = pltpu.make_async_copy(inverse, inverse_out, sems.at[3])
    leave.start()
    apply(leaves - 1, *later)
    half = slice(leaves // 2 - 1, leaves)
    second = pltpu.make_async_copy(near.at[half], near_out.at[half], sems.at[1])
    second.start()
    for copy in (leave, first, second):
        copy.wait()


def far_kernel(groups, subtrees, *refs):
    place, leaf_src, leaf_count, node_src, node_count = refs[:5]
    leaf_packs, refs = refs[5 : 5 + groups], refs[5 + groups :]
    given, out_at, held = refs[:10], refs[10], refs[11:21]
    leaf_all, source, coef, twice, cols, out, rows, srcs, dsts, sems = refs[21:]
    own = leaf_packs[0].shape[0]
    grp_pos = lax.rem(place[0], groups)
    owner = [lax.rem(grp_pos - shift + groups, groups) for shift in range(groups)]
    arrive = [leaf_all.at[pl.ds(each * own, own)] for each in owner]
    copies = fetch(list(zip(leaf_packs + given, arrive + list(held))), sems)
    leaf_copies, copies = copies[:groups], [None] + copies[groups:]
    tree_all, leaf_skel, node_skel, sub_skel, tables = held[:5]
    leaf_maps, node_maps, bases, near, inverse = held[5:]
    count_rows(rows)
    leaves, nvec, block = near.shape
    rank = bases.shape[1]
    nodes = tree_all.shape[0]
    pairs = leaf_all.shape[0]
    node_at = 2 * pairs
    beside = 3 * groups
    sub_at = node_at + beside
    blank = sub_at + subtrees
    sub_pos = lax.div(place[0], groups)
    left = lax.broadcasted_iota(jnp.int32, (PACK_ROWS, 2 * rank), 1) < rank

    def list_leaf(leaf, at):
        count = leaf_count[leaf]

        def one(step, carry):
            srcs[2 * (at + step)] = leaf_src[leaf, 2 * step]
            second = jnp.where(2 * step + 1 < count, leaf_src[leaf, 2 * step + 1], blank)
            srcs[2 * (at + step) + 1] = second
            dsts[at + step] = leaf
            return carry

        steps = (count + 1) // 2
        lax.fori_loop(0, steps, one, 0)
        return at + steps

    size = lax.fori_loop(0, leaves, list_leaf, 0)
    count = node_count[0]

    def list_node(step, carry):
        srcs[2 * (size + step)] = node_at + node_src[0, 2 * step]
        second = jnp.where(2 * step + 1 < count, node_at + node_src[0, 2 * step + 1], blank)
        srcs[2 * (size + step) + 1] = second
        dsts[size + step] = leaves
        return carry

    steps = (count + 1) // 2
    lax.fori_loop(0, steps, list_node, 0)

    def list_sub(sub, at):
        srcs[at] = sub_at + sub
        dsts[at // 2] = leaves + 1
        return at + jnp.where(jnp.abs(sub - sub_pos) >= 2, 1, 0)

    ends = lax.fori_loop(0, subtrees, list_sub, 2 * (size + steps))
    srcs[ends] = blank
    dsts[ends // 2] = leaves + 1
    ends = (ends + 1) // 2
    for each in range(AT_ONCE):
        srcs[2 * (ends + each)] = blank
        srcs[2 * (ends + each) + 1] = blank
        dsts[ends + each] = leaves + 1

    for copy in leaf_copies:
        copy.wait()

    def both_leaves(pair, carry):
        packs = leaf_all[pair]
        turned = pltpu.roll(packs, rank, 1)
        twice[2 * pair] = jnp.where(left, packs, turned)
        twice[2 * pair + 1] = jnp.where(left, turned, packs)
        return carry

    lax.fori_loop(0, pairs, both_leaves, 0, unroll=4)
    copies[1].wait()

    def both_node(each, carry):
        packs = tree_all[jnp.clip((sub_pos - 1) * groups + each, 0, nodes - 1)]
        twice[node_at + each] = jnp.where(left, packs, pltpu.roll(packs, rank, 1))
        return carry

    lax.fori_loop(0, beside, both_node, 0, unroll=4)

    def both_sub(sub, carry):
        total = tree_all[sub * groups, :nvec]
        for each in range(1, groups):
            total = total + tree_all[sub * groups + each, :nvec]
        packs = jnp.concatenate([total, tree_all[sub * groups, nvec:]], axis=0)
        twice[sub_at + sub] = jnp.where(left, pltpu.roll(packs, rank, 1), packs)
        return carry

    lax.fori_loop(0, subtrees, both_sub, 0, unroll=2)
    twice[blank] = jnp.zeros_like(twice[blank])
    coef[...] = jnp.zeros_like(coef)
    for copy in copies[2:6]:
        copy.wait()

    def upright(skel, at):
        for axis in range(2):
            row = jnp.broadcast_to(skel[axis : axis + 1], (2 * rank, rank))
            cols[at, axis] = jnp.transpose(row)

    def upright_leaf(leaf, carry):
        upright(leaf_skel[leaf], leaf)
        return carry

    lax.fori_loop(0, leaves, upright_leaf, 0, unroll=4)
    upright(node_skel[0], leaves)
    upright(sub_skel[0], leaves + 1)

    def couple(step, carry):
        terms = []
        for each in range(AT_ONCE):
            item = step * AT_ONCE + each
            packs = jnp.where(left, twice[srcs[2 * item]], twice[srcs[2 * item + 1]])
            target = dsts[item]
            diff_x = cols[target, 0] - packs[nvec : nvec + 1]
            diff_y = cols[target, 1] - packs[nvec + 1 : nvec + 2]
            square = (diff_x * diff_x + diff_y * diff_y) * tables[0]
            arg = square * lax.rsqrt(TINY - square)
            value = tables[5]
            for power in (4, 3, 2, 1):
                value = value * arg + tables[power]
            value = value * jnp.exp2(arg)
            terms.append((target, product(packs[:nvec], value, True)))
        for target, total in terms:
            coef[target] += total
        return carry

    lax.fori_loop(0, (ends + AT_ONCE - 1) // AT_ONCE, couple, 0)
    for copy in copies[6:]:
        copy.wait()
    down_node = coef[leaves] + product(coef[leaves + 1], node_maps[0], True)
    for leaf in range(leaves):
        down_leaf = coef[leaf] + product(down_node, leaf_maps[leaf], True)
        whole = near[leaf] + product(down_leaf, bases[leaf])
        for each in range(block // WIDE):
            fill(
                source,
                whole[:, each * WIDE : (each + 1) * WIDE],
                (leaf * (block // WIDE) + each) * nvec,
                nvec,
            )

    def scatter(each, carry):
        at = pl.multiple_of(each * block, block)
        out[:, pl.ds(at, block)] = pick(rows, source, leaf_index(inverse, each, block), nvec)
        return carry

    steps = inverse.shape[0] * WIDE // block
    segments = 2
    leaving = []
    for each in range(segments):
        start, stop = each * steps // segments, (each + 1) * steps // segments
        lax.fori_loop(start, stop, scatter, 0, unroll=8)
        span = slice(start * block, stop * block)
        leaving.append(pltpu.make_async_copy(out.at[:, span], out_at.at[:, span], sems.at[each]))
        leaving[-1].start()
    for copy in leaving:
        copy.wait()


def skeleton_tables(rank):
    scale, poly = make_tables(1.0 / math.sqrt(rank))
    var = np.arange(rank) % 3
    rows, cols = var[:, None], np.tile(var, 2)[None, :]
    return np.stack([scale[rows, cols]] + [poly[power][rows, cols] for power in range(5)]).astype(
        np.float32
    )


def shards(
    vectors,
    coords,
    perm,
    bases,
    leaf_maps,
    node_maps,
    leaf_skel,
    node_skel,
    sub_skel,
    leaf_src,
    leaf_count,
    node_src,
    node_count,
):
    nvec, rows_dev = vectors.shape
    leaves, rank, block = bases.shape
    groups = lax.axis_size("grp")
    subtrees = lax.axis_size("leaf")
    nodes = groups * subtrees
    sub_pos = lax.axis_index("leaf")
    device_pos = sub_pos * groups + lax.axis_index("grp")
    chunks = rows_dev // WIDE
    vmem = pl.BlockSpec(memory_space=pltpu.VMEM)
    smem = pl.BlockSpec(memory_space=pltpu.SMEM)
    hbm = pl.BlockSpec(memory_space=pltpu.HBM)
    anywhere = pl.BlockSpec(memory_space=pl.ANY)
    params = pltpu.CompilerParams(vmem_limit_bytes=60 * 1024 * 1024)
    order = perm.reshape(rows_dev // 128, 128)

    def like(*arrays):
        return [pltpu.VMEM(each.shape, each.dtype) for each in arrays]

    given = (vectors, order, bases, leaf_maps, node_maps, leaf_skel, node_skel, sub_skel)
    tree_vec, leaf_pack, tree_pack = pl.pallas_call(
        up_kernel,
        out_shape=(
            jax.ShapeDtypeStruct((leaves, nvec, block), F32),
            jax.ShapeDtypeStruct((leaves // 2, PACK_ROWS, 2 * rank), F32),
            jax.ShapeDtypeStruct((nodes, PACK_ROWS, 2 * rank), F32),
        ),
        in_specs=[hbm] * 8,
        out_specs=(hbm, vmem, vmem),
        scratch_shapes=like(*given)
        + [
            pltpu.VMEM((leaves, nvec, block), F32),
            pltpu.VMEM((chunks * nvec, 2 * WIDE), BF16),
            pltpu.VMEM((WIDE, block), jnp.int16),
            pltpu.SemaphoreType.DMA((9,)),
        ],
        compiler_params=params,
        name="up",
    )(*given)
    tree_all = lax.all_to_all(tree_pack, ("leaf", "grp"), 0, 0, tiled=True)
    leaf_all = [leaf_pack] + [
        lax.ppermute(leaf_pack, "grp", [(each, (each + shift) % groups) for each in range(groups)])
        for shift in range(1, groups)
    ]
    shift = (device_pos * (rows_dev % 3) % 3).astype(jnp.int32).reshape(1)
    near, inverse = pl.pallas_call(
        near_kernel,
        out_shape=(
            jax.ShapeDtypeStruct((leaves, nvec, block), F32),
            jax.ShapeDtypeStruct((chunks, WIDE), jnp.int32),
        ),
        in_specs=[smem, hbm, hbm, hbm],
        out_specs=(hbm,) * 2,
        scratch_shapes=like(coords, order, tree_vec)
        + [
            pltpu.VMEM((leaves, nvec, block), F32),
            pltpu.VMEM((chunks, WIDE), jnp.int32),
            pltpu.VMEM((2 * chunks, WIDE), F32),
            pltpu.VMEM((6 * chunks, WIDE), BF16),
            pltpu.VMEM((WIDE, block), jnp.int16),
            pltpu.VMEM((2 * chunks, WIDE), F32),
            *[
                pltpu.VMEM((3, 8, block), F32),
                pltpu.VMEM((3, block // 8, 8, 128), F32),
            ]
            * 2,
            *[pltpu.VMEM((block, block), BF16)] * 4,
            pltpu.SemaphoreType.DMA((4,)),
        ],
        compiler_params=params,
        cost_estimate=pl.CostEstimate(
            flops=128 * leaves * block * block,
            bytes_accessed=8 * leaves * nvec * block,
            transcendentals=leaves * block * block,
        ),
        name="near",
    )(shift, coords, order, tree_vec)
    tables = jnp.asarray(skeleton_tables(rank))
    given = (tree_all, leaf_skel, node_skel, sub_skel, tables)
    given = given + (leaf_maps, node_maps, bases, near, inverse)
    items = (leaf_src.size + node_src.size + subtrees + 2) // 2 + AT_ONCE
    sources = groups * leaves + 3 * groups + subtrees + 1
    return pl.pallas_call(
        functools.partial(far_kernel, groups, subtrees),
        out_shape=jax.ShapeDtypeStruct((nvec, rows_dev), F32),
        in_specs=[smem] * 5 + [anywhere] * (groups + 1) + [hbm] * 9,
        out_specs=hbm,
        scratch_shapes=like(*given)
        + [
            pltpu.VMEM((groups * leaf_pack.shape[0],) + leaf_pack.shape[1:], F32),
            pltpu.VMEM((chunks * nvec, 2 * WIDE), BF16),
            pltpu.VMEM((leaves + 2, nvec, rank), F32),
            pltpu.VMEM((sources, PACK_ROWS, 2 * rank), F32),
            pltpu.VMEM((leaves + 2, 2, rank, 2 * rank), F32),
            pltpu.VMEM((nvec, rows_dev), F32),
            pltpu.VMEM((WIDE, block), jnp.int16),
            pltpu.SMEM((2 * items,), jnp.int32),
            pltpu.SMEM((items,), jnp.int32),
            pltpu.SemaphoreType.DMA((10 + groups,)),
        ],
        compiler_params=params,
        name="far",
    )(
        device_pos.astype(jnp.int32).reshape(1),
        leaf_src,
        leaf_count,
        node_src,
        node_count,
        *leaf_all,
        *given,
    )


def solution(mesh):
    placed = (
        P(None, ("leaf", "grp")),
        P(None, ("leaf", "grp")),
        P(("leaf", "grp")),
        P(("leaf", "grp"), None, None),
        P(("leaf", "grp"), None, None),
        P(("leaf", "grp"), None, None),
        P(("leaf", "grp"), None, None),
        P(("leaf", "grp"), None, None),
        P("leaf", None, None),
        P(("leaf", "grp"), None),
        P(("leaf", "grp")),
        P(("leaf", "grp"), None),
        P(("leaf", "grp")),
    )
    return jax.shard_map(
        shards, mesh=mesh, in_specs=placed, out_specs=P(None, ("leaf", "grp")), check_vma=False
    )
```

```python
import functools
import math

import jax
import jax.numpy as jnp
import numpy as np
from jax import lax
from jax.experimental import pallas as pl
from jax.experimental.pallas import tpu as pltpu
from jax.sharding import PartitionSpec as P

F32 = jnp.float32
BF16 = jnp.bfloat16
WIDE = 128
SHIFT = 7
LOG2E = math.log2(math.e)
TINY = 1e-37
PACK_ROWS = 24
PART = 32
AT_ONCE = 16


def make_tables(norm):
    smooth = [0, 2, 4]
    sigmas = [1.0, 0.8, 1.2]
    rho = [[1.0, 0.5, 0.3], [0.5, 1.0, 0.4], [0.3, 0.4, 1.0]]
    scale = np.zeros((3, 3))
    poly = np.zeros((5, 3, 3))
    for first in range(3):
        for second in range(3):
            order = (smooth[first] + smooth[second]) // 2
            scale[first, second] = -(2.0 * order + 1.0) * (LOG2E / 0.3) ** 2
            amp = sigmas[first] * sigmas[second] * rho[first][second] * norm
            for power in range(order + 1):
                kterm = order - power
                coeff = math.factorial(order) / math.factorial(2 * order)
                coeff = (
                    coeff
                    * math.factorial(order + kterm)
                    / (math.factorial(kterm) * math.factorial(order - kterm))
                )
                poly[power, first, second] = amp * coeff * 2.0**power * (-1.0 / LOG2E) ** power
    return scale, poly


def dot(one, two, turned=False):
    dims = (((1,), (1 if turned else 0,)), ((), ()))
    return lax.dot_general(one, two, dims, preferred_element_type=F32)


def parts(value):
    high = value.astype(BF16)
    return high, (value - high.astype(F32)).astype(BF16)


def product(one, two, turned=False):
    rows = one.shape[0]
    one_hi, one_lo = parts(one)
    two_hi, two_lo = parts(two)
    both = dot(jnp.concatenate([one_hi, one_lo], axis=0), two_hi, turned)
    return both[:rows] + both[rows:] + dot(one_hi, two_lo, turned)


def count_rows(rows):
    rows[...] = lax.broadcasted_iota(jnp.int32, rows.shape, 0).astype(jnp.int16)


def one_hot(rows, low):
    count = low.shape[1]
    low = jnp.broadcast_to(low, (16, count)).astype(jnp.int16)[None]
    same = rows[:, :count].reshape(WIDE // 16, 16, count) == low
    return jnp.where(same, jnp.bfloat16(1), jnp.bfloat16(0)).reshape(WIDE, count)


def fill(source, value, at, nvec):
    high, low = parts(value)
    source[pl.ds(at, nvec), :WIDE] = high
    source[pl.ds(at, nvec), WIDE:] = low


def pick(rows, source, index, nvec):
    count = index.shape[1]
    hot = one_hot(rows, index & (WIDE - 1))
    hot = jnp.concatenate([hot, hot], axis=0)
    chunk = jnp.broadcast_to(index >> SHIFT, (8, count))[None]
    out = jnp.zeros((nvec // 8, 8, count), F32)
    chunks = source.shape[0] // nvec
    found = dot(source[...], hot).reshape(chunks, nvec // 8, 8, count)
    for each in range(chunks):
        out = jnp.where(chunk == each, found[each], out)
    return out.reshape(nvec, count)


def leaf_index(perm, leaf, block):
    rows = block // 128
    return jnp.concatenate([perm[pl.ds(leaf * rows + each, 1), :] for each in range(rows)], axis=1)


def fetch(pairs, sems):
    copies = [pltpu.make_async_copy(src, dst, sems.at[each]) for each, (src, dst) in enumerate(pairs)]
    for copy in copies:
        copy.start()
    return copies


def up_kernel(*refs):
    given, (tree_out, leaf_pack, tree_pack) = refs[:8], refs[8:11]
    held = refs[11:19]
    tree_vec, source, rows, sems = refs[19:]
    count_rows(rows)
    copies = fetch(list(zip(given, held)), sems)
    vec, perm, bases, leaf_maps, node_maps, leaf_skel, node_skel, sub_skel = held
    leaves, nvec, block = tree_vec.shape
    rank = bases.shape[1]
    copies[0].wait()
    for each in range(vec.shape[1] // WIDE):
        fill(source, vec[:, each * WIDE : (each + 1) * WIDE], each * nvec, nvec)
    copies[1].wait()

    def gather(leaf, carry):
        tree_vec[leaf] = pick(rows, source, leaf_index(perm, leaf, block), nvec)
        return carry

    lax.fori_loop(0, leaves, gather, 0, unroll=16)
    leave = pltpu.make_async_copy(tree_vec, tree_out, sems.at[len(copies)])
    leave.start()
    for copy in copies[2:]:
        copy.wait()
    up_node = jnp.zeros((nvec, rank), F32)
    blank = jnp.zeros((PACK_ROWS - nvec - 2, 2 * rank), F32)
    for leaf in range(0, leaves, 2):
        up = [product(tree_vec[leaf + each], bases[leaf + each], True) for each in range(2)]
        leaf_pack[leaf // 2] = jnp.concatenate(
            [
                jnp.concatenate(up, axis=1),
                jnp.concatenate([leaf_skel[leaf], leaf_skel[leaf + 1]], axis=1),
                blank,
            ],
            axis=0,
        )
        for each in range(2):
            up_node = up_node + product(up[each], leaf_maps[leaf + each])
    up_sub = product(up_node, node_maps[0])
    packed = jnp.concatenate(
        [
            jnp.concatenate([up_node, up_sub], axis=1),
            jnp.concatenate([node_skel[0], sub_skel[0]], axis=1),
            blank,
        ],
        axis=0,
    )

    def spread(each, carry):
        tree_pack[each] = packed
        return carry

    lax.fori_loop(0, tree_pack.shape[0], spread, 0)
    leave.wait()


def near_kernel(shift, *refs):
    given, (near_out, inverse_out) = refs[:3], refs[3:5]
    held = refs[5:8]
    near, inverse, flat, source, rows, slots = refs[8:14]
    even, odd, sooner, later, sems = refs[14:16], refs[16:18], refs[18:20], refs[20:22], refs[22]
    copies = fetch(list(zip(given, held)), sems)
    crd, perm, tree_vec = held
    count_rows(rows)
    leaves, nvec, block = tree_vec.shape
    chunks = crd.shape[1] // WIDE
    scale, poly = make_tables(1.0 / math.sqrt(block))
    slope = scale[0, 1] - scale[0, 0]
    copies[0].wait()
    for axis in range(2):
        for each in range(chunks):
            row = axis * chunks + each
            flat[row : row + 1, :] = crd[axis : axis + 1, each * WIDE : (each + 1) * WIDE]
    rest = flat[...]
    for piece in range(3):
        rounded = rest.astype(BF16)
        source[piece * 2 * chunks : (piece + 1) * 2 * chunks, :] = rounded
        rest = rest - rounded.astype(F32)
    slots[...] = jnp.zeros_like(slots)
    copies[1].wait()
    side = 128
    tiles = block // side

    def place_leaf(leaf, across, down):
        live = jnp.where(leaf < leaves, 1.0, 0.0)
        leaf = jnp.minimum(leaf, leaves - 1)
        index = leaf_index(perm, leaf, block)
        hot = one_hot(rows, index & (WIDE - 1))
        found = dot(source[...], hot)
        found = (
            found[: 2 * chunks] + found[2 * chunks : 4 * chunks] + found[4 * chunks :]
        )
        mine = lax.broadcasted_iota(jnp.int32, (chunks, block), 0) == index >> SHIFT
        lane = lax.broadcasted_iota(jnp.int32, (chunks, block), 1) + leaf * block
        lane_low = (lane & (WIDE - 1)).astype(F32) * live
        lane_high = (lane >> SHIFT).astype(F32) * live
        marks = jnp.concatenate(
            [jnp.where(mine, lane_low, 0.0), jnp.where(mine, lane_high, 0.0)], axis=0
        ).astype(BF16)
        slots[...] += dot(marks, hot, True)
        row_x = jnp.sum(jnp.where(mine, found[:chunks], 0.0), axis=0, keepdims=True)
        row_y = jnp.sum(jnp.where(mine, found[chunks:], 0.0), axis=0, keepdims=True)
        moved = index + shift[0]
        kind = moved - 3 * ((moved * 43691) >> 17)
        row_w = kind.astype(F32) * slope
        for place, row in enumerate((row_x, row_y, row_w)):
            across[place] = jnp.broadcast_to(row, (8, block))
            turned = jnp.transpose(jnp.broadcast_to(row, (side, block)))
            down[place] = turned.reshape(block // 8, 8, side)

    copies[2].wait()

    def values(across, down, high, low):
        for col in range(tiles):
            cols = slice(col * side, (col + 1) * side)
            over_x, over_y, over_w = [across[each, :, cols] for each in range(3)]
            over_zero, over_one = over_w > 0.5 * slope, over_w > 1.5 * slope

            def across_table(power, first):
                zero, one, two = [float(each) for each in poly[power, first]]
                return jnp.where(over_zero, zero, jnp.where(over_one, one, two))[None]

            table = [[across_table(power, first) for first in range(3)] for power in range(5)]
            over_w = (over_w + float(scale[0, 0]))[None]
            over_x, over_y = over_x[None], over_y[None]
            for row in range(col + 1):
                pieces = []
                for part in range(side // PART):
                    first = row * side + part * PART
                    at = slice(first // 8, (first + PART) // 8)
                    diff_x = down[0, at] - over_x
                    diff_y = down[1, at] - over_y
                    down_w = down[2, at]
                    var_zero, var_one = down_w > 0.5 * slope, down_w > 1.5 * slope
                    square = (diff_x * diff_x + diff_y * diff_y) * (down_w + over_w)
                    arg = square * lax.rsqrt(TINY - square)
                    value = jnp.where(var_one, table[3][1], table[4][2] * arg + table[3][2])
                    rest = value * arg + jnp.where(var_one, table[2][1], table[2][2])
                    value = jnp.where(var_zero, table[2][0], rest)
                    for power in (1, 0):
                        a, b, c = table[power]
                        value = value * arg + jnp.where(var_zero, a, jnp.where(var_one, b, c))
                    pieces.append(parts((value * jnp.exp2(arg)).reshape(PART, side)))
                rows = slice(row * side, (row + 1) * side)
                for each, out in enumerate((high, low)):
                    tile = jnp.concatenate([piece[each] for piece in pieces], axis=0)
                    out[rows, cols] = tile
                    if row < col:
                        out[cols, rows] = jnp.transpose(tile)

    def apply(leaf, high, low):
        vec_hi, vec_lo = parts(tree_vec[leaf])
        both = dot(jnp.concatenate([vec_hi, vec_lo], axis=0), high[...])
        near[leaf] = both[:nvec] + both[nvec:] + dot(vec_hi, low[...])

    for each in later:
        each[...] = jnp.zeros_like(each)

    def two_leaves(step, carry):
        apply(jnp.maximum(2 * step - 1, 0), *later)
        values(*even, *sooner)
        place_leaf(2 * step + 1, *odd)
        apply(2 * step, *sooner)
        values(*odd, *later)
        place_leaf(2 * step + 2, *even)
        return carry

    place_leaf(0, *even)

    lax.fori_loop(0, leaves // 4, two_leaves, 0)
    half = slice(0, leaves // 2 - 1)
    first = pltpu.make_async_copy(near.at[half], near_out.at[half], sems.at[0])
    first.start()
    lax.fori_loop(leaves // 4, leaves // 2, two_leaves, 0)
    inverse[...] = (slots[:chunks] + slots[chunks:] * WIDE).astype(jnp.int32)
    leave = pltpu.make_async_copy(inverse, inverse_out, sems.at[3])
    leave.start()
    apply(leaves - 1, *later)
    half = slice(leaves // 2 - 1, leaves)
    second = pltpu.make_async_copy(near.at[half], near_out.at[half], sems.at[1])
    second.start()
    for copy in (leave, first, second):
        copy.wait()


def far_kernel(groups, subtrees, *refs):
    place, leaf_src, leaf_count, node_src, node_count = refs[:5]
    leaf_packs, refs = refs[5 : 5 + groups], refs[5 + groups :]
    given, out_at, held = refs[:10], refs[10], refs[11:21]
    leaf_all, source, coef, twice, cols, out, rows, srcs, dsts, sems = refs[21:]
    own = leaf_packs[0].shape[0]
    grp_pos = lax.rem(place[0], groups)
    owner = [lax.rem(grp_pos - shift + groups, groups) for shift in range(groups)]
    arrive = [leaf_all.at[pl.ds(each * own, own)] for each in owner]
    copies = fetch(list(zip(leaf_packs + given, arrive + list(held))), sems)
    leaf_copies, copies = copies[:groups], [None] + copies[groups:]
    tree_all, leaf_skel, node_skel, sub_skel, tables = held[:5]
    leaf_maps, node_maps, bases, near, inverse = held[5:]
    count_rows(rows)
    leaves, nvec, block = near.shape
    rank = bases.shape[1]
    nodes = tree_all.shape[0]
    pairs = leaf_all.shape[0]
    node_at = 2 * pairs
    beside = 3 * groups
    sub_at = node_at + beside
    blank = sub_at + subtrees
    sub_pos = lax.div(place[0], groups)
    left = lax.broadcasted_iota(jnp.int32, (PACK_ROWS, 2 * rank), 1) < rank

    def list_leaf(leaf, at):
        count = leaf_count[leaf]

        def one(step, carry):
            srcs[2 * (at + step)] = leaf_src[leaf, 2 * step]
            second = jnp.where(2 * step + 1 < count, leaf_src[leaf, 2 * step + 1], blank)
            srcs[2 * (at + step) + 1] = second
            dsts[at + step] = leaf
            return carry

        steps = (count + 1) // 2
        lax.fori_loop(0, steps, one, 0)
        return at + steps

    size = lax.fori_loop(0, leaves, list_leaf, 0)
    count = node_count[0]

    def list_node(step, carry):
        srcs[2 * (size + step)] = node_at + node_src[0, 2 * step]
        second = jnp.where(2 * step + 1 < count, node_at + node_src[0, 2 * step + 1], blank)
        srcs[2 * (size + step) + 1] = second
        dsts[size + step] = leaves
        return carry

    steps = (count + 1) // 2
    lax.fori_loop(0, steps, list_node, 0)

    def list_sub(sub, at):
        srcs[at] = sub_at + sub
        dsts[at // 2] = leaves + 1
        return at + jnp.where(jnp.abs(sub - sub_pos) >= 2, 1, 0)

    ends = lax.fori_loop(0, subtrees, list_sub, 2 * (size + steps))
    srcs[ends] = blank
    dsts[ends // 2] = leaves + 1
    ends = (ends + 1) // 2
    for each in range(AT_ONCE):
        srcs[2 * (ends + each)] = blank
        srcs[2 * (ends + each) + 1] = blank
        dsts[ends + each] = leaves + 1

    for copy in leaf_copies:
        copy.wait()

    def both_leaves(pair, carry):
        packs = leaf_all[pair]
        turned = pltpu.roll(packs, rank, 1)
        twice[2 * pair] = jnp.where(left, packs, turned)
        twice[2 * pair + 1] = jnp.where(left, turned, packs)
        return carry

    lax.fori_loop(0, pairs, both_leaves, 0, unroll=4)
    copies[1].wait()

    def both_node(each, carry):
        packs = tree_all[jnp.clip((sub_pos - 1) * groups + each, 0, nodes - 1)]
        twice[node_at + each] = jnp.where(left, packs, pltpu.roll(packs, rank, 1))
        return carry

    lax.fori_loop(0, beside, both_node, 0, unroll=4)

    def both_sub(sub, carry):
        total = tree_all[sub * groups, :nvec]
        for each in range(1, groups):
            total = total + tree_all[sub * groups + each, :nvec]
        packs = jnp.concatenate([total, tree_all[sub * groups, nvec:]], axis=0)
        twice[sub_at + sub] = jnp.where(left, pltpu.roll(packs, rank, 1), packs)
        return carry

    lax.fori_loop(0, subtrees, both_sub, 0, unroll=2)
    twice[blank] = jnp.zeros_like(twice[blank])
    coef[...] = jnp.zeros_like(coef)
    for copy in copies[2:6]:
        copy.wait()

    def upright(skel, at):
        for axis in range(2):
            row = jnp.broadcast_to(skel[axis : axis + 1], (2 * rank, rank))
            cols[at, axis] = jnp.transpose(row)

    def upright_leaf(leaf, carry):
        upright(leaf_skel[leaf], leaf)
        return carry

    lax.fori_loop(0, leaves, upright_leaf, 0, unroll=4)
    upright(node_skel[0], leaves)
    upright(sub_skel[0], leaves + 1)

    def couple(step, carry):
        terms = []
        for each in range(AT_ONCE):
            item = step * AT_ONCE + each
            packs = jnp.where(left, twice[srcs[2 * item]], twice[srcs[2 * item + 1]])
            target = dsts[item]
            diff_x = cols[target, 0] - packs[nvec : nvec + 1]
            diff_y = cols[target, 1] - packs[nvec + 1 : nvec + 2]
            square = (diff_x * diff_x + diff_y * diff_y) * tables[0]
            arg = square * lax.rsqrt(TINY - square)
            value = tables[5]
            for power in (4, 3, 2, 1):
                value = value * arg + tables[power]
            value = value * jnp.exp2(arg)
            terms.append((target, product(packs[:nvec], value, True)))
        for target, total in terms:
            coef[target] += total
        return carry

    lax.fori_loop(0, (ends + AT_ONCE - 1) // AT_ONCE, couple, 0)
    for copy in copies[6:]:
        copy.wait()
    down_node = coef[leaves] + product(coef[leaves + 1], node_maps[0], True)
    for leaf in range(leaves):
        down_leaf = coef[leaf] + product(down_node, leaf_maps[leaf], True)
        whole = near[leaf] + product(down_leaf, bases[leaf])
        for each in range(block // WIDE):
            fill(
                source,
                whole[:, each * WIDE : (each + 1) * WIDE],
                (leaf * (block // WIDE) + each) * nvec,
                nvec,
            )

    def scatter(each, carry):
        at = pl.multiple_of(each * block, block)
        out[:, pl.ds(at, block)] = pick(rows, source, leaf_index(inverse, each, block), nvec)
        return carry

    steps = inverse.shape[0] * WIDE // block
    segments = 2
    leaving = []
    for each in range(segments):
        start, stop = each * steps // segments, (each + 1) * steps // segments
        lax.fori_loop(start, stop, scatter, 0, unroll=8)
        span = slice(start * block, stop * block)
        leaving.append(pltpu.make_async_copy(out.at[:, span], out_at.at[:, span], sems.at[each]))
        leaving[-1].start()
    for copy in leaving:
        copy.wait()


def skeleton_tables(rank):
    scale, poly = make_tables(1.0 / math.sqrt(rank))
    var = np.arange(rank) % 3
    rows, cols = var[:, None], np.tile(var, 2)[None, :]
    return np.stack([scale[rows, cols]] + [poly[power][rows, cols] for power in range(5)]).astype(
        np.float32
    )


def shards(
    vectors,
    coords,
    perm,
    bases,
    leaf_maps,
    node_maps,
    leaf_skel,
    node_skel,
    sub_skel,
    leaf_src,
    leaf_count,
    node_src,
    node_count,
):
    nvec, rows_dev = vectors.shape
    leaves, rank, block = bases.shape
    groups = lax.axis_size("grp")
    subtrees = lax.axis_size("leaf")
    nodes = groups * subtrees
    sub_pos = lax.axis_index("leaf")
    device_pos = sub_pos * groups + lax.axis_index("grp")
    chunks = rows_dev // WIDE
    vmem = pl.BlockSpec(memory_space=pltpu.VMEM)
    smem = pl.BlockSpec(memory_space=pltpu.SMEM)
    hbm = pl.BlockSpec(memory_space=pltpu.HBM)
    anywhere = pl.BlockSpec(memory_space=pl.ANY)
    params = pltpu.CompilerParams(vmem_limit_bytes=60 * 1024 * 1024)
    order = perm.reshape(rows_dev // 128, 128)

    def like(*arrays):
        return [pltpu.VMEM(each.shape, each.dtype) for each in arrays]

    given = (vectors, order, bases, leaf_maps, node_maps, leaf_skel, node_skel, sub_skel)
    tree_vec, leaf_pack, tree_pack = pl.pallas_call(
        up_kernel,
        out_shape=(
            jax.ShapeDtypeStruct((leaves, nvec, block), F32),
            jax.ShapeDtypeStruct((leaves // 2, PACK_ROWS, 2 * rank), F32),
            jax.ShapeDtypeStruct((nodes, PACK_ROWS, 2 * rank), F32),
        ),
        in_specs=[hbm] * 8,
        out_specs=(hbm, vmem, vmem),
        scratch_shapes=like(*given)
        + [
            pltpu.VMEM((leaves, nvec, block), F32),
            pltpu.VMEM((chunks * nvec, 2 * WIDE), BF16),
            pltpu.VMEM((WIDE, block), jnp.int16),
            pltpu.SemaphoreType.DMA((9,)),
        ],
        compiler_params=params,
        name="up",
    )(*given)
    tree_all = lax.all_to_all(tree_pack, ("leaf", "grp"), 0, 0, tiled=True)
    leaf_all = [leaf_pack] + [
        lax.ppermute(leaf_pack, "grp", [(each, (each + shift) % groups) for each in range(groups)])
        for shift in range(1, groups)
    ]
    shift = (device_pos * (rows_dev % 3) % 3).astype(jnp.int32).reshape(1)
    near, inverse = pl.pallas_call(
        near_kernel,
        out_shape=(
            jax.ShapeDtypeStruct((leaves, nvec, block), F32),
            jax.ShapeDtypeStruct((chunks, WIDE), jnp.int32),
        ),
        in_specs=[smem, hbm, hbm, hbm],
        out_specs=(hbm,) * 2,
        scratch_shapes=like(coords, order, tree_vec)
        + [
            pltpu.VMEM((leaves, nvec, block), F32),
            pltpu.VMEM((chunks, WIDE), jnp.int32),
            pltpu.VMEM((2 * chunks, WIDE), F32),
            pltpu.VMEM((6 * chunks, WIDE), BF16),
            pltpu.VMEM((WIDE, block), jnp.int16),
            pltpu.VMEM((2 * chunks, WIDE), F32),
            *[
                pltpu.VMEM((3, 8, block), F32),
                pltpu.VMEM((3, block // 8, 8, 128), F32),
            ]
            * 2,
            *[pltpu.VMEM((block, block), BF16)] * 4,
            pltpu.SemaphoreType.DMA((4,)),
        ],
        compiler_params=params,
        cost_estimate=pl.CostEstimate(
            flops=128 * leaves * block * block,
            bytes_accessed=8 * leaves * nvec * block,
            transcendentals=leaves * block * block,
        ),
        name="near",
    )(shift, coords, order, tree_vec)
    tables = jnp.asarray(skeleton_tables(rank))
    given = (tree_all, leaf_skel, node_skel, sub_skel, tables)
    given = given + (leaf_maps, node_maps, bases, near, inverse)
    items = (leaf_src.size + node_src.size + subtrees + 2) // 2 + AT_ONCE
    sources = groups * leaves + 3 * groups + subtrees + 1
    return pl.pallas_call(
        functools.partial(far_kernel, groups, subtrees),
        out_shape=jax.ShapeDtypeStruct((nvec, rows_dev), F32),
        in_specs=[smem] * 5 + [anywhere] * (groups + 1) + [hbm] * 9,
        out_specs=hbm,
        scratch_shapes=like(*given)
        + [
            pltpu.VMEM((groups * leaf_pack.shape[0],) + leaf_pack.shape[1:], F32),
            pltpu.VMEM((chunks * nvec, 2 * WIDE), BF16),
            pltpu.VMEM((leaves + 2, nvec, rank), F32),
            pltpu.VMEM((sources, PACK_ROWS, 2 * rank), F32),
            pltpu.VMEM((leaves + 2, 2, rank, 2 * rank), F32),
            pltpu.VMEM((nvec, rows_dev), F32),
            pltpu.VMEM((WIDE, block), jnp.int16),
            pltpu.SMEM((2 * items,), jnp.int32),
            pltpu.SMEM((items,), jnp.int32),
            pltpu.SemaphoreType.DMA((10 + groups,)),
        ],
        compiler_params=params,
        name="far",
    )(
        device_pos.astype(jnp.int32).reshape(1),
        leaf_src,
        leaf_count,
        node_src,
        node_count,
        *leaf_all,
        *given,
    )


def solution(mesh):
    placed = (
        P(None, ("leaf", "grp")),
        P(None, ("leaf", "grp")),
        P(("leaf", "grp")),
        P(("leaf", "grp"), None, None),
        P(("leaf", "grp"), None, None),
        P(("leaf", "grp"), None, None),
        P(("leaf", "grp"), None, None),
        P(("leaf", "grp"), None, None),
        P("leaf", None, None),
        P(("leaf", "grp"), None),
        P(("leaf", "grp")),
        P(("leaf", "grp"), None),
        P(("leaf", "grp")),
    )
    return jax.shard_map(
        shards, mesh=mesh, in_specs=placed, out_specs=P(None, ("leaf", "grp")), check_vma=False
    )
```
